32 devices in a mesh: seq: 8 (over y, x, core), grp: 4 (over z).
Axes of the slice: x: 2, y: 2, z: 4, core: 2. Of those that a mesh axis runs over, the one named last changes fastest.
Arguments:
- queries: bfloat16 [4096, 8, 128], P(('grp', 'seq')), may hold values from -6 to 6
- key_rows: bfloat16 [4096, 8, 128], P(('grp', 'seq')), may hold values from -6 to 6
- value_rows: bfloat16 [4096, 8, 256], P(('grp', 'seq')), may hold values from -6 to 6
- log_gate: float32 [8, 4096], P(None, ('grp', 'seq')), may hold values from -1.5 to 0
- beta_rate: float32 [8, 4096], P(None, ('grp', 'seq')), may hold values from 0 to 0.9
Outputs:
- outputs: bfloat16 [4096, 8, 256], P(('grp', 'seq'))
The draws below stay inside these ranges and needn't reach their ends.
All inputs are finite; a program needn't handle non-finite values.
Results may differ from the reference program's by a relative error of at most 0.0012.
Values sent between devices are 32-bit elements; how exact they have to be, the bound alone decides.
No kernel may reach another device: no remote copies, remote signals or barrier semaphores. Data moves between devices by JAX's collectives and lax.ppermute only.
A program may use at most 128 MiB of HBM per device.

```python
import math
import jax
import jax.numpy as jnp
from jax import lax

H = 8
K = 128
V = 256
STRETCH = 64
TOK_DEV = 128
TOKENS = 4096


def gate_parts(key):
    order_ids = jax.random.permutation(jax.random.fold_in(key, 101), H)
    quick_heads = order_ids < H // 2
    block_count = TOKENS // TOK_DEV
    spread = jax.random.uniform(jax.random.fold_in(key, 102), (H, block_count), jnp.float32, -0.7, 0.7)
    device_factor = jnp.repeat(jnp.exp(spread), TOK_DEV, axis=1)
    fast_base = max(1.0 / 40.0, 4.0 / TOK_DEV) * jnp.exp(jax.random.uniform(jax.random.fold_in(key, 103), (H,), jnp.float32, -0.2, 0.2))
    slow_base = jnp.exp(jax.random.uniform(jax.random.fold_in(key, 104), (H,), jnp.float32, math.log(0.3), math.log(1.2))) / TOKENS
    base_rate = jnp.where(quick_heads, fast_base, slow_base)
    return (quick_heads, base_rate, device_factor)


def draw_log_gate(key, part):
    quick_heads, base_rate, device_factor = gate_parts(key)
    jitter = jnp.exp(jax.random.uniform(jax.random.fold_in(key, 105), (H, TOKENS), jnp.float32, -0.7, 0.7))
    rates_every_head = jnp.minimum(base_rate[:, None] * device_factor * jitter, 0.5)
    spots = jax.random.randint(jax.random.fold_in(key, 106), (4,), 0, TOKENS)
    segment_depth = jax.random.uniform(jax.random.fold_in(key, 107), (H, 4), jnp.float32, math.log(0.5), math.log(0.8))
    position_table = (jnp.arange(TOKENS)[:, None] == spots[None, :]).astype(jnp.float32)
    segment_runs = jnp.dot(segment_depth, position_table.T)
    return -rates_every_head + jnp.where(quick_heads[:, None], 0.0, segment_runs)


def draw_beta_rate(key, part):
    quick_heads, base_rate, device_factor = gate_parts(key)
    fast_beta = jnp.exp(jax.random.uniform(jax.random.fold_in(key, 108), (H, TOKENS), jnp.float32, math.log(0.1), math.log(0.9)))
    slow_jitter = jnp.exp(jax.random.uniform(jax.random.fold_in(key, 109), (H, TOKENS), jnp.float32, math.log(0.5), math.log(2.0)))
    slow_beta = K / TOKENS * device_factor * slow_jitter
    return jnp.minimum(jnp.where(quick_heads[:, None], fast_beta, slow_beta), 0.9)


def levels(rng, shape, pieces, low, high):
    def one(axis_at, shards_of):
        steps = jax.random.uniform(jax.random.fold_in(jax.random.fold_in(rng, 6), axis_at), (shards_of,), jnp.float32, low / len(pieces), high / len(pieces))
        return jnp.repeat(jnp.exp(steps), shape[axis_at] // shards_of).reshape((-1,) + (1,) * (len(shape) - axis_at - 1))

    loudness = one(*pieces[0])
    for cut in pieces[1:]:
        loudness = loudness * one(*cut)
    return loudness


def bell_draw(rng, shape, scale, reach, shards=(), kind=jnp.bfloat16):
    loudness = levels(rng, shape, shards, -0.22, 0.18) if shards else 1.0
    entries = jax.random.normal(rng, shape, jnp.float32) * scale * loudness
    return jnp.minimum(jnp.maximum(entries, -reach), reach).astype(kind)


def setup_inputs(seed: int = 0) -> dict:
    key_of = jax.random.split(jax.random.key(seed), 6)
    return {
        "queries": bell_draw(key_of[0], (TOKENS, H, K), 1.0, 6.0, ((0, 32),)),
        "key_rows": bell_draw(key_of[1], (TOKENS, H, K), 1.0, 6.0, ((0, 32),)),
        "value_rows": bell_draw(key_of[2], (TOKENS, H, V), 1.0, 6.0, ((0, 32),)),
        "log_gate": draw_log_gate(jax.random.fold_in(key_of[5], 71), 0),
        "beta_rate": draw_beta_rate(jax.random.fold_in(key_of[5], 71), 0),
    }


EXACT_MATMUL = lax.Precision.HIGHEST

def unit_rows(vectors):
    wide = vectors.astype(jnp.float32)
    return wide / jnp.sqrt(lax.optimization_barrier(jnp.sum(wide * wide, axis=-1, keepdims=True)) + 1e-06)

def invert_unit_lower(strict):
    order_len = strict.shape[-1]
    identity = jnp.eye(order_len, dtype=strict.dtype)
    powered = -strict
    inverse = identity + powered
    span_len = 2
    while span_len < order_len:
        powered = jnp.einsum('hij,hjk->hik', powered, powered, precision=EXACT_MATMUL)
        inverse = inverse + jnp.einsum('hij,hjk->hik', inverse, powered, precision=EXACT_MATMUL)
        span_len = span_len * 2
    return inverse

def stretch_terms(q_head, k_head, v_head, gates, betas):
    order_len = gates.shape[1]
    rows_idx = lax.broadcasted_iota(jnp.int32, (order_len, order_len), 0)
    cols_idx = lax.broadcasted_iota(jnp.int32, (order_len, order_len), 1)
    lower_incl = rows_idx >= cols_idx
    lower_strict = rows_idx > cols_idx
    cum_log = jnp.cumsum(gates, axis=1)
    gaps_log = cum_log[:, :, None] - cum_log[:, None, :]
    decay_mask = jnp.where(lower_incl, jnp.exp(jnp.where(lower_incl, gaps_log, 0.0)), 0.0)
    key_gram = jnp.einsum('hik,hjk->hij', k_head, k_head, precision=EXACT_MATMUL)
    strict = jnp.where(lower_strict, betas[:, :, None] * key_gram, 0.0)
    inv_plain = invert_unit_lower(strict)
    inv_decay = inv_plain * decay_mask
    w_plain = jnp.einsum('hij,hjk->hik', inv_plain, betas[:, :, None] * k_head, precision=EXACT_MATMUL)
    decayed_weight = jnp.exp(cum_log)[:, :, None] * w_plain
    update_basis = jnp.einsum('hij,hjv->hiv', inv_decay, betas[:, :, None] * v_head, precision=EXACT_MATMUL)
    scores = jnp.einsum('hik,hjk->hij', q_head, k_head, precision=EXACT_MATMUL) * decay_mask
    gated_query = jnp.exp(cum_log)[:, :, None] * q_head
    return (cum_log, w_plain, decayed_weight, update_basis, scores, gated_query)

def advance_stretch(passed_state, stretch_parts, k_head):
    cum_log, w_plain, decayed_weight, update_basis, scores, gated_query = stretch_parts
    triangular_solve = update_basis - jnp.einsum('rzi,rib->rzb', decayed_weight, passed_state, precision=EXACT_MATMUL)
    segment_output = jnp.einsum('rzi,rib->rzb', gated_query, passed_state, precision=EXACT_MATMUL)
    segment_output = segment_output + jnp.einsum('hij,hjv->hiv', scores, triangular_solve, precision=EXACT_MATMUL)
    final_log = cum_log[:, -1]
    trailing_keys = jnp.exp(final_log[:, None] - cum_log)[:, :, None] * k_head
    following_state = jnp.exp(final_log)[:, None, None] * passed_state
    following_state = following_state + jnp.einsum('atb,atm->abm', trailing_keys, triangular_solve, precision=EXACT_MATMUL)
    return (segment_output, following_state)

def reference(queries, key_rows, value_rows, log_gate, beta_rate):
    stretch_count = TOKENS // STRETCH
    q_blocks = queries.reshape(stretch_count, STRETCH, H, K)
    k_blocks = key_rows.reshape(stretch_count, STRETCH, H, K)
    v_blocks = value_rows.reshape(stretch_count, STRETCH, H, V)
    g_blocks = jnp.transpose(log_gate.reshape(H, stretch_count, STRETCH), (1, 0, 2))
    b_blocks = jnp.transpose(beta_rate.reshape(H, stretch_count, STRETCH), (1, 0, 2))

    def step_stretch(passed_state, blocks):
        q_part, k_part, v_part, gates, betas = blocks
        q_head = jnp.transpose(unit_rows(q_part), (1, 0, 2))
        k_head = jnp.transpose(unit_rows(k_part), (1, 0, 2))
        v_head = jnp.transpose(v_part.astype(jnp.float32), (1, 0, 2))
        stretch_parts = stretch_terms(q_head, k_head, v_head, gates, betas)
        segment_output, following_state = advance_stretch(passed_state, stretch_parts, k_head)
        return (following_state, jnp.transpose(segment_output, (1, 0, 2)).astype(jnp.bfloat16))
    zero_state = jnp.zeros((H, K, V), jnp.float32)
    final_state, stretch_outs = lax.scan(step_stretch, zero_state, (q_blocks, k_blocks, v_blocks, g_blocks, b_blocks))
    return stretch_outs.reshape(TOKENS, H, V)
```

```python
import functools

import jax
import jax.numpy as jnp
from jax import lax
from jax.experimental import pallas as pl
from jax.experimental.pallas import tpu as pltpu
from jax.sharding import PartitionSpec as P

F32 = jnp.float32
BF16 = jnp.bfloat16
VMEM_LIMIT = 48 * 1024 * 1024


def split2(a):
    high = a.astype(BF16)
    low = (a - high.astype(F32)).astype(BF16)
    return high, low


def mm(a, b):
    return jnp.dot(a, b, preferred_element_type=F32)


def mm_nt(a, b):
    return lax.dot_general(a, b, (((1,), (1,)), ((), ())), preferred_element_type=F32)


def mm_tn(a, b):
    return lax.dot_general(a, b, (((0,), (0,)), ((), ())), preferred_element_type=F32)


def mm_exact_right(a, b):
    high, low = split2(a)
    return mm(jnp.concatenate([high, low], axis=1), jnp.concatenate([b, b], axis=0))


def mm3(a, b):
    ah, al = split2(a)
    bh, bl = split2(b)
    return mm(jnp.concatenate([ah, al], axis=1), jnp.concatenate([bh, bh], axis=0)) + mm(ah, bl)


def compose(later, earlier, key_dim):
    moved = mm3(later[:, :key_dim], earlier)
    return jnp.concatenate(
        [moved[:, :key_dim], moved[:, key_dim:] + later[:, key_dim:]], axis=1
    )


def vmem(count):
    return [pl.BlockSpec(memory_space=pltpu.VMEM)] * count


SMEM_SPEC = pl.BlockSpec(memory_space=pltpu.SMEM)


def call(kernel, out_shape, scratch=(), flops=0, nbytes=0):
    def run(place, *arrays):
        return pl.pallas_call(
            kernel,
            out_shape=out_shape,
            in_specs=[SMEM_SPEC] + vmem(len(arrays)),
            out_specs=jax.tree.map(lambda _: pl.BlockSpec(memory_space=pltpu.VMEM), out_shape),
            scratch_shapes=list(scratch),
            compiler_params=pltpu.CompilerParams(vmem_limit_bytes=VMEM_LIMIT),
            cost_estimate=pl.CostEstimate(flops=flops, bytes_accessed=nbytes, transcendentals=0),
        )(place, *arrays)

    return run


def lane_cumsum(a):
    size = a.shape[1]
    lane = lax.broadcasted_iota(jnp.int32, a.shape, 1)
    step = 1
    while step < size:
        a = a + jnp.where(lane >= step, pltpu.roll(a, step, 1), 0.0)
        step *= 2
    return a


def head_rows(scratch, head, heads):
    count = scratch.shape[0] // heads
    return scratch[pl.ds(head, count, stride=heads), :]


def halves_of(a, flip, half):
    return jnp.where(flip, a[half:], a[:half])


def stage_rows(ref, scratch):
    wide = ref[...].astype(F32)
    scratch[...] = wide.reshape(scratch.shape)


def map_kernel(own, place, k_ref, v_ref, g_ref, b_ref, m_ref, r_ref, ks, vs0, vs1):
    tok, heads, key_dim = k_ref.shape
    value_dim = v_ref.shape[2]
    half = heads // 2
    core = place[0]
    side = core if own else 1 - core
    base = side * half
    stage_rows(k_ref, ks)
    wide = v_ref[...].astype(F32)
    vs0[...] = wide[:, :, : value_dim // 2].reshape(vs0.shape)
    vs1[...] = wide[:, :, value_dim // 2 :].reshape(vs1.shape)
    cum_row = lane_cumsum(halves_of(g_ref[...], side == 1, half))
    beta_row = halves_of(b_ref[...], side == 1, half)
    last_row = cum_row[:, tok - 1 :]
    decay_row = jnp.exp(cum_row)
    cum_col = cum_row.T
    beta_col = beta_row.T
    trail_col = jnp.exp(last_row - cum_row).T
    rows = lax.broadcasted_iota(jnp.int32, (tok, tok), 0)
    cols = lax.broadcasted_iota(jnp.int32, (tok, tok), 1)
    lower = rows > cols
    eye = rows == cols
    eye_key = (
        lax.broadcasted_iota(jnp.int32, (key_dim, key_dim), 0)
        == lax.broadcasted_iota(jnp.int32, (key_dim, key_dim), 1)
    )
    every = range(half)
    k_wide = [head_rows(ks, base + i, heads) for i in every]
    k_raw = [a.astype(BF16) for a in k_wide]
    v_raw = [
        jnp.concatenate(
            [head_rows(vs0, base + i, heads), head_rows(vs1, base + i, heads)], axis=1
        ).astype(BF16)
        for i in every
    ]
    gram = [mm_nt(a, a) for a in k_raw]
    inv_col = [lax.rsqrt(jnp.sum(a * a, axis=1, keepdims=True) + 1e-6) for a in k_wide]
    inv_row = [
        lax.rsqrt(jnp.sum(jnp.where(eye, a, 0.0), axis=0, keepdims=True) + 1e-6) for a in gram
    ]
    strict = []
    for i in every:
        gap = cum_col[:, i : i + 1] - cum_row[i : i + 1, :]
        decay = jnp.exp(jnp.where(lower, gap, 0.0))
        left = beta_col[:, i : i + 1] * inv_col[i]
        strict.append(jnp.where(lower, gram[i] * decay * left * inv_row[i], 0.0))
    pair = (rows // 2) == (cols // 2)
    inverse = [jnp.where(eye, 1.0, jnp.where(pair, -a, 0.0)) for a in strict]
    span = 2
    while span < tok:
        joint = ((rows // (2 * span)) == (cols // (2 * span))) & (
            (rows // span) != (cols // span)
        )
        off = [jnp.where(joint, a, 0.0) for a in strict]
        first = [mm3(x, o) for x, o in zip(inverse, off)]
        second = [mm3(f, x) for f, x in zip(first, inverse)]
        inverse = [x - s for x, s in zip(inverse, second)]
        span *= 2
    for i in every:
        beta_i = beta_row[i : i + 1, :]
        key_scale = -(decay_row[i : i + 1, :] * beta_i * inv_row[i])
        key_part = mm_exact_right(inverse[i] * key_scale, k_raw[i])
        value_part = mm_exact_right(inverse[i] * beta_i, v_raw[i])
        basis = jnp.concatenate([key_part, value_part], axis=1)
        r_ref[i] = basis
        bh, bl = split2(basis * (trail_col[:, i : i + 1] * inv_col[i]))
        k_twice = jnp.concatenate([k_raw[i], k_raw[i]], axis=0)
        moved = mm_tn(k_twice, jnp.concatenate([bh, bl], axis=0))
        diagonal = jnp.where(eye_key, jnp.exp(last_row[i : i + 1, :]), 0.0)
        m_ref[i] = jnp.concatenate(
            [moved[:, :key_dim] + diagonal, moved[:, key_dim:]], axis=1
        )


def query_kernel(own, place, q_ref, k_ref, g_ref, r_ref, f_ref, qs, ks):
    tok, heads, key_dim = k_ref.shape
    half = heads // 2
    core = place[0]
    side = core if own else 1 - core
    base = side * half
    stage_rows(q_ref, qs)
    stage_rows(k_ref, ks)
    cum_row = lane_cumsum(halves_of(g_ref[...], side == 1, half))
    cum_col = cum_row.T
    rows = lax.broadcasted_iota(jnp.int32, (tok, tok), 0)
    cols = lax.broadcasted_iota(jnp.int32, (tok, tok), 1)
    lower = rows >= cols
    for i in range(half):
        q_wide = head_rows(qs, base + i, heads)
        k_wide = head_rows(ks, base + i, heads)
        q_inv = lax.rsqrt(jnp.sum(q_wide * q_wide, axis=1, keepdims=True) + 1e-6)
        k_inv = lax.rsqrt(jnp.sum(k_wide * k_wide, axis=1, keepdims=True) + 1e-6)
        k_inv_row = jnp.broadcast_to(k_inv, (tok, tok)).T[:1, :]
        dots = mm_nt(q_wide.astype(BF16), k_wide.astype(BF16))
        gap = cum_col[:, i : i + 1] - cum_row[i : i + 1, :]
        decay = jnp.exp(jnp.where(lower, gap, 0.0))
        scores = jnp.where(lower, dots * decay * q_inv * k_inv_row, 0.0)
        folded = mm3(scores, r_ref[i])
        gated = q_wide * (q_inv * jnp.exp(cum_col[:, i : i + 1]))
        f_ref[i] = jnp.concatenate(
            [folded[:, :key_dim] + gated, folded[:, key_dim:]], axis=1
        )


def chip_kernel(key_dim, outs_per, place, own_ref, got_ref, *out_refs):
    core, chip = place[0], place[1]
    half = own_ref.shape[0]
    owners = half // outs_per
    for r, out in enumerate(out_refs):
        owner = jnp.bitwise_xor(chip, r)
        owner = jnp.where(owner < owners, owner, 0)
        for j in range(outs_per):
            head = owner * outs_per + j
            own, got = own_ref[head], got_ref[head]
            earlier = jnp.where(core == 0, own, got)
            later = jnp.where(core == 0, got, own)
            out[j] = compose(later, earlier, key_dim)


def plane_kernel(key_dim, chips, place, *refs):
    maps, total, prefix = refs[:chips], refs[chips], refs[chips + 1]
    chip = place[1]
    per = total.shape[0]
    prefix_store = prefix
    for j in range(per):
        ordered = []
        for index in range(chips):
            value = maps[0][j]
            for r in range(1, chips):
                value = jnp.where(jnp.bitwise_xor(chip, r) == index, maps[r][j], value)
            ordered.append(value)
        running = ordered[0]
        prefix_store[0, j] = running
        for index in range(1, chips):
            running = compose(ordered[index], running, key_dim)
            if index < chips - 1:
                prefix_store[index, j] = running
        total[j] = running


def group_kernel(key_dim, level, place, total_ref, got_ref, before_ref, new_total, new_before):
    group = place[2]
    upper = jnp.bitwise_and(jnp.right_shift(group, level), 1) == 1
    for j in range(total_ref.shape[0]):
        mine, got = total_ref[j], got_ref[j]
        later = jnp.where(upper, mine, got)
        earlier = jnp.where(upper, got, mine)
        new_total[j] = compose(later, earlier, key_dim)
        if before_ref is None:
            identity = jnp.where(
                lax.broadcasted_iota(jnp.int32, mine.shape, 0)
                == lax.broadcasted_iota(jnp.int32, mine.shape, 1),
                1.0,
                0.0,
            )
            new_before[j] = jnp.where(upper, got, identity)
        else:
            before = before_ref[j]
            new_before[j] = jnp.where(upper, compose(before, got, key_dim), before)


def first_group_kernel(key_dim, place, total_ref, got_ref, new_total, new_before):
    group_kernel(key_dim, 0, place, total_ref, got_ref, None, new_total, new_before)


def enter_kernel(key_dim, chips, level, place, got_ref, before_ref, prefix_ref, *out_refs):
    chip, group = place[1], place[2]
    upper = jnp.bitwise_and(jnp.right_shift(group, level), 1) == 1
    for j in range(got_ref.shape[0]):
        before = before_ref[j]
        joined = mm3(before[:, :key_dim], got_ref[j]) + before[:, key_dim:]
        entering = jnp.where(upper, joined, before[:, key_dim:])
        eh, el = split2(entering)
        twice = jnp.concatenate([eh, eh], axis=0)
        states = [entering]
        for index in range(chips - 1):
            one = prefix_ref[index, j]
            th, tl = split2(one[:, :key_dim])
            moved = mm(jnp.concatenate([th, tl], axis=1), twice) + mm(th, el)
            states.append(moved + one[:, key_dim:])
        for r, out in enumerate(out_refs):
            value = states[0]
            for index in range(1, chips):
                value = jnp.where(jnp.bitwise_xor(chip, r) == index, states[index], value)
            out[j] = value


def core_kernel(key_dim, outs_per, owners, place, own_ref, got_ref, *refs):
    parts, keep, give = refs[:-2], refs[-2], refs[-1]
    core, chip = place[0], place[1]
    for r, part in enumerate(parts):
        owner = jnp.bitwise_xor(chip, r)

        @pl.when(owner < owners)
        def _():
            for j in range(outs_per):
                head = owner * outs_per + j
                state = part[j]
                first = jnp.where(core == 0, own_ref[head], got_ref[head])
                second = mm3(first[:, :key_dim], state) + first[:, key_dim:]
                keep[head] = jnp.where(core == 0, state, second)
                give[head] = jnp.where(core == 0, second, state)


def output_kernel(place, keep_ref, got_ref, f_own, f_give, o_ref, os0, os1):
    half, key_dim, value_dim = keep_ref.shape
    tok = f_own.shape[1]
    heads = 2 * half
    core = place[0]
    mid = value_dim // 2
    for state_ref, folded_ref, side in ((keep_ref, f_own, core), (got_ref, f_give, 1 - core)):
        for i in range(half):
            folded = folded_ref[i]
            out = mm3(folded[:, :key_dim], state_ref[i]) + folded[:, key_dim:]
            head = side * half + i
            os0[pl.ds(head, tok, stride=heads), :] = out[:, :mid]
            os1[pl.ds(head, tok, stride=heads), :] = out[:, mid:]
    o_ref[:, :, :mid] = os0[...].reshape(tok, heads, mid).astype(BF16)
    o_ref[:, :, mid:] = os1[...].reshape(tok, heads, value_dim - mid).astype(BF16)


def body(queries, key_rows, value_rows, log_gate, beta_rate):
    tok, heads, key_dim = queries.shape
    value_dim = value_rows.shape[2]
    wide = key_dim + value_dim
    half = heads // 2
    seq, grp = lax.axis_size("seq"), lax.axis_size("grp")
    chips = seq // 2
    owners = min(chips, half)
    per = half // owners
    place_seq, place_grp = lax.axis_index("seq"), lax.axis_index("grp")
    place = jnp.stack([place_seq % 2, place_seq // 2, place_grp]).astype(jnp.int32)
    f32 = lambda *shape: jax.ShapeDtypeStruct(shape, F32)
    tall = lambda width: pltpu.VMEM((tok * heads, width), F32)
    unit = 2 * tok * key_dim * key_dim

    def maps(own):
        return call(
            functools.partial(map_kernel, own),
            (f32(half, key_dim, wide), f32(half, tok, wide)),
            [tall(key_dim), tall(value_dim // 2), tall(value_dim // 2)],
            flops=50 * half * unit,
        )(place, key_rows, value_rows, log_gate, beta_rate)

    def folded(own, basis):
        return call(
            functools.partial(query_kernel, own),
            f32(half, tok, wide),
            [tall(key_dim), tall(key_dim)],
            flops=10 * half * unit,
        )(place, queries, key_rows, log_gate, basis)

    sibling = [(i, i ^ 1) for i in range(seq)]
    give_map, give_basis = maps(False)
    got_map = lax.ppermute(give_map, "seq", sibling)
    own_map, own_basis = maps(True)
    chip_maps = call(
        functools.partial(chip_kernel, key_dim, per), [f32(per, key_dim, wide)] * chips
    )(place, own_map, got_map)
    f_own = folded(True, own_basis)
    f_give = folded(False, give_basis)

    def across(parts, to_owner):
        moved = [parts[0]]
        for r in range(1, chips):
            pairs = [
                (i, i ^ (2 * r))
                for i in range(seq)
                if ((i ^ (2 * r)) // 2 if to_owner else i // 2) < owners
            ]
            moved.append(lax.ppermute(parts[r], "seq", pairs))
        return moved

    owned = across(chip_maps, True)
    total, prefix = call(
        functools.partial(plane_kernel, key_dim, chips),
        (f32(per, key_dim, wide), f32(chips - 1, per, key_dim, wide)),
    )(place, *owned)
    before = None
    level = 0
    while 2 << level <= grp:
        swap = [(i, i ^ (1 << level)) for i in range(grp)]
        final = 4 << level > grp
        if final and before is not None:
            got_state = lax.ppermute(total[:, :, key_dim:], "grp", swap)
            states = call(
                functools.partial(enter_kernel, key_dim, chips, level),
                [f32(per, key_dim, value_dim)] * chips,
            )(place, got_state, before, prefix)
        else:
            got = lax.ppermute(total, "grp", swap)
            shapes = (f32(per, key_dim, wide), f32(per, key_dim, wide))
            if before is None:
                total, before = call(
                    functools.partial(first_group_kernel, key_dim), shapes
                )(place, total, got)
            else:
                total, before = call(
                    functools.partial(group_kernel, key_dim, level), shapes
                )(place, total, got, before)
        level += 1
    arrived = across(states, False)
    keep, give = call(
        functools.partial(core_kernel, key_dim, per, owners), [f32(half, key_dim, value_dim)] * 2
    )(place, own_map, got_map, *arrived)
    got = lax.ppermute(give, "seq", sibling)
    return call(
        output_kernel,
        jax.ShapeDtypeStruct((tok, heads, value_dim), BF16),
        [tall(value_dim // 2), tall(value_dim // 2)],
    )(place, keep, got, f_own, f_give)


def solution(mesh):
    return jax.shard_map(
        body,
        mesh=mesh,
        in_specs=(
            P(("grp", "seq"), None, None),
            P(("grp", "seq"), None, None),
            P(("grp", "seq"), None, None),
            P(None, ("grp", "seq")),
            P(None, ("grp", "seq")),
        ),
        out_specs=P(("grp", "seq"), None, None),
        check_vma=False,
    )
```

```python
import functools

import jax
import jax.numpy as jnp
from jax import lax
from jax.experimental import pallas as pl
from jax.experimental.pallas import tpu as pltpu
from jax.sharding import PartitionSpec as P

F32 = jnp.float32
BF16 = jnp.bfloat16
VMEM_LIMIT = 48 * 1024 * 1024


def split2(a):
    high = a.astype(BF16)
    low = (a - high.astype(F32)).astype(BF16)
    return high, low


def mm(a, b):
    return jnp.dot(a, b, preferred_element_type=F32)


def mm_nt(a, b):
    return lax.dot_general(a, b, (((1,), (1,)), ((), ())), preferred_element_type=F32)


def mm_tn(a, b):
    return lax.dot_general(a, b, (((0,), (0,)), ((), ())), preferred_element_type=F32)


def mm_exact_right(a, b):
    high, low = split2(a)
    return mm(jnp.concatenate([high, low], axis=1), jnp.concatenate([b, b], axis=0))


def mm3(a, b):
    ah, al = split2(a)
    bh, bl = split2(b)
    return mm(jnp.concatenate([ah, al], axis=1), jnp.concatenate([bh, bh], axis=0)) + mm(ah, bl)


def compose(later, earlier, key_dim):
    moved = mm3(later[:, :key_dim], earlier)
    return jnp.concatenate(
        [moved[:, :key_dim], moved[:, key_dim:] + later[:, key_dim:]], axis=1
    )


def vmem(count):
    return [pl.BlockSpec(memory_space=pltpu.VMEM)] * count


SMEM_SPEC = pl.BlockSpec(memory_space=pltpu.SMEM)


def call(kernel, out_shape, scratch=(), flops=0, nbytes=0):
    def run(place, *arrays):
        return pl.pallas_call(
            kernel,
            out_shape=out_shape,
            in_specs=[SMEM_SPEC] + vmem(len(arrays)),
            out_specs=jax.tree.map(lambda _: pl.BlockSpec(memory_space=pltpu.VMEM), out_shape),
            scratch_shapes=list(scratch),
            compiler_params=pltpu.CompilerParams(vmem_limit_bytes=VMEM_LIMIT),
            cost_estimate=pl.CostEstimate(flops=flops, bytes_accessed=nbytes, transcendentals=0),
        )(place, *arrays)

    return run


def lane_cumsum(a):
    size = a.shape[1]
    lane = lax.broadcasted_iota(jnp.int32, a.shape, 1)
    step = 1
    while step < size:
        a = a + jnp.where(lane >= step, pltpu.roll(a, step, 1), 0.0)
        step *= 2
    return a


def head_rows(scratch, head, heads):
    count = scratch.shape[0] // heads
    return scratch[pl.ds(head, count, stride=heads), :]


def stage_rows(ref, scratch):
    wide = ref[...].astype(F32)
    scratch[...] = wide.reshape(scratch.shape)


def rolled(a, flip):
    half = a.shape[0] // 2
    return jnp.where(flip, jnp.concatenate([a[half:], a[:half]], axis=0), a)


def block_inverse(strict, rows, cols):
    size = rows.shape[0]
    base = min(16, size)
    eye = rows == cols
    within = (rows // base) == (cols // base)
    power = [jnp.where(within, -a, 0.0) for a in strict]
    inverse = [jnp.where(eye, 1.0, a) for a in power]
    span = 2
    while span < base:
        power = [mm3(a, a) for a in power]
        inverse = [x + mm3(x, a) for x, a in zip(inverse, power)]
        span *= 2
    span = base
    while span < size:
        joint = ((rows // (2 * span)) == (cols // (2 * span))) & (
            (rows // span) != (cols // span)
        )
        off = [jnp.where(joint, a, 0.0) for a in strict]
        first = [mm3(x, o) for x, o in zip(inverse, off)]
        inverse = [x - mm3(f, x) for f, x in zip(first, inverse)]
        span *= 2
    return inverse


def trailing_map(basis, trail, k_raw, last, eye_key, key_dim):
    bh, bl = split2(basis * trail)
    moved = mm_tn(
        jnp.concatenate([k_raw, k_raw], axis=0), jnp.concatenate([bh, bl], axis=0)
    )
    return jnp.concatenate(
        [moved[:, :key_dim] + jnp.where(eye_key, last, 0.0), moved[:, key_dim:]], axis=1
    )


def eye_mask(size):
    return lax.broadcasted_iota(jnp.int32, (size, size), 0) == lax.broadcasted_iota(
        jnp.int32, (size, size), 1
    )


def basis_kernel(
    place, k_hbm, v_hbm, g_hbm, b_hbm, m_ref, r_ref, kh_ref, trail_ref, rows_ref,
    k_ref, v_ref, g_ref, b_ref, ks, vs0, vs1, sems,
):
    copies = [
        pltpu.make_async_copy(src, dst, sems.at[n])
        for n, (src, dst) in enumerate(
            ((g_hbm, g_ref), (b_hbm, b_ref), (k_hbm, k_ref), (v_hbm, v_ref))
        )
    ]
    for copy in copies:
        copy.start()
    tok, heads, key_dim = k_ref.shape
    value_dim = v_ref.shape[2]
    half = heads // 2
    first_side = 1 - place[0]
    flip = first_side == 1
    order = [first_side * half + i for i in range(half)]
    order += [(1 - first_side) * half + i for i in range(half)]
    copies[0].wait()
    copies[1].wait()
    cum_row = lane_cumsum(rolled(g_ref[...], flip))
    beta_row = rolled(b_ref[...], flip)
    last_row = cum_row[:, tok - 1 :]
    decay_row = jnp.exp(cum_row)
    cum_col = cum_row.T
    beta_col = beta_row.T
    trail_col = jnp.exp(last_row - cum_row).T
    rows = lax.broadcasted_iota(jnp.int32, (tok, tok), 0)
    cols = lax.broadcasted_iota(jnp.int32, (tok, tok), 1)
    lower = rows > cols
    eye = rows == cols
    eye_key = eye_mask(key_dim)
    every = range(heads)
    copies[2].wait()
    stage_rows(k_ref, ks)
    k_wide = [head_rows(ks, h, heads) for h in order]
    k_raw = [a.astype(BF16) for a in k_wide]
    for i in every:
        kh_ref[i] = k_raw[i]
    gram = [mm_nt(a, a) for a in k_raw]
    inv_col = [lax.rsqrt(jnp.sum(a * a, axis=1, keepdims=True) + 1e-6) for a in k_wide]
    inv_row = [
        lax.rsqrt(jnp.sum(jnp.where(eye, a, 0.0), axis=0, keepdims=True) + 1e-6) for a in gram
    ]
    strict = []
    for i in every:
        gap = cum_col[:, i : i + 1] - cum_row[i : i + 1, :]
        decay = jnp.exp(jnp.where(lower, gap, 0.0))
        left = beta_col[:, i : i + 1] * inv_col[i]
        strict.append(jnp.where(lower, gram[i] * decay * left * inv_row[i], 0.0))
    inverse = block_inverse(strict, rows, cols)
    copies[3].wait()
    wide = v_ref[...].astype(F32)
    vs0[...] = wide[:, :, : value_dim // 2].reshape(vs0.shape)
    vs1[...] = wide[:, :, value_dim // 2 :].reshape(vs1.shape)
    rows_ref[0] = jnp.concatenate(inv_row, axis=0)
    rows_ref[1] = cum_row
    for i in every:
        v_raw = jnp.concatenate(
            [head_rows(vs0, order[i], heads), head_rows(vs1, order[i], heads)], axis=1
        ).astype(BF16)
        beta_i = beta_row[i : i + 1, :]
        key_scale = -(decay_row[i : i + 1, :] * beta_i * inv_row[i])
        key_part = mm_exact_right(inverse[i] * key_scale, k_raw[i])
        value_part = mm_exact_right(inverse[i] * beta_i, v_raw)
        basis = jnp.concatenate([key_part, value_part], axis=1)
        r_ref[i] = basis
        trail = trail_col[:, i : i + 1] * inv_col[i]
        if i < half:
            m_ref[i] = trailing_map(
                basis, trail, k_raw[i], jnp.exp(last_row[i : i + 1, :]), eye_key, key_dim
            )
        else:
            trail_ref[i - half] = jnp.broadcast_to(trail, (tok, key_dim))


def own_map_kernel(place, r_ref, kh_ref, trail_ref, rows_ref, m_ref):
    half, key_dim, wide = m_ref.shape
    tok = r_ref.shape[1]
    eye_key = eye_mask(key_dim)
    for i in range(half):
        trail = trail_ref[i][:, :1]
        last = jnp.exp(rows_ref[1, half + i : half + i + 1, tok - 1 :])
        m_ref[i] = trailing_map(r_ref[half + i], trail, kh_ref[half + i], last, eye_key, key_dim)


def query_kernel(place, q_ref, kh_ref, rows_ref, r_ref, got_ref, got_own_ref, f_ref, qs):
    heads, tok, key_dim = kh_ref.shape
    half = heads // 2
    core = place[0]
    stage_rows(q_ref, qs)
    cum_row = rows_ref[1]
    cum_col = cum_row.T
    rows = lax.broadcasted_iota(jnp.int32, (tok, tok), 0)
    cols = lax.broadcasted_iota(jnp.int32, (tok, tok), 1)
    lower = rows >= cols
    for i in range(heads):
        head = ((1 - core) * half + i) if i < half else (core * half + i - half)
        q_wide = head_rows(qs, head, heads)
        q_inv = lax.rsqrt(jnp.sum(q_wide * q_wide, axis=1, keepdims=True) + 1e-6)
        dots = mm_nt(q_wide.astype(BF16), kh_ref[i])
        gap = cum_col[:, i : i + 1] - cum_row[i : i + 1, :]
        decay = jnp.exp(jnp.where(lower, gap, 0.0))
        scores = jnp.where(lower, dots * decay * q_inv * rows_ref[0, i : i + 1, :], 0.0)
        folded = mm3(scores, r_ref[i])
        gated = q_wide * (q_inv * jnp.exp(cum_col[:, i : i + 1]))
        f_ref[i] = jnp.concatenate(
            [folded[:, :key_dim] + gated, folded[:, key_dim:]], axis=1
        )

    @pl.when(core == 1)
    def _():
        for i in range(heads):
            earlier = got_own_ref[i] if i < half else got_ref[i - half]
            f_ref[i] = compose(f_ref[i], earlier, key_dim)


def chip_kernel(key_dim, outs_per, place, own_ref, got_ref, *out_refs):
    core, chip = place[0], place[1]
    half = own_ref.shape[0]
    owners = half // outs_per
    for r, out in enumerate(out_refs):
        owner = jnp.bitwise_xor(chip, r)
        owner = jnp.where(owner < owners, owner, 0)
        for j in range(outs_per):
            head = owner * outs_per + j
            own, got = own_ref[head], got_ref[head]
            earlier = jnp.where(core == 0, own, got)
            later = jnp.where(core == 0, got, own)
            out[j] = compose(later, earlier, key_dim)


def in_order(chip, maps):
    maps = list(maps)
    bit = 1
    while bit < len(maps):
        swapped = jnp.bitwise_and(chip, bit) != 0
        maps = [jnp.where(swapped, maps[i ^ bit], maps[i]) for i in range(len(maps))]
        bit *= 2
    return maps


def total_kernel(key_dim, place, *refs):
    maps, total = refs[:-1], refs[-1]
    chip = place[1]
    for j in range(total.shape[0]):
        level = [ref[j] for ref in maps]
        bit = 1
        while len(level) > 1:
            swapped = jnp.bitwise_and(chip, bit) != 0
            level = [
                compose(
                    jnp.where(swapped, low, high), jnp.where(swapped, high, low), key_dim
                )
                for low, high in zip(level[::2], level[1::2])
            ]
            bit *= 2
        total[j] = level[0]


def prefix_kernel(key_dim, place, *refs):
    maps, prefix = refs[:-1], refs[-1]
    for j in range(prefix.shape[1]):
        ordered = in_order(place[1], [ref[j] for ref in maps])
        running = ordered[0]
        prefix[0, j] = running
        for index in range(1, len(ordered) - 1):
            running = compose(ordered[index], running, key_dim)
            prefix[index, j] = running


def is_upper(place, level):
    return jnp.bitwise_and(jnp.right_shift(place[2], level), 1) == 1


def group_total_kernel(key_dim, level, place, total_ref, got_ref, out_ref):
    upper = is_upper(place, level)
    for j in range(total_ref.shape[0]):
        mine, got = total_ref[j], got_ref[j]
        later = jnp.where(upper, mine, got)
        earlier = jnp.where(upper, got, mine)
        if out_ref.shape[2] == mine.shape[1]:
            out_ref[j] = compose(later, earlier, key_dim)
        else:
            out_ref[j] = mm3(later[:, :key_dim], earlier[:, key_dim:]) + later[:, key_dim:]


def before_kernel(key_dim, level, place, got_ref, prefix_ref, out_ref):
    upper = is_upper(place, level)
    count = out_ref.shape[0]

    @pl.when(upper)
    def _():
        for j in range(out_ref.shape[1]):
            for index in range(count):
                if prefix_ref.shape[0] == count:
                    out_ref[index, j] = compose(prefix_ref[index, j], got_ref[j], key_dim)
                elif index == 0:
                    out_ref[index, j] = got_ref[j]
                else:
                    out_ref[index, j] = compose(prefix_ref[index - 1, j], got_ref[j], key_dim)

    @pl.when(jnp.logical_not(upper))
    def _():
        for j in range(out_ref.shape[1]):
            for index in range(count):
                if prefix_ref.shape[0] == count:
                    out_ref[index, j] = prefix_ref[index, j]
                elif index == 0:
                    out_ref[index, j] = jnp.where(
                        lax.broadcasted_iota(jnp.int32, out_ref.shape[2:], 0)
                        == lax.broadcasted_iota(jnp.int32, out_ref.shape[2:], 1),
                        1.0,
                        0.0,
                    )
                else:
                    out_ref[index, j] = prefix_ref[index - 1, j]


def enter_kernel(key_dim, level, place, got_ref, prefix_ref, *out_refs):
    chip = place[1]
    upper = is_upper(place, level)
    for j in range(got_ref.shape[0]):
        eh, el = split2(jnp.where(upper, got_ref[j], 0.0))
        twice = jnp.concatenate([eh, eh], axis=0)
        for r, out in enumerate(out_refs):
            one = prefix_ref[jnp.bitwise_xor(chip, r), j]
            th, tl = split2(one[:, :key_dim])
            moved = mm(jnp.concatenate([th, tl], axis=1), twice) + mm(th, el)
            out[j] = moved + one[:, key_dim:]


def output_kernel(per, owners, place, f_ref, *refs):
    o_ref, os0, os1 = refs[-3:]
    parts = refs[:-3]
    chips = len(parts) // 2
    heads, tok, wide = f_ref.shape
    half = heads // 2
    key_dim = wide - o_ref.shape[2]
    core, chip = place[0], place[1]
    mid = o_ref.shape[2] // 2

    def one(index, state, head):
        folded = f_ref[index]
        out = mm3(folded[:, :key_dim], state) + folded[:, key_dim:]
        os0[pl.ds(head, tok, stride=heads), :] = out[:, :mid]
        os1[pl.ds(head, tok, stride=heads), :] = out[:, mid:]

    for r in range(chips):
        owner = jnp.bitwise_xor(chip, r)

        def both(owner=owner, r=r):
            for j in range(per):
                head = owner * per + j
                one(half + head, parts[r][j], core * half + head)
                one(head, parts[chips + r][j], (1 - core) * half + head)

        if owners < chips:
            pl.when(owner < owners)(both)
        else:
            both()
    o_ref[:, :, :mid] = os0[...].reshape(tok, heads, mid).astype(BF16)
    o_ref[:, :, mid:] = os1[...].reshape(tok, heads, mid).astype(BF16)


def body(queries, key_rows, value_rows, log_gate, beta_rate):
    tok, heads, key_dim = queries.shape
    value_dim = value_rows.shape[2]
    wide = key_dim + value_dim
    half = heads // 2
    seq, grp = lax.axis_size("seq"), lax.axis_size("grp")
    chips = seq // 2
    owners = min(chips, half)
    per = half // owners
    place_seq, place_grp = lax.axis_index("seq"), lax.axis_index("grp")
    place = jnp.stack([place_seq % 2, place_seq // 2, place_grp]).astype(jnp.int32)
    f32 = lambda *shape: jax.ShapeDtypeStruct(shape, F32)
    tall = lambda width: pltpu.VMEM((tok * heads, width), F32)
    unit = 2 * tok * key_dim * key_dim
    sibling = [(i, i ^ 1) for i in range(seq)]

    give_map, basis, k_heads, trail, rows = pl.pallas_call(
        basis_kernel,
        out_shape=(
            f32(half, key_dim, wide),
            f32(heads, tok, wide),
            jax.ShapeDtypeStruct((heads, tok, key_dim), BF16),
            f32(half, tok, key_dim),
            f32(2, heads, tok),
        ),
        in_specs=[SMEM_SPEC] + [pl.BlockSpec(memory_space=pltpu.HBM)] * 4,
        out_specs=tuple(vmem(5)),
        scratch_shapes=[
            pltpu.VMEM((tok, heads, key_dim), BF16),
            pltpu.VMEM((tok, heads, value_dim), BF16),
            pltpu.VMEM((heads, tok), F32),
            pltpu.VMEM((heads, tok), F32),
            tall(key_dim),
            tall(value_dim // 2),
            tall(value_dim // 2),
            pltpu.SemaphoreType.DMA((4,)),
        ],
        compiler_params=pltpu.CompilerParams(vmem_limit_bytes=VMEM_LIMIT),
        cost_estimate=pl.CostEstimate(
            flops=50 * heads * unit, bytes_accessed=0, transcendentals=0
        ),
    )(place, key_rows, value_rows, log_gate, beta_rate)
    got_map = lax.ppermute(give_map, "seq", sibling)
    own_map = call(own_map_kernel, f32(half, key_dim, wide), flops=6 * half * unit)(
        place, basis, k_heads, trail, rows
    )
    chip_maps = call(
        functools.partial(chip_kernel, key_dim, per), [f32(per, key_dim, wide)] * chips
    )(place, own_map, got_map)

    def across(parts, to_owner):
        moved = [parts[0]]
        for r in range(1, chips):
            pairs = [
                (i, i ^ (2 * r))
                for i in range(seq)
                if ((i ^ (2 * r)) // 2 if to_owner else i // 2) < owners
            ]
            moved.append(lax.ppermute(parts[r], "seq", pairs))
        return moved

    owned = across(chip_maps, True)
    got_own = lax.ppermute(own_map, "seq", sibling)
    folded = call(
        query_kernel, f32(heads, tok, wide), [tall(key_dim)], flops=20 * heads * unit
    )(place, queries, k_heads, rows, basis, got_map, got_own)
    owned, folded = lax.optimization_barrier((owned, folded))
    total = call(functools.partial(total_kernel, key_dim), f32(per, key_dim, wide))(
        place, *owned
    )
    prefix = call(
        functools.partial(prefix_kernel, key_dim), f32(chips - 1, per, key_dim, wide)
    )(place, *owned)
    level = 0
    while 2 << level <= grp:
        swap = [(i, i ^ (1 << level)) for i in range(grp)]
        if 2 << level == grp:
            if level == 0:
                total = total[:, :, key_dim:]
            got_state = lax.ppermute(total, "grp", swap)
            states = call(
                functools.partial(enter_kernel, key_dim, level),
                [f32(per, key_dim, value_dim)] * chips,
            )(place, got_state, prefix)
        else:
            got = lax.ppermute(total, "grp", swap)
            width = value_dim if 4 << level == grp else wide
            total = call(
                functools.partial(group_total_kernel, key_dim, level), f32(per, key_dim, width)
            )(place, total, got)
            prefix = call(
                functools.partial(before_kernel, key_dim, level),
                f32(chips, per, key_dim, wide),
            )(place, got, prefix)
        level += 1
    arrived = across(states, False)
    others = [lax.ppermute(part, "seq", sibling) for part in arrived]
    return call(
        functools.partial(output_kernel, per, owners),
        jax.ShapeDtypeStruct((tok, heads, value_dim), BF16),
        [tall(value_dim // 2), tall(value_dim // 2)],
    )(place, folded, *arrived, *others)


def solution(mesh):
    return jax.shard_map(
        body,
        mesh=mesh,
        in_specs=(
            P(("grp", "seq"), None, None),
            P(("grp", "seq"), None, None),
            P(("grp", "seq"), None, None),
            P(None, ("grp", "seq")),
            P(None, ("grp", "seq")),
        ),
        out_specs=P(("grp", "seq"), None, None),
        check_vma=False,
    )
```

```python
import functools

import jax
import jax.numpy as jnp
from jax import lax
from jax.experimental import pallas as pl
from jax.experimental.pallas import tpu as pltpu
from jax.sharding import PartitionSpec as P

F32 = jnp.float32
BF16 = jnp.bfloat16
VMEM_LIMIT = 48 * 1024 * 1024


def split2(a):
    high = a.astype(BF16)
    low = (a - high.astype(F32)).astype(BF16)
    return high, low


def mm(a, b):
    return jnp.dot(a, b, preferred_element_type=F32)


def mm_nt(a, b):
    return lax.dot_general(a, b, (((1,), (1,)), ((), ())), preferred_element_type=F32)


def mm_tn(a, b):
    return lax.dot_general(a, b, (((0,), (0,)), ((), ())), preferred_element_type=F32)


def mm_exact_right(a, b):
    high, low = split2(a)
    return mm(jnp.concatenate([high, low], axis=1), jnp.concatenate([b, b], axis=0))


def mm3(a, b):
    ah, al = split2(a)
    bh, bl = split2(b)
    return mm(jnp.concatenate([ah, al], axis=1), jnp.concatenate([bh, bh], axis=0)) + mm(ah, bl)


def compose(later, earlier, key_dim):
    moved = mm3(later[:, :key_dim], earlier)
    return jnp.concatenate(
        [moved[:, :key_dim], moved[:, key_dim:] + later[:, key_dim:]], axis=1
    )


def vmem(count):
    return [pl.BlockSpec(memory_space=pltpu.VMEM)] * count


SMEM_SPEC = pl.BlockSpec(memory_space=pltpu.SMEM)


def call(kernel, out_shape, scratch=(), flops=0, nbytes=0):
    def run(place, *arrays):
        return pl.pallas_call(
            kernel,
            out_shape=out_shape,
            in_specs=[SMEM_SPEC] + vmem(len(arrays)),
            out_specs=jax.tree.map(lambda _: pl.BlockSpec(memory_space=pltpu.VMEM), out_shape),
            scratch_shapes=list(scratch),
            compiler_params=pltpu.CompilerParams(vmem_limit_bytes=VMEM_LIMIT),
            cost_estimate=pl.CostEstimate(flops=flops, bytes_accessed=nbytes, transcendentals=0),
        )(place, *arrays)

    return run


def lane_cumsum(a):
    size = a.shape[1]
    lane = lax.broadcasted_iota(jnp.int32, a.shape, 1)
    step = 1
    while step < size:
        a = a + jnp.where(lane >= step, pltpu.roll(a, step, 1), 0.0)
        step *= 2
    return a


def head_rows(scratch, head, heads):
    count = scratch.shape[0] // heads
    return scratch[pl.ds(head, count, stride=heads), :]


def stage_rows(ref, scratch):
    wide = ref[...].astype(F32)
    scratch[...] = wide.reshape(scratch.shape)


def rolled(a, flip):
    half = a.shape[0] // 2
    return jnp.where(flip, jnp.concatenate([a[half:], a[:half]], axis=0), a)


def mm3_packed(lhs, rhs):
    rows = lhs.shape[0]
    width = rhs.shape[1] // 2
    high, low = split2(lhs)
    out = mm(jnp.concatenate([high, low], axis=0), rhs)
    return out[:rows, :width] + (out[:rows, width:] + out[rows:, :width])


def block_inverse(strict):
    size = strict[0].shape[0]
    base = min(16, size)
    rows = lax.broadcasted_iota(jnp.int32, (size, size), 0)
    cols = lax.broadcasted_iota(jnp.int32, (size, size), 1)

    def ones_where(mask):
        return jnp.where(mask, 1.0, 0.0).astype(BF16)

    def spread(compact, mask):
        count = size // compact.shape[0]
        return jnp.concatenate(
            [jnp.concatenate([part] * count, axis=0) * mask for part in split2(compact)], axis=1
        )

    lane = lax.broadcasted_iota(jnp.int32, (base, size), 1)
    line = lax.broadcasted_iota(jnp.int32, (base, size), 0)
    power, inverse = [], []
    for a in strict:
        compact = jnp.zeros((base, size), F32)
        for n in range(size // base):
            compact = jnp.where(lane // base == n, -a[n * base : (n + 1) * base, :], compact)
        power.append(compact)
        inverse.append(jnp.where(lane % base == line, 1.0, compact))
    mask = ones_where(rows // base == cols // base)
    wide = [spread(p, mask) for p in power]
    power = [mm3_packed(p, w) for p, w in zip(power, wide)]
    span = 2
    while span < base:
        wide = [spread(p, mask) for p in power]
        if span * 2 < base:
            both = [
                mm3_packed(jnp.concatenate([p, x], axis=0), w)
                for p, x, w in zip(power, inverse, wide)
            ]
            power = [a[:base] for a in both]
            inverse = [x + a[base:] for x, a in zip(inverse, both)]
        else:
            inverse = [x + mm3_packed(x, w) for x, w in zip(inverse, wide)]
        span *= 2
    parts = [split2(a) for a in strict]
    span = base
    while span < size:
        joint = ones_where(
            (rows // (2 * span) == cols // (2 * span)) & (rows // span != cols // span)
        )
        mask = ones_where(rows // span == cols // span)
        even = (
            (lax.broadcasted_iota(jnp.int32, (span, size), 1) // span) % 2
        ) == 0
        off = [jnp.concatenate([h * joint, l * joint], axis=1) for h, l in parts]
        first = [mm3_packed(x, o) for x, o in zip(inverse, off)]
        second = [mm3_packed(f, spread(x, mask)) for f, x in zip(first, inverse)]
        inverse = [
            jnp.concatenate([jnp.where(even, x, 0.0), jnp.where(even, -y, x)], axis=0)
            for x, y in zip(inverse, second)
        ]
        span *= 2
    return inverse


def updates_basis(inverse, k_raw, v_raw, beta, key_scale):
    key_part = mm_exact_right(inverse * key_scale, k_raw)
    value_part = mm_exact_right(inverse * beta, v_raw)
    return jnp.concatenate([key_part, value_part], axis=1)


def trailing_map(basis, trail, k_raw, last, eye_key, key_dim):
    bh, bl = split2(basis * trail)
    moved = mm_tn(
        jnp.concatenate([k_raw, k_raw], axis=0), jnp.concatenate([bh, bl], axis=0)
    )
    return jnp.concatenate(
        [moved[:, :key_dim] + jnp.where(eye_key, last, 0.0), moved[:, key_dim:]], axis=1
    )


def eye_mask(size):
    return lax.broadcasted_iota(jnp.int32, (size, size), 0) == lax.broadcasted_iota(
        jnp.int32, (size, size), 1
    )


def basis_kernel(
    place, k_hbm, v_hbm, g_hbm, b_hbm, m_ref, r_ref, kh_ref, trail_ref, rows_ref, inverse_ref, v_own_ref,
    k_ref, v_ref, g_ref, b_ref, ks, vs0, vs1, sems,
):
    copies = [
        pltpu.make_async_copy(src, dst, sems.at[n])
        for n, (src, dst) in enumerate(
            ((g_hbm, g_ref), (b_hbm, b_ref), (k_hbm, k_ref), (v_hbm, v_ref))
        )
    ]
    for copy in copies:
        copy.start()
    tok, heads, key_dim = k_ref.shape
    value_dim = v_ref.shape[2]
    half = heads // 2
    first_side = 1 - place[0]
    flip = first_side == 1
    order = [first_side * half + i for i in range(half)]
    order += [(1 - first_side) * half + i for i in range(half)]
    copies[0].wait()
    copies[1].wait()
    cum_row = lane_cumsum(rolled(g_ref[...], flip))
    beta_row = rolled(b_ref[...], flip)
    last_row = cum_row[:, tok - 1 :]
    decay_row = jnp.exp(cum_row)
    cum_col = cum_row.T
    beta_col = beta_row.T
    trail_col = jnp.exp(last_row - cum_row).T
    rows = lax.broadcasted_iota(jnp.int32, (tok, tok), 0)
    cols = lax.broadcasted_iota(jnp.int32, (tok, tok), 1)
    lower = rows > cols
    eye = rows == cols
    eye_key = eye_mask(key_dim)
    every = range(heads)
    copies[2].wait()
    stage_rows(k_ref, ks)
    k_wide = [head_rows(ks, h, heads) for h in order]
    k_raw = [a.astype(BF16) for a in k_wide]
    for i in every:
        kh_ref[i] = k_raw[i]
    gram = [mm_nt(a, a) for a in k_raw]
    inv_col = [lax.rsqrt(jnp.sum(a * a, axis=1, keepdims=True) + 1e-6) for a in k_wide]
    inv_row = [
        lax.rsqrt(jnp.sum(jnp.where(eye, a, 0.0), axis=0, keepdims=True) + 1e-6) for a in gram
    ]
    strict = []
    for i in every:
        gap = cum_col[:, i : i + 1] - cum_row[i : i + 1, :]
        decay = jnp.exp(jnp.where(lower, gap, 0.0))
        left = beta_col[:, i : i + 1] * inv_col[i]
        strict.append(jnp.where(lower, gram[i] * decay * left * inv_row[i], 0.0))
    inverse = block_inverse(strict)
    copies[3].wait()
    wide = v_ref[...].astype(F32)
    vs0[...] = wide[:, :, : value_dim // 2].reshape(vs0.shape)
    vs1[...] = wide[:, :, value_dim // 2 :].reshape(vs1.shape)
    rows_ref[0] = jnp.concatenate(inv_row, axis=0)
    rows_ref[1] = cum_row
    rows_ref[2] = beta_row
    rows_ref[3] = -(decay_row * beta_row * jnp.concatenate(inv_row, axis=0))
    for i in every:
        v_raw = jnp.concatenate(
            [head_rows(vs0, order[i], heads), head_rows(vs1, order[i], heads)], axis=1
        ).astype(BF16)
        trail = trail_col[:, i : i + 1] * inv_col[i]
        if i < half:
            beta_i = beta_row[i : i + 1, :]
            key_scale = -(decay_row[i : i + 1, :] * beta_i * inv_row[i])
            basis = updates_basis(inverse[i], k_raw[i], v_raw, beta_i, key_scale)
            r_ref[i] = basis
            m_ref[i] = trailing_map(
                basis, trail, k_raw[i], jnp.exp(last_row[i : i + 1, :]), eye_key, key_dim
            )
        else:
            trail_ref[i - half] = jnp.broadcast_to(trail, (tok, key_dim))
            inverse_ref[i - half] = inverse[i]
            v_own_ref[i - half] = v_raw


def own_map_kernel(place, inverse_ref, kh_ref, v_ref, trail_ref, rows_ref, m_ref, r_ref):
    half, key_dim, wide = m_ref.shape
    tok = r_ref.shape[1]
    eye_key = eye_mask(key_dim)
    for i in range(half):
        at = slice(half + i, half + i + 1)
        k_raw = kh_ref[half + i]
        basis = updates_basis(
            inverse_ref[i], k_raw, v_ref[i], rows_ref[2, at, :], rows_ref[3, at, :]
        )
        r_ref[i] = basis
        last = jnp.exp(rows_ref[1, at, tok - 1 :])
        m_ref[i] = trailing_map(basis, trail_ref[i][:, :1], k_raw, last, eye_key, key_dim)


def query_kernel(place, q_ref, kh_ref, rows_ref, r_give, r_own, got_ref, got_own_ref, f_ref, qs):
    heads, tok, key_dim = kh_ref.shape
    half = heads // 2
    core = place[0]
    stage_rows(q_ref, qs)
    cum_row = rows_ref[1]
    cum_col = cum_row.T
    rows = lax.broadcasted_iota(jnp.int32, (tok, tok), 0)
    cols = lax.broadcasted_iota(jnp.int32, (tok, tok), 1)
    lower = rows >= cols
    for i in range(heads):
        head = ((1 - core) * half + i) if i < half else (core * half + i - half)
        q_wide = head_rows(qs, head, heads)
        q_inv = lax.rsqrt(jnp.sum(q_wide * q_wide, axis=1, keepdims=True) + 1e-6)
        dots = mm_nt(q_wide.astype(BF16), kh_ref[i])
        gap = cum_col[:, i : i + 1] - cum_row[i : i + 1, :]
        decay = jnp.exp(jnp.where(lower, gap, 0.0))
        scores = jnp.where(lower, dots * decay * q_inv * rows_ref[0, i : i + 1, :], 0.0)
        folded = mm3(scores, r_give[i] if i < half else r_own[i - half])
        gated = q_wide * (q_inv * jnp.exp(cum_col[:, i : i + 1]))
        f_ref[i] = jnp.concatenate(
            [folded[:, :key_dim] + gated, folded[:, key_dim:]], axis=1
        )

    @pl.when(core == 1)
    def _():
        for i in range(heads):
            earlier = got_own_ref[i] if i < half else got_ref[i - half]
            f_ref[i] = compose(f_ref[i], earlier, key_dim)


def chip_kernel(key_dim, outs_per, place, own_ref, got_ref, *out_refs):
    core, chip = place[0], place[1]
    half = own_ref.shape[0]
    owners = half // outs_per
    for r, out in enumerate(out_refs):
        owner = jnp.bitwise_xor(chip, r)
        owner = jnp.where(owner < owners, owner, 0)
        for j in range(outs_per):
            head = owner * outs_per + j
            own, got = own_ref[head], got_ref[head]
            earlier = jnp.where(core == 0, own, got)
            later = jnp.where(core == 0, got, own)
            out[j] = compose(later, earlier, key_dim)


def in_order(chip, maps):
    maps = list(maps)
    bit = 1
    while bit < len(maps):
        swapped = jnp.bitwise_and(chip, bit) != 0
        maps = [jnp.where(swapped, maps[i ^ bit], maps[i]) for i in range(len(maps))]
        bit *= 2
    return maps


def total_kernel(key_dim, place, *refs):
    maps, total = refs[:-1], refs[-1]
    chip = place[1]
    for j in range(total.shape[0]):
        level = [ref[j] for ref in maps]
        bit = 1
        while len(level) > 1:
            swapped = jnp.bitwise_and(chip, bit) != 0
            level = [
                compose(
                    jnp.where(swapped, low, high), jnp.where(swapped, high, low), key_dim
                )
                for low, high in zip(level[::2], level[1::2])
            ]
            bit *= 2
        total[j] = level[0]


def prefix_kernel(key_dim, place, *refs):
    maps, prefix = refs[:-1], refs[-1]
    for j in range(prefix.shape[1]):
        ordered = in_order(place[1], [ref[j] for ref in maps])
        running = ordered[0]
        prefix[0, j] = running
        for index in range(1, len(ordered) - 1):
            running = compose(ordered[index], running, key_dim)
            prefix[index, j] = running


def is_upper(place, level):
    return jnp.bitwise_and(jnp.right_shift(place[2], level), 1) == 1


def group_total_kernel(key_dim, level, place, total_ref, got_ref, out_ref):
    upper = is_upper(place, level)
    for j in range(total_ref.shape[0]):
        mine, got = total_ref[j], got_ref[j]
        later = jnp.where(upper, mine, got)
        earlier = jnp.where(upper, got, mine)
        if out_ref.shape[2] == mine.shape[1]:
            out_ref[j] = compose(later, earlier, key_dim)
        else:
            out_ref[j] = mm3(later[:, :key_dim], earlier[:, key_dim:]) + later[:, key_dim:]


def before_kernel(key_dim, level, place, got_ref, prefix_ref, out_ref):
    upper = is_upper(place, level)
    count = out_ref.shape[0]

    @pl.when(upper)
    def _():
        for j in range(out_ref.shape[1]):
            for index in range(count):
                if prefix_ref.shape[0] == count:
                    out_ref[index, j] = compose(prefix_ref[index, j], got_ref[j], key_dim)
                elif index == 0:
                    out_ref[index, j] = got_ref[j]
                else:
                    out_ref[index, j] = compose(prefix_ref[index - 1, j], got_ref[j], key_dim)

    @pl.when(jnp.logical_not(upper))
    def _():
        for j in range(out_ref.shape[1]):
            for index in range(count):
                if prefix_ref.shape[0] == count:
                    out_ref[index, j] = prefix_ref[index, j]
                elif index == 0:
                    out_ref[index, j] = jnp.where(
                        lax.broadcasted_iota(jnp.int32, out_ref.shape[2:], 0)
                        == lax.broadcasted_iota(jnp.int32, out_ref.shape[2:], 1),
                        1.0,
                        0.0,
                    )
                else:
                    out_ref[index, j] = prefix_ref[index - 1, j]


def enter_kernel(key_dim, level, place, got_ref, prefix_ref, *out_refs):
    chip = place[1]
    upper = is_upper(place, level)
    for j in range(got_ref.shape[0]):
        eh, el = split2(jnp.where(upper, got_ref[j], 0.0))
        twice = jnp.concatenate([eh, eh], axis=0)
        for r, out in enumerate(out_refs):
            one = prefix_ref[jnp.bitwise_xor(chip, r), j]
            th, tl = split2(one[:, :key_dim])
            moved = mm(jnp.concatenate([th, tl], axis=1), twice) + mm(th, el)
            out[j] = moved + one[:, key_dim:]


def read_out(folded, state):
    key_dim = state.shape[0]
    return mm3(folded[:, :key_dim], state) + folded[:, key_dim:]


def early_kernel(per, owners, first, chips, place, f_ref, *refs):
    parts, out_ref = refs[:-1], refs[-1]
    half = f_ref.shape[0] // 2
    chip = place[1]
    count = len(parts) // 2
    for n in range(count):
        owner = jnp.bitwise_xor(chip, first + n)

        def both(owner=owner, n=n):
            for j in range(per):
                head = owner * per + j
                out_ref[n, 0, j] = read_out(f_ref[half + head], parts[n][j])
                out_ref[n, 1, j] = read_out(f_ref[head], parts[count + n][j])

        if owners < chips:
            pl.when(owner < owners)(both)
        else:
            both()


def output_kernel(per, owners, first, chips, place, f_ref, early_ref, *refs):
    o_ref, os0, os1 = refs[-3:]
    parts = refs[:-3]
    count = len(parts) // 2
    heads, tok, wide = f_ref.shape
    half = heads // 2
    core, chip = place[0], place[1]
    mid = o_ref.shape[2] // 2

    def put(head, out):
        os0[pl.ds(head, tok, stride=heads), :] = out[:, :mid]
        os1[pl.ds(head, tok, stride=heads), :] = out[:, mid:]

    for r in range(chips):
        owner = jnp.bitwise_xor(chip, r)

        def both(owner=owner, r=r):
            for j in range(per):
                head = owner * per + j
                if r < first:
                    own, other = early_ref[r, 0, j], early_ref[r, 1, j]
                else:
                    own = read_out(f_ref[half + head], parts[r - first][j])
                    other = read_out(f_ref[head], parts[count + r - first][j])
                put(core * half + head, own)
                put((1 - core) * half + head, other)

        if owners < chips:
            pl.when(owner < owners)(both)
        else:
            both()
    o_ref[:, :, :mid] = os0[...].reshape(tok, heads, mid).astype(BF16)
    o_ref[:, :, mid:] = os1[...].reshape(tok, heads, mid).astype(BF16)


def body(queries, key_rows, value_rows, log_gate, beta_rate):
    tok, heads, key_dim = queries.shape
    value_dim = value_rows.shape[2]
    wide = key_dim + value_dim
    half = heads // 2
    seq, grp = lax.axis_size("seq"), lax.axis_size("grp")
    chips = seq // 2
    owners = min(chips, half)
    per = half // owners
    place_seq, place_grp = lax.axis_index("seq"), lax.axis_index("grp")
    place = jnp.stack([place_seq % 2, place_seq // 2, place_grp]).astype(jnp.int32)
    f32 = lambda *shape: jax.ShapeDtypeStruct(shape, F32)
    tall = lambda width: pltpu.VMEM((tok * heads, width), F32)
    unit = 2 * tok * key_dim * key_dim
    sibling = [(i, i ^ 1) for i in range(seq)]

    give_map, give_basis, k_heads, trail, rows, inverse, v_own = pl.pallas_call(
        basis_kernel,
        out_shape=(
            f32(half, key_dim, wide),
            f32(half, tok, wide),
            jax.ShapeDtypeStruct((heads, tok, key_dim), BF16),
            f32(half, tok, key_dim),
            f32(4, heads, tok),
            f32(half, tok, tok),
            jax.ShapeDtypeStruct((half, tok, value_dim), BF16),
        ),
        in_specs=[SMEM_SPEC] + [pl.BlockSpec(memory_space=pltpu.HBM)] * 4,
        out_specs=tuple(vmem(7)),
        scratch_shapes=[
            pltpu.VMEM((tok, heads, key_dim), BF16),
            pltpu.VMEM((tok, heads, value_dim), BF16),
            pltpu.VMEM((heads, tok), F32),
            pltpu.VMEM((heads, tok), F32),
            tall(key_dim),
            tall(value_dim // 2),
            tall(value_dim // 2),
            pltpu.SemaphoreType.DMA((4,)),
        ],
        compiler_params=pltpu.CompilerParams(vmem_limit_bytes=VMEM_LIMIT),
        cost_estimate=pl.CostEstimate(
            flops=50 * heads * unit, bytes_accessed=0, transcendentals=0
        ),
    )(place, *(pltpu.with_memory_space_constraint(a, pltpu.HBM) for a in (key_rows, value_rows, log_gate, beta_rate)))
    got_map = lax.ppermute(give_map, "seq", sibling)
    own_map, own_basis = call(
        own_map_kernel,
        (f32(half, key_dim, wide), f32(half, tok, wide)),
        flops=12 * half * unit,
    )(place, inverse, k_heads, v_own, trail, rows)
    chip_maps = call(
        functools.partial(chip_kernel, key_dim, per), [f32(per, key_dim, wide)] * chips
    )(place, own_map, got_map)

    def across(parts, to_owner):
        moved = [parts[0]]
        for r in range(1, chips):
            pairs = [
                (i, i ^ (2 * r))
                for i in range(seq)
                if ((i ^ (2 * r)) // 2 if to_owner else i // 2) < owners
            ]
            moved.append(lax.ppermute(parts[r], "seq", pairs))
        return moved

    owned = across(chip_maps, True)
    got_own = lax.ppermute(own_map, "seq", sibling)
    folded = call(
        query_kernel, f32(heads, tok, wide), [tall(key_dim)], flops=20 * heads * unit
    )(place, queries, k_heads, rows, give_basis, own_basis, got_map, got_own)
    owned, folded = lax.optimization_barrier((owned, folded))
    total = call(functools.partial(total_kernel, key_dim), f32(per, key_dim, wide))(
        place, *owned
    )
    prefix = call(
        functools.partial(prefix_kernel, key_dim), f32(chips - 1, per, key_dim, wide)
    )(place, *owned)
    level = 0
    while 2 << level <= grp:
        swap = [(i, i ^ (1 << level)) for i in range(grp)]
        if 2 << level == grp:
            if level == 0:
                total = total[:, :, key_dim:]
            got_state = lax.ppermute(total, "grp", swap)
            states = call(
                functools.partial(enter_kernel, key_dim, level),
                [f32(per, key_dim, value_dim)] * chips,
            )(place, got_state, prefix)
        else:
            got = lax.ppermute(total, "grp", swap)
            width = value_dim if 4 << level == grp else wide
            total = call(
                functools.partial(group_total_kernel, key_dim, level), f32(per, key_dim, width)
            )(place, total, got)
            prefix = call(
                functools.partial(before_kernel, key_dim, level),
                f32(chips, per, key_dim, wide),
            )(place, got, prefix)
        level += 1
    arrived = across(states, False)
    others = [lax.ppermute(part, "seq", sibling) for part in arrived]
    first = max(chips // 2, 1)
    early = call(
        functools.partial(early_kernel, per, owners, 0, chips),
        f32(first, 2, per, tok, value_dim),
        flops=6 * first * per * unit,
    )(place, folded, *arrived[:first], *others[:first])
    return call(
        functools.partial(output_kernel, per, owners, first, chips),
        jax.ShapeDtypeStruct((tok, heads, value_dim), BF16),
        [tall(value_dim // 2), tall(value_dim // 2)],
    )(place, folded, early, *arrived[first:], *others[first:])


def solution(mesh):
    return jax.shard_map(
        body,
        mesh=mesh,
        in_specs=(
            P(("grp", "seq"), None, None),
            P(("grp", "seq"), None, None),
            P(("grp", "seq"), None, None),
            P(None, ("grp", "seq")),
            P(None, ("grp", "seq")),
        ),
        out_specs=P(("grp", "seq"), None, None),
        check_vma=False,
    )
```

```python
import functools

import jax
import jax.numpy as jnp
from jax import lax
from jax.experimental import pallas as pl
from jax.experimental.pallas import tpu as pltpu
from jax.sharding import PartitionSpec as P

F32 = jnp.float32
BF16 = jnp.bfloat16
VMEM_LIMIT = 48 * 1024 * 1024


def split2(a):
    high = a.astype(BF16)
    low = (a - high.astype(F32)).astype(BF16)
    return high, low


def mm(a, b):
    return jnp.dot(a, b, preferred_element_type=F32)


def mm_nt(a, b):
    return lax.dot_general(a, b, (((1,), (1,)), ((), ())), preferred_element_type=F32)


def mm_tn(a, b):
    return lax.dot_general(a, b, (((0,), (0,)), ((), ())), preferred_element_type=F32)


def mm_exact_right(a, b):
    high, low = split2(a)
    return mm(jnp.concatenate([high, low], axis=1), jnp.concatenate([b, b], axis=0))


def mm3(a, b):
    ah, al = split2(a)
    bh, bl = split2(b)
    return mm(jnp.concatenate([ah, al], axis=1), jnp.concatenate([bh, bh], axis=0)) + mm(ah, bl)


def compose(later, earlier, key_dim):
    moved = mm3(later[:, :key_dim], earlier)
    return jnp.concatenate(
        [moved[:, :key_dim], moved[:, key_dim:] + later[:, key_dim:]], axis=1
    )


def vmem(count):
    return [pl.BlockSpec(memory_space=pltpu.VMEM)] * count


def placed(kernel):
    def run(*refs):
        seq = lax.axis_index("seq")
        kernel((lax.rem(seq, 2), lax.div(seq, 2), lax.axis_index("grp")), *refs)

    return run


def call(kernel, out_shape, scratch=(), flops=0, nbytes=0):
    def run(*arrays):
        return pl.pallas_call(
            placed(kernel),
            out_shape=out_shape,
            in_specs=vmem(len(arrays)),
            out_specs=jax.tree.map(lambda _: pl.BlockSpec(memory_space=pltpu.VMEM), out_shape),
            scratch_shapes=list(scratch),
            compiler_params=pltpu.CompilerParams(vmem_limit_bytes=VMEM_LIMIT),
            cost_estimate=pl.CostEstimate(flops=flops, bytes_accessed=nbytes, transcendentals=0),
        )(*arrays)

    return run


def lane_cumsum(a):
    size = a.shape[1]
    lane = lax.broadcasted_iota(jnp.int32, a.shape, 1)
    step = 1
    while step < size:
        a = a + jnp.where(lane >= step, pltpu.roll(a, step, 1), 0.0)
        step *= 2
    return a


def head_rows(scratch, head, heads):
    count = scratch.shape[0] // heads
    return scratch[pl.ds(head, count, stride=heads), :]


def stage_rows(ref, scratch):
    wide = ref[...].astype(F32)
    scratch[...] = wide.reshape(scratch.shape)


def rolled(a, flip):
    half = a.shape[0] // 2
    return jnp.where(flip, jnp.concatenate([a[half:], a[:half]], axis=0), a)


def mm3_packed(lhs, rhs):
    rows = lhs.shape[0]
    width = rhs.shape[1] // 2
    high, low = split2(lhs)
    out = mm(jnp.concatenate([high, low], axis=0), rhs)
    return out[:rows, :width] + (out[:rows, width:] + out[rows:, :width])


def block_inverse(strict):
    size = strict[0].shape[0]
    base = min(16, size)
    rows = lax.broadcasted_iota(jnp.int32, (size, size), 0)
    cols = lax.broadcasted_iota(jnp.int32, (size, size), 1)

    def ones_where(mask):
        return jnp.where(mask, 1.0, 0.0).astype(BF16)

    def spread(compact, mask):
        count = size // compact.shape[0]
        return jnp.concatenate(
            [jnp.concatenate([part] * count, axis=0) * mask for part in split2(compact)], axis=1
        )

    lane = lax.broadcasted_iota(jnp.int32, (base, size), 1)
    line = lax.broadcasted_iota(jnp.int32, (base, size), 0)
    power, inverse = [], []
    for a in strict:
        compact = jnp.zeros((base, size), F32)
        for n in range(size // base):
            compact = jnp.where(lane // base == n, -a[n * base : (n + 1) * base, :], compact)
        power.append(compact)
        inverse.append(jnp.where(lane % base == line, 1.0, compact))
    mask = ones_where(rows // base == cols // base)
    wide = [spread(p, mask) for p in power]
    power = [mm3_packed(p, w) for p, w in zip(power, wide)]
    span = 2
    while span < base:
        wide = [spread(p, mask) for p in power]
        if span * 2 < base:
            both = [
                mm3_packed(jnp.concatenate([p, x], axis=0), w)
                for p, x, w in zip(power, inverse, wide)
            ]
            power = [a[:base] for a in both]
            inverse = [x + a[base:] for x, a in zip(inverse, both)]
        else:
            inverse = [x + mm3_packed(x, w) for x, w in zip(inverse, wide)]
        span *= 2
    parts = [split2(a) for a in strict]
    span = base
    while span < size:
        joint = ones_where(
            (rows // (2 * span) == cols // (2 * span)) & (rows // span != cols // span)
        )
        mask = ones_where(rows // span == cols // span)
        even = (
            (lax.broadcasted_iota(jnp.int32, (span, size), 1) // span) % 2
        ) == 0
        off = [jnp.concatenate([h * joint, l * joint], axis=1) for h, l in parts]
        first = [mm3_packed(x, o) for x, o in zip(inverse, off)]
        second = [mm3_packed(f, spread(x, mask)) for f, x in zip(first, inverse)]
        inverse = [
            jnp.concatenate([jnp.where(even, x, 0.0), jnp.where(even, -y, x)], axis=0)
            for x, y in zip(inverse, second)
        ]
        span *= 2
    return inverse


def updates_basis(inverse, k_raw, v_raw, beta, key_scale):
    key_part = mm_exact_right(inverse * key_scale, k_raw)
    value_part = mm_exact_right(inverse * beta, v_raw)
    return jnp.concatenate([key_part, value_part], axis=1)


def trailing_map(basis, trail, k_raw, last, eye_key, key_dim):
    bh, bl = split2(basis * trail)
    moved = mm_tn(
        jnp.concatenate([k_raw, k_raw], axis=0), jnp.concatenate([bh, bl], axis=0)
    )
    return jnp.concatenate(
        [moved[:, :key_dim] + jnp.where(eye_key, last, 0.0), moved[:, key_dim:]], axis=1
    )


def eye_mask(size):
    return lax.broadcasted_iota(jnp.int32, (size, size), 0) == lax.broadcasted_iota(
        jnp.int32, (size, size), 1
    )


def basis_kernel(
    place, k_hbm, v_hbm, g_hbm, b_hbm, m_ref, r_ref, kh_ref, trail_ref, rows_ref, inverse_ref, v_own_ref,
    k_ref, v_ref, g_ref, b_ref, ks, vs0, vs1, sems,
):
    copies = [
        pltpu.make_async_copy(src, dst, sems.at[n])
        for n, (src, dst) in enumerate(
            ((g_hbm, g_ref), (b_hbm, b_ref), (k_hbm, k_ref), (v_hbm, v_ref))
        )
    ]
    for copy in copies:
        copy.start()
    tok, heads, key_dim = k_ref.shape
    value_dim = v_ref.shape[2]
    half = heads // 2
    first_side = 1 - place[0]
    flip = first_side == 1
    order = [first_side * half + i for i in range(half)]
    order += [(1 - first_side) * half + i for i in range(half)]
    copies[0].wait()
    copies[1].wait()
    cum_row = lane_cumsum(rolled(g_ref[...], flip))
    beta_row = rolled(b_ref[...], flip)
    last_row = cum_row[:, tok - 1 :]
    decay_row = jnp.exp(cum_row)
    cum_col = cum_row.T
    beta_col = beta_row.T
    trail_col = jnp.exp(last_row - cum_row).T
    rows = lax.broadcasted_iota(jnp.int32, (tok, tok), 0)
    cols = lax.broadcasted_iota(jnp.int32, (tok, tok), 1)
    lower = rows > cols
    eye = rows == cols
    eye_key = eye_mask(key_dim)
    every = range(heads)
    copies[2].wait()
    stage_rows(k_ref, ks)
    k_wide = [head_rows(ks, h, heads) for h in order]
    k_raw = [a.astype(BF16) for a in k_wide]
    for i in every:
        kh_ref[i] = k_raw[i]
    gram = [mm_nt(a, a) for a in k_raw]
    inv_col = [lax.rsqrt(jnp.sum(a * a, axis=1, keepdims=True) + 1e-6) for a in k_wide]
    inv_row = [
        lax.rsqrt(jnp.sum(jnp.where(eye, a, 0.0), axis=0, keepdims=True) + 1e-6) for a in gram
    ]
    strict = []
    for i in every:
        gap = cum_col[:, i : i + 1] - cum_row[i : i + 1, :]
        decay = jnp.exp(jnp.where(lower, gap, 0.0))
        left = beta_col[:, i : i + 1] * inv_col[i]
        strict.append(jnp.where(lower, gram[i] * decay * left * inv_row[i], 0.0))
    copies[3].wait()
    wide = v_ref[...].astype(F32)
    vs0[...] = wide[:, :, : value_dim // 2].reshape(vs0.shape)
    vs1[...] = wide[:, :, value_dim // 2 :].reshape(vs1.shape)
    v_raw = [
        jnp.concatenate(
            [head_rows(vs0, h, heads), head_rows(vs1, h, heads)], axis=1
        ).astype(BF16)
        for h in order
    ]
    for i in range(half):
        v_own_ref[i] = v_raw[half + i]
    inverse = block_inverse(strict)
    rows_ref[0] = jnp.concatenate(inv_row, axis=0)
    rows_ref[1] = cum_row
    rows_ref[2] = beta_row
    rows_ref[3] = -(decay_row * beta_row * jnp.concatenate(inv_row, axis=0))
    for i in every:
        trail = trail_col[:, i : i + 1] * inv_col[i]
        if i < half:
            beta_i = beta_row[i : i + 1, :]
            key_scale = -(decay_row[i : i + 1, :] * beta_i * inv_row[i])
            basis = updates_basis(inverse[i], k_raw[i], v_raw[i], beta_i, key_scale)
            r_ref[i] = basis
            m_ref[i] = trailing_map(
                basis, trail, k_raw[i], jnp.exp(last_row[i : i + 1, :]), eye_key, key_dim
            )
        else:
            trail_ref[i - half] = jnp.broadcast_to(trail, (tok, key_dim))
            inverse_ref[i - half] = inverse[i]


def own_map_kernel(place, inverse_ref, kh_ref, v_ref, trail_ref, rows_ref, m_ref, r_ref):
    half, key_dim, wide = m_ref.shape
    tok = r_ref.shape[1]
    eye_key = eye_mask(key_dim)
    for i in range(half):
        at = slice(half + i, half + i + 1)
        k_raw = kh_ref[half + i]
        basis = updates_basis(
            inverse_ref[i], k_raw, v_ref[i], rows_ref[2, at, :], rows_ref[3, at, :]
        )
        r_ref[i] = basis
        last = jnp.exp(rows_ref[1, at, tok - 1 :])
        m_ref[i] = trailing_map(basis, trail_ref[i][:, :1], k_raw, last, eye_key, key_dim)


def query_kernel(place, q_ref, kh_ref, rows_ref, r_give, r_own, got_ref, got_own_ref, f_ref, qs):
    heads, tok, key_dim = kh_ref.shape
    half = heads // 2
    core = place[0]
    stage_rows(q_ref, qs)
    cum_row = rows_ref[1]
    cum_col = cum_row.T
    rows = lax.broadcasted_iota(jnp.int32, (tok, tok), 0)
    cols = lax.broadcasted_iota(jnp.int32, (tok, tok), 1)
    lower = rows >= cols
    for i in range(heads):
        head = ((1 - core) * half + i) if i < half else (core * half + i - half)
        q_wide = head_rows(qs, head, heads)
        q_inv = lax.rsqrt(jnp.sum(q_wide * q_wide, axis=1, keepdims=True) + 1e-6)
        dots = mm_nt(q_wide.astype(BF16), kh_ref[i])
        gap = cum_col[:, i : i + 1] - cum_row[i : i + 1, :]
        decay = jnp.exp(jnp.where(lower, gap, 0.0))
        scores = jnp.where(lower, dots * decay * q_inv * rows_ref[0, i : i + 1, :], 0.0)
        folded = mm3(scores, r_give[i] if i < half else r_own[i - half])
        gated = q_wide * (q_inv * jnp.exp(cum_col[:, i : i + 1]))
        f_ref[i] = jnp.concatenate(
            [folded[:, :key_dim] + gated, folded[:, key_dim:]], axis=1
        )

    @pl.when(core == 1)
    def _():
        for i in range(heads):
            earlier = got_own_ref[i] if i < half else got_ref[i - half]
            f_ref[i] = compose(f_ref[i], earlier, key_dim)


def chip_kernel(key_dim, outs_per, place, own_ref, got_ref, *out_refs):
    core, chip = place[0], place[1]
    half = own_ref.shape[0]
    owners = half // outs_per
    for r, out in enumerate(out_refs):
        owner = jnp.bitwise_xor(chip, r)
        owner = jnp.where(owner < owners, owner, 0)
        for j in range(outs_per):
            head = owner * outs_per + j
            own, got = own_ref[head], got_ref[head]
            earlier = jnp.where(core == 0, own, got)
            later = jnp.where(core == 0, got, own)
            out[j] = compose(later, earlier, key_dim)


def in_order(chip, maps):
    maps = list(maps)
    bit = 1
    while bit < len(maps):
        swapped = jnp.bitwise_and(chip, bit) != 0
        maps = [jnp.where(swapped, maps[i ^ bit], maps[i]) for i in range(len(maps))]
        bit *= 2
    return maps


def total_kernel(key_dim, place, *refs):
    maps, total = refs[:-1], refs[-1]
    chip = place[1]
    for j in range(total.shape[0]):
        level = [ref[j] for ref in maps]
        bit = 1
        while len(level) > 1:
            swapped = jnp.bitwise_and(chip, bit) != 0
            level = [
                compose(
                    jnp.where(swapped, low, high), jnp.where(swapped, high, low), key_dim
                )
                for low, high in zip(level[::2], level[1::2])
            ]
            bit *= 2
        total[j] = level[0]


def prefix_kernel(key_dim, place, *refs):
    maps, prefix = refs[:-1], refs[-1]
    for j in range(prefix.shape[1]):
        ordered = in_order(place[1], [ref[j] for ref in maps])
        running = ordered[0]
        prefix[0, j] = running
        for index in range(1, len(ordered) - 1):
            running = compose(ordered[index], running, key_dim)
            prefix[index, j] = running


def is_upper(place, level):
    return jnp.bitwise_and(jnp.right_shift(place[2], level), 1) == 1


def group_total_kernel(key_dim, level, place, total_ref, got_ref, out_ref):
    upper = is_upper(place, level)
    for j in range(total_ref.shape[0]):
        mine, got = total_ref[j], got_ref[j]
        later = jnp.where(upper, mine, got)
        earlier = jnp.where(upper, got, mine)
        if out_ref.shape[2] == mine.shape[1]:
            out_ref[j] = compose(later, earlier, key_dim)
        else:
            out_ref[j] = mm3(later[:, :key_dim], earlier[:, key_dim:]) + later[:, key_dim:]


def before_kernel(key_dim, level, place, got_ref, prefix_ref, out_ref):
    upper = is_upper(place, level)
    count = out_ref.shape[0]

    @pl.when(upper)
    def _():
        for j in range(out_ref.shape[1]):
            for index in range(count):
                if prefix_ref.shape[0] == count:
                    out_ref[index, j] = compose(prefix_ref[index, j], got_ref[j], key_dim)
                elif index == 0:
                    out_ref[index, j] = got_ref[j]
                else:
                    out_ref[index, j] = compose(prefix_ref[index - 1, j], got_ref[j], key_dim)

    @pl.when(jnp.logical_not(upper))
    def _():
        for j in range(out_ref.shape[1]):
            for index in range(count):
                if prefix_ref.shape[0] == count:
                    out_ref[index, j] = prefix_ref[index, j]
                elif index == 0:
                    out_ref[index, j] = jnp.where(
                        lax.broadcasted_iota(jnp.int32, out_ref.shape[2:], 0)
                        == lax.broadcasted_iota(jnp.int32, out_ref.shape[2:], 1),
                        1.0,
                        0.0,
                    )
                else:
                    out_ref[index, j] = prefix_ref[index - 1, j]


def enter_kernel(key_dim, level, place, got_ref, prefix_ref, *out_refs):
    chip = place[1]
    upper = is_upper(place, level)
    for j in range(got_ref.shape[0]):
        eh, el = split2(jnp.where(upper, got_ref[j], 0.0))
        twice = jnp.concatenate([eh, eh], axis=0)
        for r, out in enumerate(out_refs):
            one = prefix_ref[jnp.bitwise_xor(chip, r), j]
            th, tl = split2(one[:, :key_dim])
            moved = mm(jnp.concatenate([th, tl], axis=1), twice) + mm(th, el)
            out[j] = moved + one[:, key_dim:]


def read_out(folded, state):
    key_dim = state.shape[0]
    return mm3(folded[:, :key_dim], state) + folded[:, key_dim:]


def early_kernel(per, owners, first, chips, place, f_ref, *refs):
    parts, out_ref = refs[:-1], refs[-1]
    half = f_ref.shape[0] // 2
    chip = place[1]
    count = len(parts) // 2
    for n in range(count):
        owner = jnp.bitwise_xor(chip, first + n)

        def both(owner=owner, n=n):
            for j in range(per):
                head = owner * per + j
                out_ref[n, 0, j] = read_out(f_ref[half + head], parts[n][j])
                out_ref[n, 1, j] = read_out(f_ref[head], parts[count + n][j])

        if owners < chips:
            pl.when(owner < owners)(both)
        else:
            both()


def output_kernel(per, owners, first, chips, place, f_ref, early_ref, *refs):
    o_ref, os0, os1 = refs[-3:]
    parts = refs[:-3]
    count = len(parts) // 2
    heads, tok, wide = f_ref.shape
    half = heads // 2
    core, chip = place[0], place[1]
    mid = o_ref.shape[2] // 2

    def put(head, out):
        os0[pl.ds(head, tok, stride=heads), :] = out[:, :mid]
        os1[pl.ds(head, tok, stride=heads), :] = out[:, mid:]

    for r in range(chips):
        owner = jnp.bitwise_xor(chip, r)

        def both(owner=owner, r=r):
            for j in range(per):
                head = owner * per + j
                if r < first:
                    own, other = early_ref[r, 0, j], early_ref[r, 1, j]
                else:
                    own = read_out(f_ref[half + head], parts[r - first][j])
                    other = read_out(f_ref[head], parts[count + r - first][j])
                put(core * half + head, own)
                put((1 - core) * half + head, other)

        if owners < chips:
            pl.when(owner < owners)(both)
        else:
            both()
    o_ref[:, :, :mid] = os0[...].reshape(tok, heads, mid).astype(BF16)
    o_ref[:, :, mid:] = os1[...].reshape(tok, heads, mid).astype(BF16)


def body(queries, key_rows, value_rows, log_gate, beta_rate):
    tok, heads, key_dim = queries.shape
    value_dim = value_rows.shape[2]
    wide = key_dim + value_dim
    half = heads // 2
    seq, grp = lax.axis_size("seq"), lax.axis_size("grp")
    chips = seq // 2
    owners = min(chips, half)
    per = half // owners
    f32 = lambda *shape: jax.ShapeDtypeStruct(shape, F32)
    tall = lambda width: pltpu.VMEM((tok * heads, width), F32)
    unit = 2 * tok * key_dim * key_dim
    sibling = [(i, i ^ 1) for i in range(seq)]

    give_map, give_basis, k_heads, trail, rows, inverse, v_own = pl.pallas_call(
        placed(basis_kernel),
        out_shape=(
            f32(half, key_dim, wide),
            f32(half, tok, wide),
            jax.ShapeDtypeStruct((heads, tok, key_dim), BF16),
            f32(half, tok, key_dim),
            f32(4, heads, tok),
            f32(half, tok, tok),
            jax.ShapeDtypeStruct((half, tok, value_dim), BF16),
        ),
        in_specs=[pl.BlockSpec(memory_space=pltpu.HBM)] * 4,
        out_specs=tuple(vmem(7)),
        scratch_shapes=[
            pltpu.VMEM((tok, heads, key_dim), BF16),
            pltpu.VMEM((tok, heads, value_dim), BF16),
            pltpu.VMEM((heads, tok), F32),
            pltpu.VMEM((heads, tok), F32),
            tall(key_dim),
            tall(value_dim // 2),
            tall(value_dim // 2),
            pltpu.SemaphoreType.DMA((4,)),
        ],
        compiler_params=pltpu.CompilerParams(vmem_limit_bytes=VMEM_LIMIT),
        cost_estimate=pl.CostEstimate(
            flops=50 * heads * unit, bytes_accessed=0, transcendentals=0
        ),
    )(*(pltpu.with_memory_space_constraint(a, pltpu.HBM) for a in (key_rows, value_rows, log_gate, beta_rate)))
    got_map = lax.ppermute(give_map, "seq", sibling)
    own_map, own_basis = call(
        own_map_kernel,
        (f32(half, key_dim, wide), f32(half, tok, wide)),
        flops=12 * half * unit,
    )(inverse, k_heads, v_own, trail, rows)
    chip_maps = call(
        functools.partial(chip_kernel, key_dim, per), [f32(per, key_dim, wide)] * chips
    )(own_map, got_map)

    def across(parts, to_owner):
        moved = [parts[0]]
        for r in range(1, chips):
            pairs = [
                (i, i ^ (2 * r))
                for i in range(seq)
                if ((i ^ (2 * r)) // 2 if to_owner else i // 2) < owners
            ]
            moved.append(lax.ppermute(parts[r], "seq", pairs))
        return moved

    owned = across(chip_maps, True)
    got_own = lax.ppermute(own_map, "seq", sibling)
    folded = call(
        query_kernel, f32(heads, tok, wide), [tall(key_dim)], flops=20 * heads * unit
    )(queries, k_heads, rows, give_basis, own_basis, got_map, got_own)
    owned, folded = lax.optimization_barrier((owned, folded))
    total = call(functools.partial(total_kernel, key_dim), f32(per, key_dim, wide))(
        *owned
    )
    prefix = call(
        functools.partial(prefix_kernel, key_dim), f32(chips - 1, per, key_dim, wide)
    )(*owned)
    level = 0
    while 2 << level <= grp:
        swap = [(i, i ^ (1 << level)) for i in range(grp)]
        if 2 << level == grp:
            if level == 0:
                total = total[:, :, key_dim:]
            got_state = lax.ppermute(total, "grp", swap)
            states = call(
                functools.partial(enter_kernel, key_dim, level),
                [f32(per, key_dim, value_dim)] * chips,
            )(got_state, prefix)
        else:
            got = lax.ppermute(total, "grp", swap)
            width = value_dim if 4 << level == grp else wide
            total = call(
                functools.partial(group_total_kernel, key_dim, level), f32(per, key_dim, width)
            )(total, got)
            prefix = call(
                functools.partial(before_kernel, key_dim, level),
                f32(chips, per, key_dim, wide),
            )(got, prefix)
        level += 1
    arrived = across(states, False)
    others = [lax.ppermute(part, "seq", sibling) for part in arrived]
    first = max(chips // 2, 1)
    early = call(
        functools.partial(early_kernel, per, owners, 0, chips),
        f32(first, 2, per, tok, value_dim),
        flops=6 * first * per * unit,
    )(folded, *arrived[:first], *others[:first])
    return call(
        functools.partial(output_kernel, per, owners, first, chips),
        jax.ShapeDtypeStruct((tok, heads, value_dim), BF16),
        [tall(value_dim // 2), tall(value_dim // 2)],
    )(folded, early, *arrived[first:], *others[first:])


def solution(mesh):
    return jax.shard_map(
        body,
        mesh=mesh,
        in_specs=(
            P(("grp", "seq"), None, None),
            P(("grp", "seq"), None, None),
            P(("grp", "seq"), None, None),
            P(None, ("grp", "seq")),
            P(None, ("grp", "seq")),
        ),
        out_specs=P(("grp", "seq"), None, None),
        check_vma=False,
    )
```

```python
import functools

import jax
import jax.numpy as jnp
from jax import lax
from jax.experimental import pallas as pl
from jax.experimental.pallas import tpu as pltpu
from jax.sharding import PartitionSpec as P

F32 = jnp.float32
BF16 = jnp.bfloat16
VMEM_LIMIT = 48 * 1024 * 1024


def split2(a):
    high = a.astype(BF16)
    low = (a - high.astype(F32)).astype(BF16)
    return high, low


def mm(a, b):
    return jnp.dot(a, b, preferred_element_type=F32)


def mm_nt(a, b):
    return lax.dot_general(a, b, (((1,), (1,)), ((), ())), preferred_element_type=F32)


def mm_tn(a, b):
    return lax.dot_general(a, b, (((0,), (0,)), ((), ())), preferred_element_type=F32)


def mm_exact_right(a, b):
    high, low = split2(a)
    return mm(jnp.concatenate([high, low], axis=1), jnp.concatenate([b, b], axis=0))


def mm3(a, b):
    ah, al = split2(a)
    bh, bl = split2(b)
    return mm(jnp.concatenate([ah, al], axis=1), jnp.concatenate([bh, bh], axis=0)) + mm(ah, bl)


def compose(later, earlier, key_dim):
    moved = mm3(later[:, :key_dim], earlier)
    return jnp.concatenate(
        [moved[:, :key_dim], moved[:, key_dim:] + later[:, key_dim:]], axis=1
    )


def turned(distance, chips):
    bits = chips.bit_length() - 1
    low = bits // 2
    return (distance >> low) | ((distance & ((1 << low) - 1)) << (bits - low))


def slot_list(chips):
    plain = [chips - 1] + list(range(1, chips - 1)) + [0] if chips > 1 else [0]
    return plain, plain


def owner_of(slot, core, chip, chips):
    plain, other = slot_list(chips)
    if plain[slot] == other[slot]:
        return jnp.bitwise_xor(chip, plain[slot])
    return jnp.bitwise_xor(chip, jnp.where(core == 0, plain[slot], other[slot]))


def by_distance(core, maps):
    plain, other = slot_list(len(maps))
    ordered = []
    for d in range(len(maps)):
        a, b = maps[plain.index(d)], maps[other.index(d)]
        ordered.append(a if plain.index(d) == other.index(d) else jnp.where(core == 0, a, b))
    return ordered


def local_heads(core, chip, chips, half):
    if half % chips:
        return list(range(half))
    per = half // chips
    return [owner_of(n // per, core, chip, chips) * per + n % per for n in range(half)]


def positions(heads, per):
    half = heads // 2
    first = [*range(per), *range(half, half + per)]
    return first, [n for n in range(heads) if n not in first]


def vmem(count):
    return [pl.BlockSpec(memory_space=pltpu.VMEM)] * count


def placed(kernel):
    def run(*refs):
        seq = lax.axis_index("seq")
        kernel((lax.rem(seq, 2), lax.div(seq, 2), lax.axis_index("grp")), *refs)

    return run


def call(kernel, out_shape, scratch=(), flops=0, nbytes=0):
    def run(*arrays):
        return pl.pallas_call(
            placed(kernel),
            out_shape=out_shape,
            in_specs=vmem(len(arrays)),
            out_specs=jax.tree.map(lambda _: pl.BlockSpec(memory_space=pltpu.VMEM), out_shape),
            scratch_shapes=list(scratch),
            compiler_params=pltpu.CompilerParams(vmem_limit_bytes=VMEM_LIMIT),
            cost_estimate=pl.CostEstimate(flops=flops, bytes_accessed=nbytes, transcendentals=0),
        )(*arrays)

    return run


def lane_cumsum(a):
    size = a.shape[1]
    lane = lax.broadcasted_iota(jnp.int32, a.shape, 1)
    step = 1
    while step < size:
        a = a + jnp.where(lane >= step, pltpu.roll(a, step, 1), 0.0)
        step *= 2
    return a


def head_rows(scratch, head, heads):
    count = scratch.shape[0] // heads
    return scratch[pl.ds(head, count, stride=heads), :]


def stage_rows(ref, scratch):
    wide = ref[...].astype(F32)
    scratch[...] = wide.reshape(scratch.shape)


def mm3_packed(lhs, rhs):
    rows = lhs.shape[0]
    width = rhs.shape[1] // 2
    high, low = split2(lhs)
    out = mm(jnp.concatenate([high, low], axis=0), rhs)
    return out[:rows, :width] + (out[:rows, width:] + out[rows:, :width])


def block_inverse(strict):
    size = strict[0].shape[0]
    base = min(16, size)
    rows = lax.broadcasted_iota(jnp.int32, (size, size), 0)
    cols = lax.broadcasted_iota(jnp.int32, (size, size), 1)

    def ones_where(mask):
        return jnp.where(mask, 1.0, 0.0).astype(BF16)

    def spread(compact, mask):
        count = size // compact.shape[0]
        return jnp.concatenate(
            [jnp.concatenate([part] * count, axis=0) * mask for part in split2(compact)], axis=1
        )

    lane = lax.broadcasted_iota(jnp.int32, (base, size), 1)
    line = lax.broadcasted_iota(jnp.int32, (base, size), 0)
    power, inverse = [], []
    for a in strict:
        compact = jnp.zeros((base, size), F32)
        for n in range(size // base):
            compact = jnp.where(lane // base == n, -a[n * base : (n + 1) * base, :], compact)
        power.append(compact)
        inverse.append(jnp.where(lane % base == line, 1.0, compact))
    mask = ones_where(rows // base == cols // base)
    wide = [spread(p, mask) for p in power]
    power = [mm3_packed(p, w) for p, w in zip(power, wide)]
    span = 2
    while span < base:
        wide = [spread(p, mask) for p in power]
        if span * 2 < base:
            both = [
                mm3_packed(jnp.concatenate([p, x], axis=0), w)
                for p, x, w in zip(power, inverse, wide)
            ]
            power = [a[:base] for a in both]
            inverse = [x + a[base:] for x, a in zip(inverse, both)]
        else:
            inverse = [x + mm3_packed(x, w) for x, w in zip(inverse, wide)]
        span *= 2
    parts = [split2(a) for a in strict]
    span = base
    while span < size:
        joint = ones_where(
            (rows // (2 * span) == cols // (2 * span)) & (rows // span != cols // span)
        )
        mask = ones_where(rows // span == cols // span)
        even = (
            (lax.broadcasted_iota(jnp.int32, (span, size), 1) // span) % 2
        ) == 0
        off = [jnp.concatenate([h * joint, l * joint], axis=1) for h, l in parts]
        first = [mm3_packed(x, o) for x, o in zip(inverse, off)]
        second = [mm3_packed(f, spread(x, mask)) for f, x in zip(first, inverse)]
        inverse = [
            jnp.concatenate([jnp.where(even, x, 0.0), jnp.where(even, -y, x)], axis=0)
            for x, y in zip(inverse, second)
        ]
        span *= 2
    return inverse


def updates_basis(inverse, k_raw, v_raw, beta, key_scale):
    key_part = mm_exact_right(inverse * key_scale, k_raw)
    value_part = mm_exact_right(inverse * beta, v_raw)
    return jnp.concatenate([key_part, value_part], axis=1)


def trailing_map(basis, trail, k_raw, last, eye_key, key_dim):
    bh, bl = split2(basis * trail)
    moved = mm_tn(
        jnp.concatenate([k_raw, k_raw], axis=0), jnp.concatenate([bh, bl], axis=0)
    )
    return jnp.concatenate(
        [moved[:, :key_dim] + jnp.where(eye_key, last, 0.0), moved[:, key_dim:]], axis=1
    )


def eye_mask(size):
    return lax.broadcasted_iota(jnp.int32, (size, size), 0) == lax.broadcasted_iota(
        jnp.int32, (size, size), 1
    )


def basis_kernel(
    chips, per, place, k_hbm, v_hbm, g_hbm, b_hbm,
    give_ref, own_ref, r_ref, kh_ref, trail_ref, rows_ref, inverse_ref, v_rest_ref,
    k_ref, v_ref, g_ref, b_ref, ks, vs0, vs1, sems,
):
    copies = [
        pltpu.make_async_copy(src, dst, sems.at[n])
        for n, (src, dst) in enumerate(
            ((k_hbm, k_ref), (g_hbm, g_ref), (b_hbm, b_ref), (v_hbm, v_ref))
        )
    ]
    for copy in copies:
        copy.start()
    tok, heads, key_dim = k_ref.shape
    value_dim = v_ref.shape[2]
    half = heads // 2
    core, chip = place[0], place[1]
    order = [(1 - core) * half + h for h in local_heads(1 - core, chip, chips, half)]
    order += [core * half + h for h in local_heads(core, chip, chips, half)]
    copies[1].wait()
    copies[2].wait()

    def picked(ref):
        return jnp.concatenate([ref[pl.ds(h, 1), :] for h in order], axis=0)

    cum_row = lane_cumsum(picked(g_ref))
    beta_row = picked(b_ref)
    last_row = cum_row[:, tok - 1 :]
    decay_row = jnp.exp(cum_row)
    cum_col = cum_row.T
    beta_col = beta_row.T
    trail_col = jnp.exp(last_row - cum_row).T
    rows = lax.broadcasted_iota(jnp.int32, (tok, tok), 0)
    cols = lax.broadcasted_iota(jnp.int32, (tok, tok), 1)
    lower = rows > cols
    eye = rows == cols
    eye_key = eye_mask(key_dim)
    every = range(heads)
    copies[0].wait()
    stage_rows(k_ref, ks)
    k_wide = [head_rows(ks, h, heads) for h in order]
    k_raw = [a.astype(BF16) for a in k_wide]
    for i in every:
        kh_ref[i] = k_raw[i]
    gram = [mm_nt(a, a) for a in k_raw]
    inv_col = [lax.rsqrt(jnp.sum(a * a, axis=1, keepdims=True) + 1e-6) for a in k_wide]
    inv_row = [
        lax.rsqrt(jnp.sum(jnp.where(eye, a, 0.0), axis=0, keepdims=True) + 1e-6) for a in gram
    ]
    strict = []
    for i in every:
        gap = cum_col[:, i : i + 1] - cum_row[i : i + 1, :]
        decay = jnp.exp(jnp.where(lower, gap, 0.0))
        left = beta_col[:, i : i + 1] * inv_col[i]
        strict.append(jnp.where(lower, gram[i] * decay * left * inv_row[i], 0.0))
    copies[3].wait()
    wide = v_ref[...].astype(F32)
    vs0[...] = wide[:, :, : value_dim // 2].reshape(vs0.shape)
    vs1[...] = wide[:, :, value_dim // 2 :].reshape(vs1.shape)
    v_raw = [
        jnp.concatenate(
            [head_rows(vs0, h, heads), head_rows(vs1, h, heads)], axis=1
        ).astype(BF16)
        for h in order
    ]
    first, rest = positions(heads, per)
    for n, i in enumerate(rest):
        v_rest_ref[n] = v_raw[i]
    inverse = block_inverse(strict)
    rows_ref[0] = jnp.concatenate(inv_row, axis=0)
    rows_ref[1] = cum_row
    rows_ref[2] = beta_row
    rows_ref[3] = -(decay_row * beta_row * jnp.concatenate(inv_row, axis=0))
    for n, i in enumerate(first):
        trail = trail_col[:, i : i + 1] * inv_col[i]
        beta_i = beta_row[i : i + 1, :]
        key_scale = -(decay_row[i : i + 1, :] * beta_i * inv_row[i])
        basis = updates_basis(inverse[i], k_raw[i], v_raw[i], beta_i, key_scale)
        r_ref[n] = basis
        made = trailing_map(
            basis, trail, k_raw[i], jnp.exp(last_row[i : i + 1, :]), eye_key, key_dim
        )
        if n < per:
            give_ref[n] = made
        else:
            own_ref[n - per] = made
    for n, i in enumerate(rest):
        trail_ref[n] = jnp.broadcast_to(trail_col[:, i : i + 1] * inv_col[i], (tok, key_dim))
        inverse_ref[n] = inverse[i]


def rest_kernel(place, inverse_ref, kh_ref, v_ref, trail_ref, rows_ref, give_ref, own_ref, r_ref):
    rest, tok, wide = r_ref.shape
    key_dim = wide - v_ref.shape[2]
    heads = kh_ref.shape[0]
    eye_key = eye_mask(key_dim)
    for n, i in enumerate(positions(heads, (heads - rest) // 2)[1]):
        at = slice(i, i + 1)
        k_raw = kh_ref[i]
        basis = updates_basis(
            inverse_ref[n], k_raw, v_ref[n], rows_ref[2, at, :], rows_ref[3, at, :]
        )
        r_ref[n] = basis
        last = jnp.exp(rows_ref[1, at, tok - 1 :])
        made = trailing_map(basis, trail_ref[n][:, :1], k_raw, last, eye_key, key_dim)
        if n < rest // 2:
            give_ref[n] = made
        else:
            own_ref[n - rest // 2] = made


def query_rows(chips, place, q_ref, kh_ref, rows_ref, r_first, r_rest, f_ref, qs):
    heads, tok, key_dim = kh_ref.shape
    half = heads // 2
    first, rest = positions(heads, r_first.shape[0] // 2)
    core, chip = place[0], place[1]
    order = [(1 - core) * half + h for h in local_heads(1 - core, chip, chips, half)]
    order += [core * half + h for h in local_heads(core, chip, chips, half)]
    stage_rows(q_ref, qs)
    cum_row = rows_ref[1]
    cum_col = cum_row.T
    rows = lax.broadcasted_iota(jnp.int32, (tok, tok), 0)
    cols = lax.broadcasted_iota(jnp.int32, (tok, tok), 1)
    lower = rows >= cols
    for i in range(heads):
        q_wide = head_rows(qs, order[i], heads)
        q_inv = lax.rsqrt(jnp.sum(q_wide * q_wide, axis=1, keepdims=True) + 1e-6)
        dots = mm_nt(q_wide.astype(BF16), kh_ref[i])
        gap = cum_col[:, i : i + 1] - cum_row[i : i + 1, :]
        decay = jnp.exp(jnp.where(lower, gap, 0.0))
        scores = jnp.where(lower, dots * decay * q_inv * rows_ref[0, i : i + 1, :], 0.0)
        folded = mm3(scores, r_first[first.index(i)] if i in first else r_rest[rest.index(i)])
        gated = q_wide * (q_inv * jnp.exp(cum_col[:, i : i + 1]))
        f_ref[i] = jnp.concatenate(
            [folded[:, :key_dim] + gated, folded[:, key_dim:]], axis=1
        )


def query_kernel(chips, place, *refs):
    @pl.when(place[0] == 0)
    def _():
        query_rows(chips, place, *refs)


def query_late_kernel(chips, place, done_ref, *refs):
    f_ref = refs[-2]

    @pl.when(place[0] == 0)
    def _():
        f_ref[...] = done_ref[...]

    @pl.when(place[0] != 0)
    def _():
        query_rows(chips, place, *refs)


def read_out(folded, state):
    key_dim = state.shape[0]
    return mm3(folded[:, :key_dim], state) + folded[:, key_dim:]


def pair_kernel(chips, slot, place, *refs):
    map_refs, (state_ref, keep_ref, give_ref) = refs[:-3], refs[-3:]
    core, chip = place[0], place[1]
    per = state_ref.shape[0]
    for j in range(per):
        own, got = picked_maps(map_refs, slot, j, per, chips, core, chip)
        state = state_ref[j]
        second = read_out(jnp.where(core == 0, own, got), state)
        keep_ref[j] = jnp.where(core == 0, state, second)
        give_ref[j] = jnp.where(core == 0, second, state)


def picked_maps(refs, slot, j, per, chips, core, chip):
    own_first, own_rest, got_first, got_rest = refs
    half = per + own_rest.shape[0]
    if half % chips:
        at = owner_of(slot, core, chip, chips) * per + j
        at_tail = jnp.clip(at - per, 0, half - per - 1)
        return tuple(
            jnp.where(at < per, first[0], rest[at_tail])
            for first, rest in ((own_first, own_rest), (got_first, got_rest))
        )
    at = slot * per + j
    if at < per:
        return own_first[at], got_first[at]
    return own_rest[at - per], got_rest[at - per]


def chip_kernel(key_dim, chips, slots, place, *refs):
    in_refs, out_refs = refs[: -len(slots)], refs[-len(slots) :]
    core, chip = place[0], place[1]
    per = out_refs[0].shape[0]
    for slot, out in zip(slots, out_refs):
        for j in range(per):
            if len(in_refs) == 4:
                at = owner_of(slot, core, chip, chips) * per + j
                tail = in_refs[1].shape[0]
                at_tail = jnp.clip(at - per, 0, tail - 1)
                own, got = (
                    jnp.where(at < per, head[0], rest[at_tail])
                    for head, rest in (in_refs[:2], in_refs[2:])
                )
            else:
                at = (slot - slots[0]) * per + j
                own, got = in_refs[0][at], in_refs[1][at]
            earlier = jnp.where(core == 0, own, got)
            later = jnp.where(core == 0, got, own)
            out[j] = compose(later, earlier, key_dim)


def in_order(chip, maps):
    maps = list(maps)
    bit = 1
    while bit < len(maps):
        swapped = jnp.bitwise_and(chip, bit) != 0
        maps = [jnp.where(swapped, maps[i ^ bit], maps[i]) for i in range(len(maps))]
        bit *= 2
    return maps


def total_kernel(key_dim, place, *refs):
    maps, total = refs[:-1], refs[-1]
    chip = place[1]
    for j in range(total.shape[0]):
        level = by_distance(place[0], [ref[j] for ref in maps])
        bit = 1
        while len(level) > 1:
            swapped = jnp.bitwise_and(chip, bit) != 0
            level = [
                compose(
                    jnp.where(swapped, low, high), jnp.where(swapped, high, low), key_dim
                )
                for low, high in zip(level[::2], level[1::2])
            ]
            bit *= 2
        total[j] = level[0]


def prefix_kernel(key_dim, place, *refs):
    maps, prefix = refs[:-1], refs[-1]
    for j in range(prefix.shape[1]):
        ordered = in_order(place[1], by_distance(place[0], [ref[j] for ref in maps]))
        running = ordered[0]
        prefix[0, j] = running
        for index in range(1, len(ordered) - 1):
            running = compose(ordered[index], running, key_dim)
            prefix[index, j] = running


def is_upper(place, level):
    return jnp.bitwise_and(jnp.right_shift(place[2], level), 1) == 1


def group_total_kernel(key_dim, level, place, total_ref, got_ref, out_ref):
    upper = is_upper(place, level)
    for j in range(total_ref.shape[0]):
        mine, got = total_ref[j], got_ref[j]
        later = jnp.where(upper, mine, got)
        earlier = jnp.where(upper, got, mine)
        if out_ref.shape[2] == mine.shape[1]:
            out_ref[j] = compose(later, earlier, key_dim)
        else:
            out_ref[j] = mm3(later[:, :key_dim], earlier[:, key_dim:]) + later[:, key_dim:]


def before_kernel(key_dim, level, place, got_ref, prefix_ref, out_ref):
    upper = is_upper(place, level)
    count = out_ref.shape[0]

    @pl.when(upper)
    def _():
        for j in range(out_ref.shape[1]):
            for index in range(count):
                if prefix_ref.shape[0] == count:
                    out_ref[index, j] = compose(prefix_ref[index, j], got_ref[j], key_dim)
                elif index == 0:
                    out_ref[index, j] = got_ref[j]
                else:
                    out_ref[index, j] = compose(prefix_ref[index - 1, j], got_ref[j], key_dim)

    @pl.when(jnp.logical_not(upper))
    def _():
        for j in range(out_ref.shape[1]):
            for index in range(count):
                if prefix_ref.shape[0] == count:
                    out_ref[index, j] = prefix_ref[index, j]
                elif index == 0:
                    out_ref[index, j] = jnp.where(
                        lax.broadcasted_iota(jnp.int32, out_ref.shape[2:], 0)
                        == lax.broadcasted_iota(jnp.int32, out_ref.shape[2:], 1),
                        1.0,
                        0.0,
                    )
                else:
                    out_ref[index, j] = prefix_ref[index - 1, j]


def enter_kernel(key_dim, level, place, got_ref, prefix_ref, *out_refs):
    core, chip, chips = place[0], place[1], len(out_refs)
    upper = is_upper(place, level)
    for j in range(got_ref.shape[0]):
        eh, el = split2(jnp.where(upper, got_ref[j], 0.0))
        twice = jnp.concatenate([eh, eh], axis=0)
        for slot, out in enumerate(out_refs):
            one = prefix_ref[owner_of(slot, core, chip, chips), j]
            th, tl = split2(one[:, :key_dim])
            moved = mm(jnp.concatenate([th, tl], axis=1), twice) + mm(th, el)
            out[j] = moved + one[:, key_dim:]


def each_slot(place, slots, chips, half, per, use):
    core, chip = place[0], place[1]
    for n, slot in enumerate(slots):
        for own in (True, False):
            side = core if own else 1 - core
            owner = owner_of(slot, side, chip, chips)

            def run(n=n, slot=slot, own=own, side=side, owner=owner):
                for j in range(per):
                    local = owner * per + j
                    position = local if half % chips else slot * per + j
                    use(n, j, own, position + (half if own else 0), side * half + local)

            if half % chips:
                pl.when(owner < half // per)(run)
            else:
                run()


def early_kernel(per, slots, chips, place, f_ref, *refs):
    parts, out_ref = refs[:-1], refs[-1]

    def use(n, j, own, position, head):
        part = parts[n if own else len(slots) + n]
        out_ref[n, 0 if own else 1, j] = read_out(f_ref[position], part[j])

    each_slot(place, slots, chips, f_ref.shape[0] // 2, per, use)


def output_kernel(per, early, late, chips, place, f_ref, early_ref, *refs):
    o_ref, os0, os1 = refs[-3:]
    parts = refs[:-3]
    heads, tok, wide = f_ref.shape
    mid = o_ref.shape[2] // 2

    def put(head, out):
        os0[pl.ds(head, tok, stride=heads), :] = out[:, :mid]
        os1[pl.ds(head, tok, stride=heads), :] = out[:, mid:]

    def use_early(n, j, own, position, head):
        put(head, early_ref[n, 0 if own else 1, j])

    def use_late(n, j, own, position, head):
        put(head, read_out(f_ref[position], parts[n if own else len(late) + n][j]))

    each_slot(place, early, chips, heads // 2, per, use_early)
    each_slot(place, late, chips, heads // 2, per, use_late)
    o_ref[:, :, :mid] = os0[...].reshape(tok, heads, mid).astype(BF16)
    o_ref[:, :, mid:] = os1[...].reshape(tok, heads, mid).astype(BF16)


def body(queries, key_rows, value_rows, log_gate, beta_rate):
    tok, heads, key_dim = queries.shape
    value_dim = value_rows.shape[2]
    wide = key_dim + value_dim
    half = heads // 2
    seq, grp = lax.axis_size("seq"), lax.axis_size("grp")
    chips = seq // 2
    owners = min(chips, half)
    per = half // owners
    f32 = lambda *shape: jax.ShapeDtypeStruct(shape, F32)
    tall = lambda width: pltpu.VMEM((tok * heads, width), F32)
    unit = 2 * tok * key_dim * key_dim
    sibling = [(i, i ^ 1) for i in range(seq)]

    give_first, own_first, first_basis, k_heads, trail, rows, inverse, v_rest = pl.pallas_call(
        placed(functools.partial(basis_kernel, chips, per)),
        out_shape=(
            f32(per, key_dim, wide),
            f32(per, key_dim, wide),
            f32(2 * per, tok, wide),
            jax.ShapeDtypeStruct((heads, tok, key_dim), BF16),
            f32(heads - 2 * per, tok, key_dim),
            f32(4, heads, tok),
            f32(heads - 2 * per, tok, tok),
            jax.ShapeDtypeStruct((heads - 2 * per, tok, value_dim), BF16),
        ),
        in_specs=[pl.BlockSpec(memory_space=pltpu.HBM)] * 4,
        out_specs=tuple(vmem(8)),
        scratch_shapes=[
            pltpu.VMEM((tok, heads, key_dim), BF16),
            pltpu.VMEM((tok, heads, value_dim), BF16),
            pltpu.VMEM((heads, tok), F32),
            pltpu.VMEM((heads, tok), F32),
            tall(key_dim),
            tall(value_dim // 2),
            tall(value_dim // 2),
            pltpu.SemaphoreType.DMA((4,)),
        ],
        compiler_params=pltpu.CompilerParams(vmem_limit_bytes=VMEM_LIMIT),
        cost_estimate=pl.CostEstimate(
            flops=50 * heads * unit, bytes_accessed=0, transcendentals=0
        ),
    )(
        *(
            pltpu.with_memory_space_constraint(a, pltpu.HBM)
            for a in (key_rows, value_rows, log_gate, beta_rate)
        )
    )
    got_first = lax.ppermute(give_first, "seq", sibling)
    give_rest, own_rest, rest_basis = call(
        rest_kernel,
        (
            f32(half - per, key_dim, wide),
            f32(half - per, key_dim, wide),
            f32(heads - 2 * per, tok, wide),
        ),
        flops=200 * heads * unit,
    )(inverse, k_heads, v_rest, trail, rows)
    give_rest, got_first = lax.optimization_barrier((give_rest, got_first))
    got_rest = lax.ppermute(give_rest, "seq", sibling)

    def chip_maps(slots, *maps):
        return call(
            functools.partial(chip_kernel, key_dim, chips, slots),
            [f32(per, key_dim, wide)] * len(slots),
        )(*maps)

    slots = list(range(chips))
    if half % chips:
        made = chip_maps(slots, own_first, own_rest, got_first, got_rest)
    else:
        made = chip_maps(slots[:1], own_first, got_first)
        if chips > 1:
            made = made + chip_maps(slots[1:], own_rest, got_rest)
    distances = slot_list(chips)

    def across(parts, to_owner):
        moved = []
        for slot in slots[:-1]:
            swap = [(i, i ^ (2 * distances[i % 2][slot])) for i in range(seq)]
            pairs = [(a, b) for a, b in swap if (b if to_owner else a) // 2 < owners]
            moved.append(lax.ppermute(parts[slot], "seq", pairs))
        return moved + [parts[-1]]

    def folded_by(kernel, *arrays):
        return call(
            functools.partial(kernel, chips),
            f32(heads, tok, wide),
            [tall(key_dim)],
            flops=20 * heads * unit,
        )(*arrays, queries, k_heads, rows, first_basis, rest_basis)

    made = list(made)
    folded = folded_by(query_kernel)
    made[0], folded = lax.optimization_barrier((made[0], folded))
    owned = across(made, True)
    owned[0], folded = lax.optimization_barrier((owned[0], folded))
    folded = folded_by(query_late_kernel, folded)
    owned, folded = lax.optimization_barrier((owned, folded))
    total = call(functools.partial(total_kernel, key_dim), f32(per, key_dim, wide))(
        *owned
    )
    total, *owned = lax.optimization_barrier((total, *owned))
    prefix = call(
        functools.partial(prefix_kernel, key_dim), f32(chips - 1, per, key_dim, wide)
    )(*owned)
    level = 0
    while 2 << level <= grp:
        swap = [(i, i ^ (1 << level)) for i in range(grp)]
        if 2 << level == grp:
            if level == 0:
                total = total[:, :, key_dim:]
            got_state = lax.ppermute(total, "grp", swap)
            states = call(
                functools.partial(enter_kernel, key_dim, level),
                [f32(per, key_dim, value_dim)] * chips,
            )(got_state, prefix)
        else:
            got = lax.ppermute(total, "grp", swap)
            width = value_dim if 4 << level == grp else wide
            total = call(
                functools.partial(group_total_kernel, key_dim, level), f32(per, key_dim, width)
            )(total, got)
            prefix = call(
                functools.partial(before_kernel, key_dim, level),
                f32(chips, per, key_dim, wide),
            )(got, prefix)
        level += 1
    arrived = across(states, False)
    kept, others = [], []
    for slot, part in enumerate(arrived):
        keep, give = call(
            functools.partial(pair_kernel, chips, slot),
            [f32(per, key_dim, value_dim)] * 2,
        )(own_first, own_rest, got_first, got_rest, part)
        kept.append(keep)
        others.append(lax.ppermute(give, "seq", sibling))
    early = (slots[-1:] + slots[:-1])[: max(chips // 2, 1)]
    late = [slot for slot in slots if slot not in early]
    early_outs = call(
        functools.partial(early_kernel, per, early, chips),
        f32(len(early), 2, per, tok, value_dim),
        flops=6 * len(early) * per * unit,
    )(folded, *(kept[n] for n in early), *(others[n] for n in early))
    return call(
        functools.partial(output_kernel, per, early, late, chips),
        jax.ShapeDtypeStruct((tok, heads, value_dim), BF16),
        [tall(value_dim // 2), tall(value_dim // 2)],
    )(folded, early_outs, *(kept[n] for n in late), *(others[n] for n in late))


def solution(mesh):
    return jax.shard_map(
        body,
        mesh=mesh,
        in_specs=(
            P(("grp", "seq"), None, None),
            P(("grp", "seq"), None, None),
            P(("grp", "seq"), None, None),
            P(None, ("grp", "seq")),
            P(None, ("grp", "seq")),
        ),
        out_specs=P(("grp", "seq"), None, None),
        check_vma=False,
    )
```

```python
import functools

import jax
import jax.numpy as jnp
from jax import lax
from jax.experimental import pallas as pl
from jax.experimental.pallas import tpu as pltpu
from jax.sharding import PartitionSpec as P

F32 = jnp.float32
BF16 = jnp.bfloat16
VMEM_LIMIT = 48 * 1024 * 1024


def split2(a):
    high = a.astype(BF16)
    low = (a - high.astype(F32)).astype(BF16)
    return high, low


def mm(a, b):
    return jnp.dot(a, b, preferred_element_type=F32)


def mm_nt(a, b):
    return lax.dot_general(a, b, (((1,), (1,)), ((), ())), preferred_element_type=F32)


def mm_tn(a, b):
    return lax.dot_general(a, b, (((0,), (0,)), ((), ())), preferred_element_type=F32)


def mm_exact_right(a, b):
    high, low = split2(a)
    return mm(jnp.concatenate([high, low], axis=1), jnp.concatenate([b, b], axis=0))


def mm3(a, b):
    ah, al = split2(a)
    bh, bl = split2(b)
    return mm(jnp.concatenate([ah, al], axis=1), jnp.concatenate([bh, bh], axis=0)) + mm(ah, bl)


def compose(later, earlier, key_dim):
    moved = mm3(later[:, :key_dim], earlier)
    return jnp.concatenate(
        [moved[:, :key_dim], moved[:, key_dim:] + later[:, key_dim:]], axis=1
    )


def turned(distance, chips):
    bits = chips.bit_length() - 1
    low = bits // 2
    return (distance >> low) | ((distance & ((1 << low) - 1)) << (bits - low))


def slot_list(chips):
    plain = [chips - 1] + list(range(1, chips - 1)) + [0] if chips > 1 else [0]
    return plain, plain


def owner_of(slot, core, chip, chips):
    plain, other = slot_list(chips)
    if plain[slot] == other[slot]:
        return jnp.bitwise_xor(chip, plain[slot])
    return jnp.bitwise_xor(chip, jnp.where(core == 0, plain[slot], other[slot]))


def by_distance(core, maps):
    plain, other = slot_list(len(maps))
    ordered = []
    for d in range(len(maps)):
        a, b = maps[plain.index(d)], maps[other.index(d)]
        ordered.append(a if plain.index(d) == other.index(d) else jnp.where(core == 0, a, b))
    return ordered


def local_heads(core, chip, chips, half):
    if half % chips:
        return list(range(half))
    per = half // chips
    return [owner_of(n // per, core, chip, chips) * per + n % per for n in range(half)]


def positions(heads, per):
    half = heads // 2
    first = [*range(per), *range(half, half + per)]
    return first, [n for n in range(heads) if n not in first]


def vmem(count):
    return [pl.BlockSpec(memory_space=pltpu.VMEM)] * count


def placed(kernel):
    def run(*refs):
        seq = lax.axis_index("seq")
        kernel((lax.rem(seq, 2), lax.div(seq, 2), lax.axis_index("grp")), *refs)

    return run


def call(kernel, out_shape, scratch=(), flops=0, nbytes=0):
    def run(*arrays):
        return pl.pallas_call(
            placed(kernel),
            out_shape=out_shape,
            in_specs=vmem(len(arrays)),
            out_specs=jax.tree.map(lambda _: pl.BlockSpec(memory_space=pltpu.VMEM), out_shape),
            scratch_shapes=list(scratch),
            compiler_params=pltpu.CompilerParams(vmem_limit_bytes=VMEM_LIMIT),
            cost_estimate=pl.CostEstimate(flops=flops, bytes_accessed=nbytes, transcendentals=0),
        )(*arrays)

    return run


def lane_cumsum(a):
    size = a.shape[1]
    lane = lax.broadcasted_iota(jnp.int32, a.shape, 1)
    step = 1
    while step < size:
        a = a + jnp.where(lane >= step, pltpu.roll(a, step, 1), 0.0)
        step *= 2
    return a


def head_rows(scratch, head, heads):
    count = scratch.shape[0] // heads
    return scratch[pl.ds(head, count, stride=heads), :]


def stage_rows(ref, scratch):
    wide = ref[...].astype(F32)
    scratch[...] = wide.reshape(scratch.shape)


def mm3_packed(lhs, rhs):
    rows = lhs.shape[0]
    width = rhs.shape[1] // 2
    high, low = split2(lhs)
    out = mm(jnp.concatenate([high, low], axis=0), rhs)
    return out[:rows, :width] + (out[:rows, width:] + out[rows:, :width])


def block_inverse(strict):
    size = strict[0].shape[0]
    base = min(16, size)
    rows = lax.broadcasted_iota(jnp.int32, (size, size), 0)
    cols = lax.broadcasted_iota(jnp.int32, (size, size), 1)

    def ones_where(mask):
        return jnp.where(mask, 1.0, 0.0).astype(BF16)

    def spread(compact, mask):
        count = size // compact.shape[0]
        return jnp.concatenate(
            [jnp.concatenate([part] * count, axis=0) * mask for part in split2(compact)], axis=1
        )

    lane = lax.broadcasted_iota(jnp.int32, (base, size), 1)
    line = lax.broadcasted_iota(jnp.int32, (base, size), 0)
    power, inverse = [], []
    for a in strict:
        compact = jnp.zeros((base, size), F32)
        for n in range(size // base):
            compact = jnp.where(lane // base == n, -a[n * base : (n + 1) * base, :], compact)
        power.append(compact)
        inverse.append(jnp.where(lane % base == line, 1.0, compact))
    mask = ones_where(rows // base == cols // base)
    wide = [spread(p, mask) for p in power]
    power = [mm3_packed(p, w) for p, w in zip(power, wide)]
    span = 2
    while span < base:
        wide = [spread(p, mask) for p in power]
        if span * 2 < base:
            both = [
                mm3_packed(jnp.concatenate([p, x], axis=0), w)
                for p, x, w in zip(power, inverse, wide)
            ]
            power = [a[:base] for a in both]
            inverse = [x + a[base:] for x, a in zip(inverse, both)]
        else:
            inverse = [x + mm3_packed(x, w) for x, w in zip(inverse, wide)]
        span *= 2
    parts = [split2(a) for a in strict]
    span = base
    while span < size:
        joint = ones_where(
            (rows // (2 * span) == cols // (2 * span)) & (rows // span != cols // span)
        )
        mask = ones_where(rows // span == cols // span)
        even = (
            (lax.broadcasted_iota(jnp.int32, (span, size), 1) // span) % 2
        ) == 0
        off = [jnp.concatenate([h * joint, l * joint], axis=1) for h, l in parts]
        first = [mm3_packed(x, o) for x, o in zip(inverse, off)]
        second = [mm3_packed(f, spread(x, mask)) for f, x in zip(first, inverse)]
        inverse = [
            jnp.concatenate([jnp.where(even, x, 0.0), jnp.where(even, -y, x)], axis=0)
            for x, y in zip(inverse, second)
        ]
        span *= 2
    return inverse


def updates_basis(inverse, k_raw, v_raw, beta, key_scale):
    key_part = mm_exact_right(inverse * key_scale, k_raw)
    value_part = mm_exact_right(inverse * beta, v_raw)
    return jnp.concatenate([key_part, value_part], axis=1)


def trailing_map(basis, trail, k_raw, last, eye_key, key_dim):
    bh, bl = split2(basis * trail)
    moved = mm_tn(
        jnp.concatenate([k_raw, k_raw], axis=0), jnp.concatenate([bh, bl], axis=0)
    )
    return jnp.concatenate(
        [moved[:, :key_dim] + jnp.where(eye_key, last, 0.0), moved[:, key_dim:]], axis=1
    )


def eye_mask(size):
    return lax.broadcasted_iota(jnp.int32, (size, size), 0) == lax.broadcasted_iota(
        jnp.int32, (size, size), 1
    )


def basis_kernel(
    chips, per, place, k_hbm, v_hbm, g_hbm, b_hbm,
    give_ref, own_ref, r_ref, kh_ref, trail_ref, rows_ref, inverse_ref, v_rest_ref,
    k_ref, v_ref, g_ref, b_ref, ks, vs0, vs1, sems,
):
    copies = [
        pltpu.make_async_copy(src, dst, sems.at[n])
        for n, (src, dst) in enumerate(
            ((k_hbm, k_ref), (g_hbm, g_ref), (b_hbm, b_ref), (v_hbm, v_ref))
        )
    ]
    for copy in copies:
        copy.start()
    tok, heads, key_dim = k_ref.shape
    value_dim = v_ref.shape[2]
    half = heads // 2
    core, chip = place[0], place[1]
    order = [(1 - core) * half + h for h in local_heads(1 - core, chip, chips, half)]
    order += [core * half + h for h in local_heads(core, chip, chips, half)]
    copies[1].wait()
    copies[2].wait()

    def picked(ref):
        return jnp.concatenate([ref[pl.ds(h, 1), :] for h in order], axis=0)

    cum_row = lane_cumsum(picked(g_ref))
    beta_row = picked(b_ref)
    last_row = cum_row[:, tok - 1 :]
    decay_row = jnp.exp(cum_row)
    cum_col = cum_row.T
    beta_col = beta_row.T
    trail_col = jnp.exp(last_row - cum_row).T
    rows = lax.broadcasted_iota(jnp.int32, (tok, tok), 0)
    cols = lax.broadcasted_iota(jnp.int32, (tok, tok), 1)
    lower = rows > cols
    eye = rows == cols
    eye_key = eye_mask(key_dim)
    every = range(heads)
    copies[0].wait()
    stage_rows(k_ref, ks)
    k_wide = [head_rows(ks, h, heads) for h in order]
    k_raw = [a.astype(BF16) for a in k_wide]
    for i in every:
        kh_ref[i] = k_raw[i]
    gram = [mm_nt(a, a) for a in k_raw]
    inv_col = [lax.rsqrt(jnp.sum(a * a, axis=1, keepdims=True) + 1e-6) for a in k_wide]
    inv_row = [
        lax.rsqrt(jnp.sum(jnp.where(eye, a, 0.0), axis=0, keepdims=True) + 1e-6) for a in gram
    ]
    strict = []
    for i in every:
        gap = cum_col[:, i : i + 1] - cum_row[i : i + 1, :]
        decay = jnp.exp(jnp.where(lower, gap, 0.0))
        left = beta_col[:, i : i + 1] * inv_col[i]
        strict.append(jnp.where(lower, gram[i] * decay * left * inv_row[i], 0.0))
    copies[3].wait()
    wide = v_ref[...].astype(F32)
    vs0[...] = wide[:, :, : value_dim // 2].reshape(vs0.shape)
    vs1[...] = wide[:, :, value_dim // 2 :].reshape(vs1.shape)
    v_raw = [
        jnp.concatenate(
            [head_rows(vs0, h, heads), head_rows(vs1, h, heads)], axis=1
        ).astype(BF16)
        for h in order
    ]
    first, rest = positions(heads, per)
    for n, i in enumerate(rest):
        v_rest_ref[n] = v_raw[i]
    inverse = block_inverse(strict)
    rows_ref[0] = jnp.concatenate(inv_row, axis=0)
    rows_ref[1] = cum_row
    rows_ref[2] = beta_row
    rows_ref[3] = -(decay_row * beta_row * jnp.concatenate(inv_row, axis=0))
    for n, i in enumerate(first):
        trail = trail_col[:, i : i + 1] * inv_col[i]
        beta_i = beta_row[i : i + 1, :]
        key_scale = -(decay_row[i : i + 1, :] * beta_i * inv_row[i])
        basis = updates_basis(inverse[i], k_raw[i], v_raw[i], beta_i, key_scale)
        r_ref[n] = basis
        made = trailing_map(
            basis, trail, k_raw[i], jnp.exp(last_row[i : i + 1, :]), eye_key, key_dim
        )
        if n < per:
            give_ref[n] = made
        else:
            own_ref[n - per] = made
    for n, i in enumerate(rest):
        trail_ref[n] = jnp.broadcast_to(trail_col[:, i : i + 1] * inv_col[i], (tok, key_dim))
        inverse_ref[n] = inverse[i]


def rest_kernel(place, inverse_ref, kh_ref, v_ref, trail_ref, rows_ref, give_ref, own_ref, r_ref):
    rest, tok, wide = r_ref.shape
    key_dim = wide - v_ref.shape[2]
    heads = kh_ref.shape[0]
    eye_key = eye_mask(key_dim)
    where = positions(heads, (heads - rest) // 2)[1]
    k_raw = [kh_ref[i] for i in where]
    trail = [trail_ref[n][:, :1] for n in range(rest)]
    last = [jnp.exp(rows_ref[1, i : i + 1, tok - 1 :]) for i in where]
    bases = [
        updates_basis(
            inverse_ref[n], k_raw[n], v_ref[n], rows_ref[2, i : i + 1, :], rows_ref[3, i : i + 1, :]
        )
        for n, i in enumerate(where)
    ]
    made = [
        trailing_map(b, t, k, e, eye_key, key_dim)
        for b, t, k, e in zip(bases, trail, k_raw, last)
    ]
    for n in range(rest):
        r_ref[n] = bases[n]
        if n < rest // 2:
            give_ref[n] = made[n]
        else:
            own_ref[n - rest // 2] = made[n]


def query_rows(chips, place, q_ref, kh_ref, rows_ref, r_first, r_rest, f_ref, qs):
    heads, tok, key_dim = kh_ref.shape
    half = heads // 2
    first, rest = positions(heads, r_first.shape[0] // 2)
    core, chip = place[0], place[1]
    order = [(1 - core) * half + h for h in local_heads(1 - core, chip, chips, half)]
    order += [core * half + h for h in local_heads(core, chip, chips, half)]
    stage_rows(q_ref, qs)
    cum_row = rows_ref[1]
    cum_col = cum_row.T
    rows = lax.broadcasted_iota(jnp.int32, (tok, tok), 0)
    cols = lax.broadcasted_iota(jnp.int32, (tok, tok), 1)
    lower = rows >= cols
    for i in range(heads):
        q_wide = head_rows(qs, order[i], heads)
        q_inv = lax.rsqrt(jnp.sum(q_wide * q_wide, axis=1, keepdims=True) + 1e-6)
        dots = mm_nt(q_wide.astype(BF16), kh_ref[i])
        gap = cum_col[:, i : i + 1] - cum_row[i : i + 1, :]
        decay = jnp.exp(jnp.where(lower, gap, 0.0))
        scores = jnp.where(lower, dots * decay * q_inv * rows_ref[0, i : i + 1, :], 0.0)
        folded = mm3(scores, r_first[first.index(i)] if i in first else r_rest[rest.index(i)])
        gated = q_wide * (q_inv * jnp.exp(cum_col[:, i : i + 1]))
        f_ref[i] = jnp.concatenate(
            [folded[:, :key_dim] + gated, folded[:, key_dim:]], axis=1
        )


def query_kernel(chips, place, *refs):
    @pl.when(place[0] == 0)
    def _():
        query_rows(chips, place, *refs)


def query_late_kernel(chips, place, done_ref, *refs):
    f_ref = refs[-2]

    @pl.when(place[0] == 0)
    def _():
        f_ref[...] = done_ref[...]

    @pl.when(place[0] != 0)
    def _():
        query_rows(chips, place, *refs)


def read_out(folded, state):
    key_dim = state.shape[0]
    return mm3(folded[:, :key_dim], state) + folded[:, key_dim:]


def pair_kernel(chips, slot, place, *refs):
    map_refs, (state_ref, keep_ref, give_ref) = refs[:-3], refs[-3:]
    core, chip = place[0], place[1]
    per = state_ref.shape[0]
    for j in range(per):
        own, got = picked_maps(map_refs, slot, j, per, chips, core, chip)
        state = state_ref[j]
        second = read_out(jnp.where(core == 0, own, got), state)
        keep_ref[j] = jnp.where(core == 0, state, second)
        give_ref[j] = jnp.where(core == 0, second, state)


def picked_maps(refs, slot, j, per, chips, core, chip):
    own_first, own_rest, got_first, got_rest = refs
    half = per + own_rest.shape[0]
    if half % chips:
        at = owner_of(slot, core, chip, chips) * per + j
        at_tail = jnp.clip(at - per, 0, half - per - 1)
        return tuple(
            jnp.where(at < per, first[0], rest[at_tail])
            for first, rest in ((own_first, own_rest), (got_first, got_rest))
        )
    at = slot * per + j
    if at < per:
        return own_first[at], got_first[at]
    return own_rest[at - per], got_rest[at - per]


def chip_kernel(key_dim, chips, slots, place, *refs):
    in_refs, out_refs = refs[: -len(slots)], refs[-len(slots) :]
    core, chip = place[0], place[1]
    per = out_refs[0].shape[0]
    for slot, out in zip(slots, out_refs):
        for j in range(per):
            if len(in_refs) == 4:
                at = owner_of(slot, core, chip, chips) * per + j
                tail = in_refs[1].shape[0]
                at_tail = jnp.clip(at - per, 0, tail - 1)
                own, got = (
                    jnp.where(at < per, head[0], rest[at_tail])
                    for head, rest in (in_refs[:2], in_refs[2:])
                )
            else:
                at = (slot - slots[0]) * per + j
                own, got = in_refs[0][at], in_refs[1][at]
            earlier = jnp.where(core == 0, own, got)
            later = jnp.where(core == 0, got, own)
            out[j] = compose(later, earlier, key_dim)


def in_order(chip, maps):
    maps = list(maps)
    bit = 1
    while bit < len(maps):
        swapped = jnp.bitwise_and(chip, bit) != 0
        maps = [jnp.where(swapped, maps[i ^ bit], maps[i]) for i in range(len(maps))]
        bit *= 2
    return maps


def total_kernel(key_dim, place, *refs):
    maps, total = refs[:-1], refs[-1]
    chip = place[1]
    for j in range(total.shape[0]):
        level = by_distance(place[0], [ref[j] for ref in maps])
        bit = 1
        while len(level) > 1:
            swapped = jnp.bitwise_and(chip, bit) != 0
            level = [
                compose(
                    jnp.where(swapped, low, high), jnp.where(swapped, high, low), key_dim
                )
                for low, high in zip(level[::2], level[1::2])
            ]
            bit *= 2
        total[j] = level[0]


def prefix_kernel(key_dim, place, *refs):
    maps, prefix = refs[:-1], refs[-1]
    for j in range(prefix.shape[1]):
        ordered = in_order(place[1], by_distance(place[0], [ref[j] for ref in maps]))
        running = ordered[0]
        prefix[0, j] = running
        for index in range(1, len(ordered) - 1):
            running = compose(ordered[index], running, key_dim)
            prefix[index, j] = running


def is_upper(place, level):
    return jnp.bitwise_and(jnp.right_shift(place[2], level), 1) == 1


def group_total_kernel(key_dim, level, place, total_ref, got_ref, out_ref):
    upper = is_upper(place, level)
    for j in range(total_ref.shape[0]):
        mine, got = total_ref[j], got_ref[j]
        later = jnp.where(upper, mine, got)
        earlier = jnp.where(upper, got, mine)
        if out_ref.shape[2] == mine.shape[1]:
            out_ref[j] = compose(later, earlier, key_dim)
        else:
            out_ref[j] = mm3(later[:, :key_dim], earlier[:, key_dim:]) + later[:, key_dim:]


def before_kernel(key_dim, level, place, got_ref, prefix_ref, out_ref):
    upper = is_upper(place, level)
    count = out_ref.shape[0]

    @pl.when(upper)
    def _():
        for j in range(out_ref.shape[1]):
            for index in range(count):
                if prefix_ref.shape[0] == count:
                    out_ref[index, j] = compose(prefix_ref[index, j], got_ref[j], key_dim)
                elif index == 0:
                    out_ref[index, j] = got_ref[j]
                else:
                    out_ref[index, j] = compose(prefix_ref[index - 1, j], got_ref[j], key_dim)

    @pl.when(jnp.logical_not(upper))
    def _():
        for j in range(out_ref.shape[1]):
            for index in range(count):
                if prefix_ref.shape[0] == count:
                    out_ref[index, j] = prefix_ref[index, j]
                elif index == 0:
                    out_ref[index, j] = jnp.where(
                        lax.broadcasted_iota(jnp.int32, out_ref.shape[2:], 0)
                        == lax.broadcasted_iota(jnp.int32, out_ref.shape[2:], 1),
                        1.0,
                        0.0,
                    )
                else:
                    out_ref[index, j] = prefix_ref[index - 1, j]


def enter_kernel(key_dim, level, place, got_ref, prefix_ref, *out_refs):
    core, chip, chips = place[0], place[1], len(out_refs)
    upper = is_upper(place, level)
    for j in range(got_ref.shape[0]):
        eh, el = split2(jnp.where(upper, got_ref[j], 0.0))
        twice = jnp.concatenate([eh, eh], axis=0)
        for slot, out in enumerate(out_refs):
            one = prefix_ref[owner_of(slot, core, chip, chips), j]
            th, tl = split2(one[:, :key_dim])
            moved = mm(jnp.concatenate([th, tl], axis=1), twice) + mm(th, el)
            out[j] = moved + one[:, key_dim:]


def each_slot(place, slots, chips, half, per, use):
    core, chip = place[0], place[1]
    for n, slot in enumerate(slots):
        for own in (True, False):
            side = core if own else 1 - core
            owner = owner_of(slot, side, chip, chips)

            def run(n=n, slot=slot, own=own, side=side, owner=owner):
                for j in range(per):
                    local = owner * per + j
                    position = local if half % chips else slot * per + j
                    use(n, j, own, position + (half if own else 0), side * half + local)

            if half % chips:
                pl.when(owner < half // per)(run)
            else:
                run()


def early_kernel(per, slots, chips, place, f_ref, *refs):
    parts, out_ref = refs[:-1], refs[-1]

    def use(n, j, own, position, head):
        part = parts[n if own else len(slots) + n]
        out_ref[n, 0 if own else 1, j] = read_out(f_ref[position], part[j])

    each_slot(place, slots, chips, f_ref.shape[0] // 2, per, use)


def output_kernel(per, early, late, chips, place, f_ref, early_ref, *refs):
    o_ref, os0, os1 = refs[-3:]
    parts = refs[:-3]
    heads, tok, wide = f_ref.shape
    mid = o_ref.shape[2] // 2

    def put(head, out):
        os0[pl.ds(head, tok, stride=heads), :] = out[:, :mid]
        os1[pl.ds(head, tok, stride=heads), :] = out[:, mid:]

    def use_early(n, j, own, position, head):
        put(head, early_ref[n, 0 if own else 1, j])

    def use_late(n, j, own, position, head):
        put(head, read_out(f_ref[position], parts[n if own else len(late) + n][j]))

    each_slot(place, early, chips, heads // 2, per, use_early)
    each_slot(place, late, chips, heads // 2, per, use_late)
    o_ref[:, :, :mid] = os0[...].reshape(tok, heads, mid).astype(BF16)
    o_ref[:, :, mid:] = os1[...].reshape(tok, heads, mid).astype(BF16)


def body(queries, key_rows, value_rows, log_gate, beta_rate):
    tok, heads, key_dim = queries.shape
    value_dim = value_rows.shape[2]
    wide = key_dim + value_dim
    half = heads // 2
    seq, grp = lax.axis_size("seq"), lax.axis_size("grp")
    chips = seq // 2
    owners = min(chips, half)
    per = half // owners
    f32 = lambda *shape: jax.ShapeDtypeStruct(shape, F32)
    tall = lambda width: pltpu.VMEM((tok * heads, width), F32)
    unit = 2 * tok * key_dim * key_dim
    sibling = [(i, i ^ 1) for i in range(seq)]

    give_first, own_first, first_basis, k_heads, trail, rows, inverse, v_rest = pl.pallas_call(
        placed(functools.partial(basis_kernel, chips, per)),
        out_shape=(
            f32(per, key_dim, wide),
            f32(per, key_dim, wide),
            f32(2 * per, tok, wide),
            jax.ShapeDtypeStruct((heads, tok, key_dim), BF16),
            f32(heads - 2 * per, tok, key_dim),
            f32(4, heads, tok),
            f32(heads - 2 * per, tok, tok),
            jax.ShapeDtypeStruct((heads - 2 * per, tok, value_dim), BF16),
        ),
        in_specs=[pl.BlockSpec(memory_space=pltpu.HBM)] * 4,
        out_specs=tuple(vmem(8)),
        scratch_shapes=[
            pltpu.VMEM((tok, heads, key_dim), BF16),
            pltpu.VMEM((tok, heads, value_dim), BF16),
            pltpu.VMEM((heads, tok), F32),
            pltpu.VMEM((heads, tok), F32),
            tall(key_dim),
            tall(value_dim // 2),
            tall(value_dim // 2),
            pltpu.SemaphoreType.DMA((4,)),
        ],
        compiler_params=pltpu.CompilerParams(vmem_limit_bytes=VMEM_LIMIT),
        cost_estimate=pl.CostEstimate(
            flops=50 * heads * unit, bytes_accessed=0, transcendentals=0
        ),
    )(
        *(
            pltpu.with_memory_space_constraint(a, pltpu.HBM)
            for a in (key_rows, value_rows, log_gate, beta_rate)
        )
    )
    got_first = lax.ppermute(give_first, "seq", sibling)
    give_rest, own_rest, rest_basis = call(
        rest_kernel,
        (
            f32(half - per, key_dim, wide),
            f32(half - per, key_dim, wide),
            f32(heads - 2 * per, tok, wide),
        ),
        flops=200 * heads * unit,
    )(inverse, k_heads, v_rest, trail, rows)
    give_rest, got_first = lax.optimization_barrier((give_rest, got_first))
    got_rest = lax.ppermute(give_rest, "seq", sibling)

    def chip_maps(slots, *maps):
        return call(
            functools.partial(chip_kernel, key_dim, chips, slots),
            [f32(per, key_dim, wide)] * len(slots),
        )(*maps)

    slots = list(range(chips))
    if half % chips:
        made = chip_maps(slots, own_first, own_rest, got_first, got_rest)
    else:
        made = chip_maps(slots[:1], own_first, got_first)
        if chips > 1:
            made = made + chip_maps(slots[1:], own_rest, got_rest)
    distances = slot_list(chips)

    def across(parts, to_owner):
        moved = []
        for slot in slots[:-1]:
            swap = [(i, i ^ (2 * distances[i % 2][slot])) for i in range(seq)]
            pairs = [(a, b) for a, b in swap if (b if to_owner else a) // 2 < owners]
            moved.append(lax.ppermute(parts[slot], "seq", pairs))
        return moved + [parts[-1]]

    def folded_by(kernel, *arrays):
        return call(
            functools.partial(kernel, chips),
            f32(heads, tok, wide),
            [tall(key_dim)],
            flops=20 * heads * unit,
        )(*arrays, queries, k_heads, rows, first_basis, rest_basis)

    made = list(made)
    folded = folded_by(query_kernel)
    made[0], folded = lax.optimization_barrier((made[0], folded))
    owned = across(made, True)
    owned[0], folded = lax.optimization_barrier((owned[0], folded))
    folded = folded_by(query_late_kernel, folded)
    owned, folded = lax.optimization_barrier((owned, folded))
    total = call(functools.partial(total_kernel, key_dim), f32(per, key_dim, wide))(
        *owned
    )
    total, *owned = lax.optimization_barrier((total, *owned))
    prefix = call(
        functools.partial(prefix_kernel, key_dim), f32(chips - 1, per, key_dim, wide)
    )(*owned)
    level = 0
    while 2 << level <= grp:
        swap = [(i, i ^ (1 << level)) for i in range(grp)]
        if 2 << level == grp:
            if level == 0:
                total = total[:, :, key_dim:]
            got_state = lax.ppermute(total, "grp", swap)
            states = call(
                functools.partial(enter_kernel, key_dim, level),
                [f32(per, key_dim, value_dim)] * chips,
            )(got_state, prefix)
        else:
            got = lax.ppermute(total, "grp", swap)
            width = value_dim if 4 << level == grp else wide
            total = call(
                functools.partial(group_total_kernel, key_dim, level), f32(per, key_dim, width)
            )(total, got)
            prefix = call(
                functools.partial(before_kernel, key_dim, level),
                f32(chips, per, key_dim, wide),
            )(got, prefix)
        level += 1
    arrived = across(states, False)
    arrived[0], arrived[-1] = lax.optimization_barrier((arrived[0], arrived[-1]))
    kept, others = [], []
    for slot, part in enumerate(arrived):
        keep, give = call(
            functools.partial(pair_kernel, chips, slot),
            [f32(per, key_dim, value_dim)] * 2,
        )(own_first, own_rest, got_first, got_rest, part)
        kept.append(keep)
        others.append(lax.ppermute(give, "seq", sibling))
    early = (slots[-1:] + slots[:-1])[: max(chips // 2, 1)]
    late = [slot for slot in slots if slot not in early]
    early_outs = call(
        functools.partial(early_kernel, per, early, chips),
        f32(len(early), 2, per, tok, value_dim),
        flops=6 * len(early) * per * unit,
    )(folded, *(kept[n] for n in early), *(others[n] for n in early))
    return call(
        functools.partial(output_kernel, per, early, late, chips),
        jax.ShapeDtypeStruct((tok, heads, value_dim), BF16),
        [tall(value_dim // 2), tall(value_dim // 2)],
    )(folded, early_outs, *(kept[n] for n in late), *(others[n] for n in late))


def solution(mesh):
    return jax.shard_map(
        body,
        mesh=mesh,
        in_specs=(
            P(("grp", "seq"), None, None),
            P(("grp", "seq"), None, None),
            P(("grp", "seq"), None, None),
            P(None, ("grp", "seq")),
            P(None, ("grp", "seq")),
        ),
        out_specs=P(("grp", "seq"), None, None),
        check_vma=False,
    )
```

```python
import functools

import jax
import jax.numpy as jnp
from jax import lax
from jax.experimental import pallas as pl
from jax.experimental.pallas import tpu as pltpu
from jax.sharding import PartitionSpec as P

F32 = jnp.float32
BF16 = jnp.bfloat16
VMEM_LIMIT = 48 * 1024 * 1024


def split2(a):
    high = a.astype(BF16)
    low = (a - high.astype(F32)).astype(BF16)
    return high, low


def mm(a, b):
    return jnp.dot(a, b, preferred_element_type=F32)


def mm_nt(a, b):
    return lax.dot_general(a, b, (((1,), (1,)), ((), ())), preferred_element_type=F32)


def mm_tn(a, b):
    return lax.dot_general(a, b, (((0,), (0,)), ((), ())), preferred_element_type=F32)


def mm_exact_right(a, b):
    high, low = split2(a)
    return mm(jnp.concatenate([high, low], axis=1), jnp.concatenate([b, b], axis=0))


def mm3(a, b):
    ah, al = split2(a)
    bh, bl = split2(b)
    return mm(jnp.concatenate([ah, al], axis=1), jnp.concatenate([bh, bh], axis=0)) + mm(ah, bl)


def compose(later, earlier, key_dim):
    moved = mm3(later[:, :key_dim], earlier)
    return jnp.concatenate(
        [moved[:, :key_dim], moved[:, key_dim:] + later[:, key_dim:]], axis=1
    )


def turned(distance, chips):
    bits = chips.bit_length() - 1
    low = bits // 2
    return (distance >> low) | ((distance & ((1 << low) - 1)) << (bits - low))


def slot_list(chips):
    plain = [chips - 1] + list(range(1, chips - 1)) + [0] if chips > 1 else [0]
    return plain, plain


def owner_of(slot, core, chip, chips):
    plain, other = slot_list(chips)
    if plain[slot] == other[slot]:
        return jnp.bitwise_xor(chip, plain[slot])
    return jnp.bitwise_xor(chip, jnp.where(core == 0, plain[slot], other[slot]))


def by_distance(core, maps):
    plain, other = slot_list(len(maps))
    ordered = []
    for d in range(len(maps)):
        a, b = maps[plain.index(d)], maps[other.index(d)]
        ordered.append(a if plain.index(d) == other.index(d) else jnp.where(core == 0, a, b))
    return ordered


def local_heads(core, chip, chips, half):
    if half % chips:
        return list(range(half))
    per = half // chips
    return [owner_of(n // per, core, chip, chips) * per + n % per for n in range(half)]


def positions(heads, per):
    half = heads // 2
    first = [*range(per), *range(half, half + per)]
    return first, [n for n in range(heads) if n not in first]


def vmem(count):
    return [pl.BlockSpec(memory_space=pltpu.VMEM)] * count


def placed(kernel):
    def run(*refs):
        seq = lax.axis_index("seq")
        kernel((lax.rem(seq, 2), lax.div(seq, 2), lax.axis_index("grp")), *refs)

    return run


def call(kernel, out_shape, scratch=(), flops=0, nbytes=0):
    def run(*arrays):
        return pl.pallas_call(
            placed(kernel),
            out_shape=out_shape,
            in_specs=vmem(len(arrays)),
            out_specs=jax.tree.map(lambda _: pl.BlockSpec(memory_space=pltpu.VMEM), out_shape),
            scratch_shapes=list(scratch),
            compiler_params=pltpu.CompilerParams(vmem_limit_bytes=VMEM_LIMIT),
            cost_estimate=pl.CostEstimate(flops=flops, bytes_accessed=nbytes, transcendentals=0),
        )(*arrays)

    return run


def lane_cumsum(a):
    size = a.shape[1]
    lane = lax.broadcasted_iota(jnp.int32, a.shape, 1)
    step = 1
    while step < size:
        a = a + jnp.where(lane >= step, pltpu.roll(a, step, 1), 0.0)
        step *= 2
    return a


def head_rows(scratch, head, heads):
    count = scratch.shape[0] // heads
    return scratch[pl.ds(head, count, stride=heads), :]


def stage_rows(ref, scratch):
    wide = ref[...].astype(F32)
    scratch[...] = wide.reshape(scratch.shape)


def mm3_packed(lhs, rhs):
    rows = lhs.shape[0]
    width = rhs.shape[1] // 2
    high, low = split2(lhs)
    out = mm(jnp.concatenate([high, low], axis=0), rhs)
    return out[:rows, :width] + (out[:rows, width:] + out[rows:, :width])


def block_inverse(strict):
    size = strict[0].shape[0]
    base = min(16, size)
    rows = lax.broadcasted_iota(jnp.int32, (size, size), 0)
    cols = lax.broadcasted_iota(jnp.int32, (size, size), 1)

    def ones_where(mask):
        return jnp.where(mask, 1.0, 0.0).astype(BF16)

    def spread(compact, mask):
        count = size // compact.shape[0]
        return jnp.concatenate(
            [jnp.concatenate([part] * count, axis=0) * mask for part in split2(compact)], axis=1
        )

    lane = lax.broadcasted_iota(jnp.int32, (base, size), 1)
    line = lax.broadcasted_iota(jnp.int32, (base, size), 0)
    power, inverse = [], []
    for a in strict:
        compact = jnp.zeros((base, size), F32)
        for n in range(size // base):
            compact = jnp.where(lane // base == n, -a[n * base : (n + 1) * base, :], compact)
        power.append(compact)
        inverse.append(jnp.where(lane % base == line, 1.0, compact))
    mask = ones_where(rows // base == cols // base)
    wide = [spread(p, mask) for p in power]
    power = [mm3_packed(p, w) for p, w in zip(power, wide)]
    span = 2
    while span < base:
        wide = [spread(p, mask) for p in power]
        if span * 2 < base:
            both = [
                mm3_packed(jnp.concatenate([p, x], axis=0), w)
                for p, x, w in zip(power, inverse, wide)
            ]
            power = [a[:base] for a in both]
            inverse = [x + a[base:] for x, a in zip(inverse, both)]
        else:
            inverse = [x + mm3_packed(x, w) for x, w in zip(inverse, wide)]
        span *= 2
    parts = [split2(a) for a in strict]
    span = base
    while span < size:
        joint = ones_where(
            (rows // (2 * span) == cols // (2 * span)) & (rows // span != cols // span)
        )
        mask = ones_where(rows // span == cols // span)
        even = (
            (lax.broadcasted_iota(jnp.int32, (span, size), 1) // span) % 2
        ) == 0
        off = [jnp.concatenate([h * joint, l * joint], axis=1) for h, l in parts]
        first = [mm3_packed(x, o) for x, o in zip(inverse, off)]
        second = [mm3_packed(f, spread(x, mask)) for f, x in zip(first, inverse)]
        inverse = [
            jnp.concatenate([jnp.where(even, x, 0.0), jnp.where(even, -y, x)], axis=0)
            for x, y in zip(inverse, second)
        ]
        span *= 2
    return inverse


def updates_basis(inverse, k_raw, v_raw, beta, key_scale):
    key_part = mm_exact_right(inverse * key_scale, k_raw)
    value_part = mm_exact_right(inverse * beta, v_raw)
    return jnp.concatenate([key_part, value_part], axis=1)


def trailing_map(basis, trail, k_raw, last, eye_key, key_dim):
    bh, bl = split2(basis * trail)
    moved = mm_tn(
        jnp.concatenate([k_raw, k_raw], axis=0), jnp.concatenate([bh, bl], axis=0)
    )
    return jnp.concatenate(
        [moved[:, :key_dim] + jnp.where(eye_key, last, 0.0), moved[:, key_dim:]], axis=1
    )


def eye_mask(size):
    return lax.broadcasted_iota(jnp.int32, (size, size), 0) == lax.broadcasted_iota(
        jnp.int32, (size, size), 1
    )


def basis_kernel(
    chips, per, place, k_hbm, v_hbm, g_hbm, b_hbm,
    give_ref, own_ref, r_ref, kh_ref, trail_ref, rows_ref, inverse_ref, v_rest_ref,
    k_ref, v_ref, g_ref, b_ref, ks, vs0, vs1, sems,
):
    copies = [
        pltpu.make_async_copy(src, dst, sems.at[n])
        for n, (src, dst) in enumerate(
            ((k_hbm, k_ref), (g_hbm, g_ref), (b_hbm, b_ref), (v_hbm, v_ref))
        )
    ]
    for copy in copies:
        copy.start()
    tok, heads, key_dim = k_ref.shape
    value_dim = v_ref.shape[2]
    half = heads // 2
    core, chip = place[0], place[1]
    order = [(1 - core) * half + h for h in local_heads(1 - core, chip, chips, half)]
    order += [core * half + h for h in local_heads(core, chip, chips, half)]
    copies[1].wait()
    copies[2].wait()

    def picked(ref):
        return jnp.concatenate([ref[pl.ds(h, 1), :] for h in order], axis=0)

    cum_row = lane_cumsum(picked(g_ref))
    beta_row = picked(b_ref)
    last_row = cum_row[:, tok - 1 :]
    decay_row = jnp.exp(cum_row)
    cum_col = cum_row.T
    beta_col = beta_row.T
    trail_col = jnp.exp(last_row - cum_row).T
    rows = lax.broadcasted_iota(jnp.int32, (tok, tok), 0)
    cols = lax.broadcasted_iota(jnp.int32, (tok, tok), 1)
    lower = rows > cols
    eye = rows == cols
    eye_key = eye_mask(key_dim)
    every = range(heads)
    copies[0].wait()
    stage_rows(k_ref, ks)
    k_wide = [head_rows(ks, h, heads) for h in order]
    k_raw = [a.astype(BF16) for a in k_wide]
    for i in every:
        kh_ref[i] = k_raw[i]
    gram = [mm_nt(a, a) for a in k_raw]
    inv_col = [lax.rsqrt(jnp.sum(a * a, axis=1, keepdims=True) + 1e-6) for a in k_wide]
    inv_row = [
        lax.rsqrt(jnp.sum(jnp.where(eye, a, 0.0), axis=0, keepdims=True) + 1e-6) for a in gram
    ]
    strict = []
    for i in every:
        gap = cum_col[:, i : i + 1] - cum_row[i : i + 1, :]
        decay = jnp.exp(jnp.where(lower, gap, 0.0))
        left = beta_col[:, i : i + 1] * inv_col[i]
        strict.append(jnp.where(lower, gram[i] * decay * left * inv_row[i], 0.0))
    copies[3].wait()
    wide = v_ref[...].astype(F32)
    vs0[...] = wide[:, :, : value_dim // 2].reshape(vs0.shape)
    vs1[...] = wide[:, :, value_dim // 2 :].reshape(vs1.shape)
    v_raw = [
        jnp.concatenate(
            [head_rows(vs0, h, heads), head_rows(vs1, h, heads)], axis=1
        ).astype(BF16)
        for h in order
    ]
    first, rest = positions(heads, per)
    for n, i in enumerate(rest):
        v_rest_ref[n] = v_raw[i]
    inverse = block_inverse(strict)
    rows_ref[0] = jnp.concatenate(inv_row, axis=0)
    rows_ref[1] = cum_row
    rows_ref[2] = beta_row
    rows_ref[3] = -(decay_row * beta_row * jnp.concatenate(inv_row, axis=0))
    for n, i in enumerate(first):
        trail = trail_col[:, i : i + 1] * inv_col[i]
        beta_i = beta_row[i : i + 1, :]
        key_scale = -(decay_row[i : i + 1, :] * beta_i * inv_row[i])
        basis = updates_basis(inverse[i], k_raw[i], v_raw[i], beta_i, key_scale)
        r_ref[n] = basis
        made = trailing_map(
            basis, trail, k_raw[i], jnp.exp(last_row[i : i + 1, :]), eye_key, key_dim
        )
        if n < per:
            give_ref[n] = made
        else:
            own_ref[n - per] = made
    for n, i in enumerate(rest):
        trail_ref[n] = jnp.broadcast_to(trail_col[:, i : i + 1] * inv_col[i], (tok, key_dim))
        inverse_ref[n] = inverse[i]


def rest_kernel(place, inverse_ref, kh_ref, v_ref, trail_ref, rows_ref, give_ref, own_ref, r_ref):
    rest, tok, wide = r_ref.shape
    key_dim = wide - v_ref.shape[2]
    heads = kh_ref.shape[0]
    eye_key = eye_mask(key_dim)
    where = positions(heads, (heads - rest) // 2)[1]
    k_raw = [kh_ref[i] for i in where]
    trail = [trail_ref[n][:, :1] for n in range(rest)]
    last = [jnp.exp(rows_ref[1, i : i + 1, tok - 1 :]) for i in where]
    bases = [
        updates_basis(
            inverse_ref[n], k_raw[n], v_ref[n], rows_ref[2, i : i + 1, :], rows_ref[3, i : i + 1, :]
        )
        for n, i in enumerate(where)
    ]
    made = [
        trailing_map(b, t, k, e, eye_key, key_dim)
        for b, t, k, e in zip(bases, trail, k_raw, last)
    ]
    for n in range(rest):
        r_ref[n] = bases[n]
        if n < rest // 2:
            give_ref[n] = made[n]
        else:
            own_ref[n - rest // 2] = made[n]


def query_rows(chips, place, q_ref, kh_ref, rows_ref, r_first, r_rest, f_ref, qs):
    heads, tok, key_dim = kh_ref.shape
    half = heads // 2
    first, rest = positions(heads, r_first.shape[0] // 2)
    core, chip = place[0], place[1]
    order = [(1 - core) * half + h for h in local_heads(1 - core, chip, chips, half)]
    order += [core * half + h for h in local_heads(core, chip, chips, half)]
    stage_rows(q_ref, qs)
    cum_row = rows_ref[1]
    cum_col = cum_row.T
    rows = lax.broadcasted_iota(jnp.int32, (tok, tok), 0)
    cols = lax.broadcasted_iota(jnp.int32, (tok, tok), 1)
    lower = rows >= cols
    for i in range(heads):
        q_wide = head_rows(qs, order[i], heads)
        q_inv = lax.rsqrt(jnp.sum(q_wide * q_wide, axis=1, keepdims=True) + 1e-6)
        dots = mm_nt(q_wide.astype(BF16), kh_ref[i])
        gap = cum_col[:, i : i + 1] - cum_row[i : i + 1, :]
        decay = jnp.exp(jnp.where(lower, gap, 0.0))
        scores = jnp.where(lower, dots * decay * q_inv * rows_ref[0, i : i + 1, :], 0.0)
        folded = mm3(scores, r_first[first.index(i)] if i in first else r_rest[rest.index(i)])
        gated = q_wide * (q_inv * jnp.exp(cum_col[:, i : i + 1]))
        f_ref[i] = jnp.concatenate(
            [folded[:, :key_dim] + gated, folded[:, key_dim:]], axis=1
        )


def query_kernel(chips, place, *refs):
    @pl.when(place[0] == 0)
    def _():
        query_rows(chips, place, *refs)


def query_late_kernel(chips, place, done_ref, *refs):
    f_ref = refs[-2]

    @pl.when(place[0] == 0)
    def _():
        f_ref[...] = done_ref[...]

    @pl.when(place[0] != 0)
    def _():
        query_rows(chips, place, *refs)


def read_out(folded, state):
    key_dim = state.shape[0]
    return mm3(folded[:, :key_dim], state) + folded[:, key_dim:]


def pair_kernel(chips, slot, place, *refs):
    map_refs, (state_ref, keep_ref, give_ref) = refs[:-3], refs[-3:]
    core, chip = place[0], place[1]
    per = state_ref.shape[0]
    for j in range(per):
        own, got = picked_maps(map_refs, slot, j, per, chips, core, chip)
        state = state_ref[j]
        second = read_out(jnp.where(core == 0, own, got), state)
        keep_ref[j] = jnp.where(core == 0, state, second)
        give_ref[j] = jnp.where(core == 0, second, state)


def picked_maps(refs, slot, j, per, chips, core, chip):
    own_first, own_rest, got_first, got_rest = refs
    half = per + own_rest.shape[0]
    if half % chips:
        at = owner_of(slot, core, chip, chips) * per + j
        at_tail = jnp.clip(at - per, 0, half - per - 1)
        return tuple(
            jnp.where(at < per, first[0], rest[at_tail])
            for first, rest in ((own_first, own_rest), (got_first, got_rest))
        )
    at = slot * per + j
    if at < per:
        return own_first[at], got_first[at]
    return own_rest[at - per], got_rest[at - per]


def chip_kernel(key_dim, chips, slots, place, *refs):
    in_refs, out_refs = refs[: -len(slots)], refs[-len(slots) :]
    core, chip = place[0], place[1]
    per = out_refs[0].shape[0]
    for slot, out in zip(slots, out_refs):
        for j in range(per):
            if len(in_refs) == 4:
                at = owner_of(slot, core, chip, chips) * per + j
                tail = in_refs[1].shape[0]
                at_tail = jnp.clip(at - per, 0, tail - 1)
                own, got = (
                    jnp.where(at < per, head[0], rest[at_tail])
                    for head, rest in (in_refs[:2], in_refs[2:])
                )
            else:
                at = (slot - slots[0]) * per + j
                own, got = in_refs[0][at], in_refs[1][at]
            earlier = jnp.where(core == 0, own, got)
            later = jnp.where(core == 0, got, own)
            out[j] = compose(later, earlier, key_dim)


def in_order(chip, maps):
    maps = list(maps)
    bit = 1
    while bit < len(maps):
        swapped = jnp.bitwise_and(chip, bit) != 0
        maps = [jnp.where(swapped, maps[i ^ bit], maps[i]) for i in range(len(maps))]
        bit *= 2
    return maps


def total_kernel(key_dim, place, *refs):
    maps, total = refs[:-1], refs[-1]
    chip = place[1]
    for j in range(total.shape[0]):
        level = by_distance(place[0], [ref[j] for ref in maps])
        bit = 1
        while len(level) > 1:
            swapped = jnp.bitwise_and(chip, bit) != 0
            level = [
                compose(
                    jnp.where(swapped, low, high), jnp.where(swapped, high, low), key_dim
                )
                for low, high in zip(level[::2], level[1::2])
            ]
            bit *= 2
        total[j] = level[0]


def prefix_kernel(key_dim, place, *refs):
    maps, prefix = refs[:-1], refs[-1]
    for j in range(prefix.shape[1]):
        ordered = in_order(place[1], by_distance(place[0], [ref[j] for ref in maps]))
        running = ordered[0]
        prefix[0, j] = running
        for index in range(1, len(ordered) - 1):
            running = compose(ordered[index], running, key_dim)
            prefix[index, j] = running


def is_upper(place, level):
    return jnp.bitwise_and(jnp.right_shift(place[2], level), 1) == 1


def group_total_kernel(key_dim, level, place, total_ref, got_ref, out_ref):
    upper = is_upper(place, level)
    for j in range(total_ref.shape[0]):
        mine, got = total_ref[j], got_ref[j]
        later = jnp.where(upper, mine, got)
        earlier = jnp.where(upper, got, mine)
        if out_ref.shape[2] == mine.shape[1]:
            out_ref[j] = compose(later, earlier, key_dim)
        else:
            out_ref[j] = mm3(later[:, :key_dim], earlier[:, key_dim:]) + later[:, key_dim:]


def before_kernel(key_dim, level, place, got_ref, prefix_ref, out_ref):
    upper = is_upper(place, level)
    count = out_ref.shape[0]

    @pl.when(upper)
    def _():
        for j in range(out_ref.shape[1]):
            for index in range(count):
                if prefix_ref.shape[0] == count:
                    out_ref[index, j] = compose(prefix_ref[index, j], got_ref[j], key_dim)
                elif index == 0:
                    out_ref[index, j] = got_ref[j]
                else:
                    out_ref[index, j] = compose(prefix_ref[index - 1, j], got_ref[j], key_dim)

    @pl.when(jnp.logical_not(upper))
    def _():
        for j in range(out_ref.shape[1]):
            for index in range(count):
                if prefix_ref.shape[0] == count:
                    out_ref[index, j] = prefix_ref[index, j]
                elif index == 0:
                    out_ref[index, j] = jnp.where(
                        lax.broadcasted_iota(jnp.int32, out_ref.shape[2:], 0)
                        == lax.broadcasted_iota(jnp.int32, out_ref.shape[2:], 1),
                        1.0,
                        0.0,
                    )
                else:
                    out_ref[index, j] = prefix_ref[index - 1, j]


def enter_kernel(key_dim, level, place, got_ref, prefix_ref, *out_refs):
    core, chip, chips = place[0], place[1], len(out_refs)
    upper = is_upper(place, level)
    for j in range(got_ref.shape[0]):
        eh, el = split2(jnp.where(upper, got_ref[j], 0.0))
        twice = jnp.concatenate([eh, eh], axis=0)
        for slot, out in enumerate(out_refs):
            one = prefix_ref[owner_of(slot, core, chip, chips), j]
            th, tl = split2(one[:, :key_dim])
            moved = mm(jnp.concatenate([th, tl], axis=1), twice) + mm(th, el)
            out[j] = moved + one[:, key_dim:]


def each_slot(place, slots, chips, half, per, use):
    core, chip = place[0], place[1]
    for n, slot in enumerate(slots):
        for own in (True, False):
            side = core if own else 1 - core
            owner = owner_of(slot, side, chip, chips)

            def run(n=n, slot=slot, own=own, side=side, owner=owner):
                for j in range(per):
                    local = owner * per + j
                    position = local if half % chips else slot * per + j
                    use(n, j, own, position + (half if own else 0), side * half + local)

            if half % chips:
                pl.when(owner < half // per)(run)
            else:
                run()


def early_kernel(per, slots, chips, place, f_ref, *refs):
    parts, out_ref = refs[:-1], refs[-1]

    def use(n, j, own, position, head):
        part = parts[n if own else len(slots) + n]
        out_ref[n, 0 if own else 1, j] = read_out(f_ref[position], part[j])

    each_slot(place, slots, chips, f_ref.shape[0] // 2, per, use)


def output_kernel(per, early, late, chips, place, f_ref, early_ref, *refs):
    o_ref, ob, os0, os1, sems = refs[-5:]
    parts = refs[:-5]
    heads, tok, wide = f_ref.shape
    mid = o_ref.shape[2] // 2

    def put(head, out):
        os0[pl.ds(head, tok, stride=heads), :] = out[:, :mid]
        os1[pl.ds(head, tok, stride=heads), :] = out[:, mid:]

    def use_early(n, j, own, position, head):
        put(head, early_ref[n, 0 if own else 1, j])

    def use_late(n, j, own, position, head):
        put(head, read_out(f_ref[position], parts[n if own else len(late) + n][j]))

    each_slot(place, early, chips, heads // 2, per, use_early)
    each_slot(place, late, chips, heads // 2, per, use_late)
    pieces = sems.shape[0]
    rows = tok // pieces
    copies = []
    for n in range(pieces):
        some = pl.ds(n * rows, rows)
        flat = pl.ds(n * rows * heads, rows * heads)
        ob[some, :, :mid] = os0[flat, :].reshape(rows, heads, mid).astype(BF16)
        ob[some, :, mid:] = os1[flat, :].reshape(rows, heads, mid).astype(BF16)
        copy = pltpu.make_async_copy(ob.at[some], o_ref.at[some], sems.at[n])
        copy.start()
        copies.append(copy)
    for copy in copies:
        copy.wait()


def body(queries, key_rows, value_rows, log_gate, beta_rate):
    tok, heads, key_dim = queries.shape
    value_dim = value_rows.shape[2]
    wide = key_dim + value_dim
    half = heads // 2
    seq, grp = lax.axis_size("seq"), lax.axis_size("grp")
    chips = seq // 2
    owners = min(chips, half)
    per = half // owners
    f32 = lambda *shape: jax.ShapeDtypeStruct(shape, F32)
    tall = lambda width: pltpu.VMEM((tok * heads, width), F32)
    unit = 2 * tok * key_dim * key_dim
    sibling = [(i, i ^ 1) for i in range(seq)]

    give_first, own_first, first_basis, k_heads, trail, rows, inverse, v_rest = pl.pallas_call(
        placed(functools.partial(basis_kernel, chips, per)),
        out_shape=(
            f32(per, key_dim, wide),
            f32(per, key_dim, wide),
            f32(2 * per, tok, wide),
            jax.ShapeDtypeStruct((heads, tok, key_dim), BF16),
            f32(heads - 2 * per, tok, key_dim),
            f32(4, heads, tok),
            f32(heads - 2 * per, tok, tok),
            jax.ShapeDtypeStruct((heads - 2 * per, tok, value_dim), BF16),
        ),
        in_specs=[pl.BlockSpec(memory_space=pltpu.HBM)] * 4,
        out_specs=tuple(vmem(8)),
        scratch_shapes=[
            pltpu.VMEM((tok, heads, key_dim), BF16),
            pltpu.VMEM((tok, heads, value_dim), BF16),
            pltpu.VMEM((heads, tok), F32),
            pltpu.VMEM((heads, tok), F32),
            tall(key_dim),
            tall(value_dim // 2),
            tall(value_dim // 2),
            pltpu.SemaphoreType.DMA((4,)),
        ],
        compiler_params=pltpu.CompilerParams(vmem_limit_bytes=VMEM_LIMIT),
        cost_estimate=pl.CostEstimate(
            flops=50 * heads * unit, bytes_accessed=0, transcendentals=0
        ),
    )(
        *(
            pltpu.with_memory_space_constraint(a, pltpu.HBM)
            for a in (key_rows, value_rows, log_gate, beta_rate)
        )
    )
    got_first = lax.ppermute(give_first, "seq", sibling)
    give_rest, own_rest, rest_basis = call(
        rest_kernel,
        (
            f32(half - per, key_dim, wide),
            f32(half - per, key_dim, wide),
            f32(heads - 2 * per, tok, wide),
        ),
        flops=200 * heads * unit,
    )(inverse, k_heads, v_rest, trail, rows)
    give_rest, got_first = lax.optimization_barrier((give_rest, got_first))
    got_rest = lax.ppermute(give_rest, "seq", sibling)

    def chip_maps(slots, *maps):
        return call(
            functools.partial(chip_kernel, key_dim, chips, slots),
            [f32(per, key_dim, wide)] * len(slots),
        )(*maps)

    slots = list(range(chips))
    if half % chips:
        made = chip_maps(slots, own_first, own_rest, got_first, got_rest)
    else:
        made = chip_maps(slots[:1], own_first, got_first)
        if chips > 1:
            made = made + chip_maps(slots[1:], own_rest, got_rest)
    distances = slot_list(chips)

    def across(parts, to_owner):
        moved = []
        for slot in slots[:-1]:
            swap = [(i, i ^ (2 * distances[i % 2][slot])) for i in range(seq)]
            pairs = [(a, b) for a, b in swap if (b if to_owner else a) // 2 < owners]
            moved.append(lax.ppermute(parts[slot], "seq", pairs))
        return moved + [parts[-1]]

    def folded_by(kernel, *arrays):
        return call(
            functools.partial(kernel, chips),
            f32(heads, tok, wide),
            [tall(key_dim)],
            flops=20 * heads * unit,
        )(*arrays, queries, k_heads, rows, first_basis, rest_basis)

    made = list(made)
    folded = folded_by(query_kernel)
    made[0], folded = lax.optimization_barrier((made[0], folded))
    owned = across(made, True)
    owned[0], folded = lax.optimization_barrier((owned[0], folded))
    folded = folded_by(query_late_kernel, folded)
    owned, folded = lax.optimization_barrier((owned, folded))
    total = call(functools.partial(total_kernel, key_dim), f32(per, key_dim, wide))(
        *owned
    )
    total, *owned = lax.optimization_barrier((total, *owned))
    prefix = call(
        functools.partial(prefix_kernel, key_dim), f32(chips - 1, per, key_dim, wide)
    )(*owned)
    level = 0
    while 2 << level <= grp:
        swap = [(i, i ^ (1 << level)) for i in range(grp)]
        if 2 << level == grp:
            if level == 0:
                total = total[:, :, key_dim:]
            got_state = lax.ppermute(total, "grp", swap)
            states = call(
                functools.partial(enter_kernel, key_dim, level),
                [f32(per, key_dim, value_dim)] * chips,
            )(got_state, prefix)
        else:
            got = lax.ppermute(total, "grp", swap)
            width = value_dim if 4 << level == grp else wide
            total = call(
                functools.partial(group_total_kernel, key_dim, level), f32(per, key_dim, width)
            )(total, got)
            prefix = call(
                functools.partial(before_kernel, key_dim, level),
                f32(chips, per, key_dim, wide),
            )(got, prefix)
        level += 1
    arrived = across(states, False)
    arrived[0], arrived[-1] = lax.optimization_barrier((arrived[0], arrived[-1]))
    kept, others = [], []
    for slot, part in enumerate(arrived):
        keep, give = call(
            functools.partial(pair_kernel, chips, slot),
            [f32(per, key_dim, value_dim)] * 2,
        )(own_first, own_rest, got_first, got_rest, part)
        kept.append(keep)
        others.append(lax.ppermute(give, "seq", sibling))
    early = (slots[-1:] + slots[:-1])[: max(chips // 2, 1)]
    late = [slot for slot in slots if slot not in early]
    early_outs = call(
        functools.partial(early_kernel, per, early, chips),
        f32(len(early), 2, per, tok, value_dim),
        flops=6 * len(early) * per * unit,
    )(folded, *(kept[n] for n in early), *(others[n] for n in early))
    inputs = (
        folded,
        early_outs,
        *(kept[n] for n in late),
        *(others[n] for n in late),
    )
    return pl.pallas_call(
        placed(functools.partial(output_kernel, per, early, late, chips)),
        out_shape=jax.ShapeDtypeStruct((tok, heads, value_dim), BF16),
        in_specs=vmem(len(inputs)),
        out_specs=pl.BlockSpec(memory_space=pltpu.HBM),
        scratch_shapes=[
            pltpu.VMEM((tok, heads, value_dim), BF16),
            tall(value_dim // 2),
            tall(value_dim // 2),
            pltpu.SemaphoreType.DMA((2 if tok % 32 == 0 else 1,)),
        ],
        compiler_params=pltpu.CompilerParams(vmem_limit_bytes=VMEM_LIMIT),
    )(*inputs)


def solution(mesh):
    return jax.shard_map(
        body,
        mesh=mesh,
        in_specs=(
            P(("grp", "seq"), None, None),
            P(("grp", "seq"), None, None),
            P(("grp", "seq"), None, None),
            P(None, ("grp", "seq")),
            P(None, ("grp", "seq")),
        ),
        out_specs=P(("grp", "seq"), None, None),
        check_vma=False,
    )
```

```python
import functools

import jax
import jax.numpy as jnp
from jax import lax
from jax.experimental import pallas as pl
from jax.experimental.pallas import tpu as pltpu
from jax.sharding import PartitionSpec as P

F32 = jnp.float32
BF16 = jnp.bfloat16
VMEM_LIMIT = 48 * 1024 * 1024


def split2(a):
    high = a.astype(BF16)
    low = (a - high.astype(F32)).astype(BF16)
    return high, low


def mm(a, b):
    return jnp.dot(a, b, preferred_element_type=F32)


def mm_nt(a, b):
    return lax.dot_general(a, b, (((1,), (1,)), ((), ())), preferred_element_type=F32)


def mm_tn(a, b):
    return lax.dot_general(a, b, (((0,), (0,)), ((), ())), preferred_element_type=F32)


def mm_exact_right(a, b):
    high, low = split2(a)
    return mm(jnp.concatenate([high, low], axis=1), jnp.concatenate([b, b], axis=0))


def mm3(a, b):
    ah, al = split2(a)
    bh, bl = split2(b)
    return mm(jnp.concatenate([ah, al], axis=1), jnp.concatenate([bh, bh], axis=0)) + mm(ah, bl)


def compose(later, earlier, key_dim):
    moved = mm3(later[:, :key_dim], earlier)
    return jnp.concatenate(
        [moved[:, :key_dim], moved[:, key_dim:] + later[:, key_dim:]], axis=1
    )


def turned(distance, chips):
    bits = chips.bit_length() - 1
    low = bits // 2
    return (distance >> low) | ((distance & ((1 << low) - 1)) << (bits - low))


def slot_list(chips):
    plain = [chips - 1] + list(range(1, chips - 1)) + [0] if chips > 1 else [0]
    return plain, plain


def owner_of(slot, core, chip, chips):
    plain, other = slot_list(chips)
    if plain[slot] == other[slot]:
        return jnp.bitwise_xor(chip, plain[slot])
    return jnp.bitwise_xor(chip, jnp.where(core == 0, plain[slot], other[slot]))


def by_distance(core, maps):
    plain, other = slot_list(len(maps))
    ordered = []
    for d in range(len(maps)):
        a, b = maps[plain.index(d)], maps[other.index(d)]
        ordered.append(a if plain.index(d) == other.index(d) else jnp.where(core == 0, a, b))
    return ordered


def local_heads(core, chip, chips, half):
    if half % chips:
        return list(range(half))
    per = half // chips
    return [owner_of(n // per, core, chip, chips) * per + n % per for n in range(half)]


def positions(heads, per):
    half = heads // 2
    first = [*range(per), *range(half, half + per)]
    return first, [n for n in range(heads) if n not in first]


def vmem(count):
    return [pl.BlockSpec(memory_space=pltpu.VMEM)] * count


def placed(kernel):
    def run(*refs):
        seq = lax.axis_index("seq")
        kernel((lax.rem(seq, 2), lax.div(seq, 2), lax.axis_index("grp")), *refs)

    return run


def call(kernel, out_shape, scratch=(), flops=0, nbytes=0):
    def run(*arrays):
        return pl.pallas_call(
            placed(kernel),
            out_shape=out_shape,
            in_specs=vmem(len(arrays)),
            out_specs=jax.tree.map(lambda _: pl.BlockSpec(memory_space=pltpu.VMEM), out_shape),
            scratch_shapes=list(scratch),
            compiler_params=pltpu.CompilerParams(vmem_limit_bytes=VMEM_LIMIT),
            cost_estimate=pl.CostEstimate(flops=flops, bytes_accessed=nbytes, transcendentals=0),
        )(*arrays)

    return run


def lane_cumsum(a):
    size = a.shape[1]
    lane = lax.broadcasted_iota(jnp.int32, a.shape, 1)
    step = 1
    while step < size:
        a = a + jnp.where(lane >= step, pltpu.roll(a, step, 1), 0.0)
        step *= 2
    return a


def head_rows(scratch, head, heads):
    count = scratch.shape[0] // heads
    return scratch[pl.ds(head, count, stride=heads), :]


def stage_rows(ref, scratch):
    wide = ref[...].astype(F32)
    scratch[...] = wide.reshape(scratch.shape)


def mm3_packed(lhs, rhs):
    rows = lhs.shape[0]
    width = rhs.shape[1] // 2
    high, low = split2(lhs)
    out = mm(jnp.concatenate([high, low], axis=0), rhs)
    return out[:rows, :width] + (out[:rows, width:] + out[rows:, :width])


def block_inverse(strict):
    size = strict[0].shape[0]
    base = min(16, size)
    rows = lax.broadcasted_iota(jnp.int32, (size, size), 0)
    cols = lax.broadcasted_iota(jnp.int32, (size, size), 1)

    def ones_where(mask):
        return jnp.where(mask, 1.0, 0.0).astype(BF16)

    def spread(compact, mask):
        count = size // compact.shape[0]
        return jnp.concatenate(
            [jnp.concatenate([part] * count, axis=0) * mask for part in split2(compact)], axis=1
        )

    lane = lax.broadcasted_iota(jnp.int32, (base, size), 1)
    line = lax.broadcasted_iota(jnp.int32, (base, size), 0)
    power, inverse = [], []
    for a in strict:
        compact = jnp.zeros((base, size), F32)
        for n in range(size // base):
            compact = jnp.where(lane // base == n, -a[n * base : (n + 1) * base, :], compact)
        power.append(compact)
        inverse.append(jnp.where(lane % base == line, 1.0, compact))
    mask = ones_where(rows // base == cols // base)
    wide = [spread(p, mask) for p in power]
    power = [mm3_packed(p, w) for p, w in zip(power, wide)]
    span = 2
    while span < base:
        wide = [spread(p, mask) for p in power]
        if span * 2 < base:
            both = [
                mm3_packed(jnp.concatenate([p, x], axis=0), w)
                for p, x, w in zip(power, inverse, wide)
            ]
            power = [a[:base] for a in both]
            inverse = [x + a[base:] for x, a in zip(inverse, both)]
        else:
            inverse = [x + mm3_packed(x, w) for x, w in zip(inverse, wide)]
        span *= 2
    parts = [split2(a) for a in strict]
    span = base
    while span < size:
        joint = ones_where(
            (rows // (2 * span) == cols // (2 * span)) & (rows // span != cols // span)
        )
        mask = ones_where(rows // span == cols // span)
        even = (
            (lax.broadcasted_iota(jnp.int32, (span, size), 1) // span) % 2
        ) == 0
        off = [jnp.concatenate([h * joint, l * joint], axis=1) for h, l in parts]
        first = [mm3_packed(x, o) for x, o in zip(inverse, off)]
        second = [mm3_packed(f, spread(x, mask)) for f, x in zip(first, inverse)]
        inverse = [
            jnp.concatenate([jnp.where(even, x, 0.0), jnp.where(even, -y, x)], axis=0)
            for x, y in zip(inverse, second)
        ]
        span *= 2
    return inverse


def updates_basis(inverse, k_raw, v_raw, beta, key_scale):
    key_part = mm_exact_right(inverse * key_scale, k_raw)
    value_part = mm_exact_right(inverse * beta, v_raw)
    return jnp.concatenate([key_part, value_part], axis=1)


def trailing_map(basis, trail, k_raw, last, eye_key, key_dim):
    bh, bl = split2(basis * trail)
    moved = mm_tn(
        jnp.concatenate([k_raw, k_raw], axis=0), jnp.concatenate([bh, bl], axis=0)
    )
    return jnp.concatenate(
        [moved[:, :key_dim] + jnp.where(eye_key, last, 0.0), moved[:, key_dim:]], axis=1
    )


def eye_mask(size):
    return lax.broadcasted_iota(jnp.int32, (size, size), 0) == lax.broadcasted_iota(
        jnp.int32, (size, size), 1
    )


def basis_kernel(
    chips, per, place, k_hbm, v_hbm, g_hbm, b_hbm,
    give_ref, own_ref, r_ref, kh_ref, trail_ref, rows_ref, inverse_ref, v_rest_ref,
    k_ref, v_ref, g_ref, b_ref, ks, vs0, vs1, sems,
):
    copies = [
        pltpu.make_async_copy(src, dst, sems.at[n])
        for n, (src, dst) in enumerate(
            ((g_hbm, g_ref), (k_hbm, k_ref), (b_hbm, b_ref), (v_hbm, v_ref))
        )
    ]
    for copy in copies:
        copy.start()
    tok, heads, key_dim = k_ref.shape
    value_dim = v_ref.shape[2]
    half = heads // 2
    core, chip = place[0], place[1]
    order = [(1 - core) * half + h for h in local_heads(1 - core, chip, chips, half)]
    order += [core * half + h for h in local_heads(core, chip, chips, half)]
    copies[0].wait()
    copies[2].wait()

    def picked(ref):
        return jnp.concatenate([ref[pl.ds(h, 1), :] for h in order], axis=0)

    cum_row = lane_cumsum(picked(g_ref))
    beta_row = picked(b_ref)
    last_row = cum_row[:, tok - 1 :]
    decay_row = jnp.exp(cum_row)
    cum_col = cum_row.T
    beta_col = beta_row.T
    trail_col = jnp.exp(last_row - cum_row).T
    rows = lax.broadcasted_iota(jnp.int32, (tok, tok), 0)
    cols = lax.broadcasted_iota(jnp.int32, (tok, tok), 1)
    lower = rows > cols
    eye = rows == cols
    eye_key = eye_mask(key_dim)
    every = range(heads)
    copies[1].wait()
    stage_rows(k_ref, ks)
    k_wide = [head_rows(ks, h, heads) for h in order]
    k_raw = [a.astype(BF16) for a in k_wide]
    for i in every:
        kh_ref[i] = k_raw[i]
    gram = [mm_nt(a, a) for a in k_raw]
    inv_col = [lax.rsqrt(jnp.sum(a * a, axis=1, keepdims=True) + 1e-6) for a in k_wide]
    inv_row = [
        lax.rsqrt(jnp.sum(jnp.where(eye, a, 0.0), axis=0, keepdims=True) + 1e-6) for a in gram
    ]
    strict = []
    for i in every:
        gap = cum_col[:, i : i + 1] - cum_row[i : i + 1, :]
        decay = jnp.exp(jnp.where(lower, gap, 0.0))
        left = beta_col[:, i : i + 1] * inv_col[i]
        strict.append(jnp.where(lower, gram[i] * decay * left * inv_row[i], 0.0))
    copies[3].wait()
    wide = v_ref[...].astype(F32)
    vs0[...] = wide[:, :, : value_dim // 2].reshape(vs0.shape)
    vs1[...] = wide[:, :, value_dim // 2 :].reshape(vs1.shape)
    v_raw = [
        jnp.concatenate(
            [head_rows(vs0, h, heads), head_rows(vs1, h, heads)], axis=1
        ).astype(BF16)
        for h in order
    ]
    first, rest = positions(heads, per)
    for n, i in enumerate(rest):
        v_rest_ref[n] = v_raw[i]
    inverse = block_inverse(strict)
    rows_ref[0] = jnp.concatenate(inv_row, axis=0)
    rows_ref[1] = cum_row
    rows_ref[2] = beta_row
    rows_ref[3] = -(decay_row * beta_row * jnp.concatenate(inv_row, axis=0))
    for n, i in enumerate(first):
        trail = trail_col[:, i : i + 1] * inv_col[i]
        beta_i = beta_row[i : i + 1, :]
        key_scale = -(decay_row[i : i + 1, :] * beta_i * inv_row[i])
        basis = updates_basis(inverse[i], k_raw[i], v_raw[i], beta_i, key_scale)
        r_ref[n] = basis
        made = trailing_map(
            basis, trail, k_raw[i], jnp.exp(last_row[i : i + 1, :]), eye_key, key_dim
        )
        if n < per:
            give_ref[n] = made
        else:
            own_ref[n - per] = made
    for n, i in enumerate(rest):
        trail_ref[n] = jnp.broadcast_to(trail_col[:, i : i + 1] * inv_col[i], (tok, key_dim))
        inverse_ref[n] = inverse[i]


def rest_kernel(place, inverse_ref, kh_ref, v_ref, trail_ref, rows_ref, give_ref, own_ref, r_ref):
    rest, tok, wide = r_ref.shape
    key_dim = wide - v_ref.shape[2]
    heads = kh_ref.shape[0]
    eye_key = eye_mask(key_dim)
    where = positions(heads, (heads - rest) // 2)[1]
    k_raw = [kh_ref[i] for i in where]
    trail = [trail_ref[n][:, :1] for n in range(rest)]
    last = [jnp.exp(rows_ref[1, i : i + 1, tok - 1 :]) for i in where]
    bases = [
        updates_basis(
            inverse_ref[n], k_raw[n], v_ref[n], rows_ref[2, i : i + 1, :], rows_ref[3, i : i + 1, :]
        )
        for n, i in enumerate(where)
    ]
    made = [
        trailing_map(b, t, k, e, eye_key, key_dim)
        for b, t, k, e in zip(bases, trail, k_raw, last)
    ]
    for n in range(rest):
        r_ref[n] = bases[n]
        if n < rest // 2:
            give_ref[n] = made[n]
        else:
            own_ref[n - rest // 2] = made[n]


def query_rows(chips, place, q_ref, kh_ref, rows_ref, r_first, r_rest, f_ref, qs):
    heads, tok, key_dim = kh_ref.shape
    half = heads // 2
    first, rest = positions(heads, r_first.shape[0] // 2)
    core, chip = place[0], place[1]
    order = [(1 - core) * half + h for h in local_heads(1 - core, chip, chips, half)]
    order += [core * half + h for h in local_heads(core, chip, chips, half)]
    stage_rows(q_ref, qs)
    cum_row = rows_ref[1]
    cum_col = cum_row.T
    rows = lax.broadcasted_iota(jnp.int32, (tok, tok), 0)
    cols = lax.broadcasted_iota(jnp.int32, (tok, tok), 1)
    lower = rows >= cols
    for i in range(heads):
        q_wide = head_rows(qs, order[i], heads)
        q_inv = lax.rsqrt(jnp.sum(q_wide * q_wide, axis=1, keepdims=True) + 1e-6)
        dots = mm_nt(q_wide.astype(BF16), kh_ref[i])
        gap = cum_col[:, i : i + 1] - cum_row[i : i + 1, :]
        decay = jnp.exp(jnp.where(lower, gap, 0.0))
        scores = jnp.where(lower, dots * decay * q_inv * rows_ref[0, i : i + 1, :], 0.0)
        folded = mm3(scores, r_first[first.index(i)] if i in first else r_rest[rest.index(i)])
        gated = q_wide * (q_inv * jnp.exp(cum_col[:, i : i + 1]))
        f_ref[i] = jnp.concatenate(
            [folded[:, :key_dim] + gated, folded[:, key_dim:]], axis=1
        )


def query_kernel(chips, place, *refs):
    @pl.when(place[0] == 0)
    def _():
        query_rows(chips, place, *refs)


def query_late_kernel(chips, place, done_ref, *refs):
    f_ref = refs[-2]

    @pl.when(place[0] == 0)
    def _():
        f_ref[...] = done_ref[...]

    @pl.when(place[0] != 0)
    def _():
        query_rows(chips, place, *refs)


def read_out(folded, state):
    key_dim = state.shape[0]
    return mm3(folded[:, :key_dim], state) + folded[:, key_dim:]


def pair_kernel(chips, slot, place, *refs):
    map_refs, (state_ref, keep_ref, give_ref) = refs[:-3], refs[-3:]
    core, chip = place[0], place[1]
    per = state_ref.shape[0]
    for j in range(per):
        own, got = picked_maps(map_refs, slot, j, per, chips, core, chip)
        state = state_ref[j]
        second = read_out(jnp.where(core == 0, own, got), state)
        keep_ref[j] = jnp.where(core == 0, state, second)
        give_ref[j] = jnp.where(core == 0, second, state)


def picked_maps(refs, slot, j, per, chips, core, chip):
    own_first, own_rest, got_first, got_rest = refs
    half = per + own_rest.shape[0]
    if half % chips:
        at = owner_of(slot, core, chip, chips) * per + j
        at_tail = jnp.clip(at - per, 0, half - per - 1)
        return tuple(
            jnp.where(at < per, first[0], rest[at_tail])
            for first, rest in ((own_first, own_rest), (got_first, got_rest))
        )
    at = slot * per + j
    if at < per:
        return own_first[at], got_first[at]
    return own_rest[at - per], got_rest[at - per]


def chip_kernel(key_dim, chips, slots, place, *refs):
    in_refs, out_refs = refs[: -len(slots)], refs[-len(slots) :]
    core, chip = place[0], place[1]
    per = out_refs[0].shape[0]
    for slot, out in zip(slots, out_refs):
        for j in range(per):
            if len(in_refs) == 4:
                at = owner_of(slot, core, chip, chips) * per + j
                tail = in_refs[1].shape[0]
                at_tail = jnp.clip(at - per, 0, tail - 1)
                own, got = (
                    jnp.where(at < per, head[0], rest[at_tail])
                    for head, rest in (in_refs[:2], in_refs[2:])
                )
            else:
                at = (slot - slots[0]) * per + j
                own, got = in_refs[0][at], in_refs[1][at]
            earlier = jnp.where(core == 0, own, got)
            later = jnp.where(core == 0, got, own)
            out[j] = compose(later, earlier, key_dim)


def in_order(chip, maps):
    maps = list(maps)
    bit = 1
    while bit < len(maps):
        swapped = jnp.bitwise_and(chip, bit) != 0
        maps = [jnp.where(swapped, maps[i ^ bit], maps[i]) for i in range(len(maps))]
        bit *= 2
    return maps


def total_kernel(key_dim, place, *refs):
    maps, total = refs[:-1], refs[-1]
    chip = place[1]
    for j in range(total.shape[0]):
        level = by_distance(place[0], [ref[j] for ref in maps])
        bit = 1
        while len(level) > 1:
            swapped = jnp.bitwise_and(chip, bit) != 0
            level = [
                compose(
                    jnp.where(swapped, low, high), jnp.where(swapped, high, low), key_dim
                )
                for low, high in zip(level[::2], level[1::2])
            ]
            bit *= 2
        total[j] = level[0]


def prefix_kernel(key_dim, place, *refs):
    maps, prefix = refs[:-1], refs[-1]
    for j in range(prefix.shape[1]):
        ordered = in_order(place[1], by_distance(place[0], [ref[j] for ref in maps]))
        running = ordered[0]
        prefix[0, j] = running
        for index in range(1, len(ordered) - 1):
            running = compose(ordered[index], running, key_dim)
            prefix[index, j] = running


def is_upper(place, level):
    return jnp.bitwise_and(jnp.right_shift(place[2], level), 1) == 1


def group_total_kernel(key_dim, level, place, total_ref, got_ref, out_ref):
    upper = is_upper(place, level)
    for j in range(total_ref.shape[0]):
        mine, got = total_ref[j], got_ref[j]
        later = jnp.where(upper, mine, got)
        earlier = jnp.where(upper, got, mine)
        if out_ref.shape[2] == mine.shape[1]:
            out_ref[j] = compose(later, earlier, key_dim)
        else:
            out_ref[j] = mm3(later[:, :key_dim], earlier[:, key_dim:]) + later[:, key_dim:]


def before_kernel(key_dim, level, place, got_ref, prefix_ref, out_ref):
    upper = is_upper(place, level)
    count = out_ref.shape[0]

    @pl.when(upper)
    def _():
        for j in range(out_ref.shape[1]):
            for index in range(count):
                if prefix_ref.shape[0] == count:
                    out_ref[index, j] = compose(prefix_ref[index, j], got_ref[j], key_dim)
                elif index == 0:
                    out_ref[index, j] = got_ref[j]
                else:
                    out_ref[index, j] = compose(prefix_ref[index - 1, j], got_ref[j], key_dim)

    @pl.when(jnp.logical_not(upper))
    def _():
        for j in range(out_ref.shape[1]):
            for index in range(count):
                if prefix_ref.shape[0] == count:
                    out_ref[index, j] = prefix_ref[index, j]
                elif index == 0:
                    out_ref[index, j] = jnp.where(
                        lax.broadcasted_iota(jnp.int32, out_ref.shape[2:], 0)
                        == lax.broadcasted_iota(jnp.int32, out_ref.shape[2:], 1),
                        1.0,
                        0.0,
                    )
                else:
                    out_ref[index, j] = prefix_ref[index - 1, j]


def enter_kernel(key_dim, level, place, got_ref, prefix_ref, *out_refs):
    core, chip, chips = place[0], place[1], len(out_refs)
    upper = is_upper(place, level)
    for j in range(got_ref.shape[0]):
        eh, el = split2(jnp.where(upper, got_ref[j], 0.0))
        twice = jnp.concatenate([eh, eh], axis=0)
        for slot, out in enumerate(out_refs):
            one = prefix_ref[owner_of(slot, core, chip, chips), j]
            th, tl = split2(one[:, :key_dim])
            moved = mm(jnp.concatenate([th, tl], axis=1), twice) + mm(th, el)
            out[j] = moved + one[:, key_dim:]


def each_slot(place, slots, chips, half, per, use):
    core, chip = place[0], place[1]
    for n, slot in enumerate(slots):
        for own in (True, False):
            side = core if own else 1 - core
            owner = owner_of(slot, side, chip, chips)

            def run(n=n, slot=slot, own=own, side=side, owner=owner):
                for j in range(per):
                    local = owner * per + j
                    position = local if half % chips else slot * per + j
                    use(n, j, own, position + (half if own else 0), side * half + local)

            if half % chips:
                pl.when(owner < half // per)(run)
            else:
                run()


def early_kernel(per, slots, chips, place, f_ref, *refs):
    parts, out_ref = refs[:-1], refs[-1]

    def use(n, j, own, position, head):
        part = parts[n if own else len(slots) + n]
        out_ref[n, 0 if own else 1, j] = read_out(f_ref[position], part[j])

    each_slot(place, slots, chips, f_ref.shape[0] // 2, per, use)


def output_kernel(per, early, late, chips, place, f_ref, early_ref, *refs):
    o_ref, ob, os0, os1, sems = refs[-5:]
    parts = refs[:-5]
    heads, tok, wide = f_ref.shape
    mid = o_ref.shape[2] // 2

    def put(head, out):
        os0[pl.ds(head, tok, stride=heads), :] = out[:, :mid]
        os1[pl.ds(head, tok, stride=heads), :] = out[:, mid:]

    def use_early(n, j, own, position, head):
        put(head, early_ref[n, 0 if own else 1, j])

    def use_late(n, j, own, position, head):
        put(head, read_out(f_ref[position], parts[n if own else len(late) + n][j]))

    each_slot(place, early, chips, heads // 2, per, use_early)
    each_slot(place, late, chips, heads // 2, per, use_late)
    pieces = sems.shape[0]
    rows = tok // pieces
    copies = []
    for n in range(pieces):
        some = pl.ds(n * rows, rows)
        flat = pl.ds(n * rows * heads, rows * heads)
        ob[some, :, :mid] = os0[flat, :].reshape(rows, heads, mid).astype(BF16)
        ob[some, :, mid:] = os1[flat, :].reshape(rows, heads, mid).astype(BF16)
        copy = pltpu.make_async_copy(ob.at[some], o_ref.at[some], sems.at[n])
        copy.start()
        copies.append(copy)
    for copy in copies:
        copy.wait()


def body(queries, key_rows, value_rows, log_gate, beta_rate):
    tok, heads, key_dim = queries.shape
    value_dim = value_rows.shape[2]
    wide = key_dim + value_dim
    half = heads // 2
    seq, grp = lax.axis_size("seq"), lax.axis_size("grp")
    chips = seq // 2
    owners = min(chips, half)
    per = half // owners
    f32 = lambda *shape: jax.ShapeDtypeStruct(shape, F32)
    tall = lambda width: pltpu.VMEM((tok * heads, width), F32)
    unit = 2 * tok * key_dim * key_dim
    sibling = [(i, i ^ 1) for i in range(seq)]

    give_first, own_first, first_basis, k_heads, trail, rows, inverse, v_rest = pl.pallas_call(
        placed(functools.partial(basis_kernel, chips, per)),
        out_shape=(
            f32(per, key_dim, wide),
            f32(per, key_dim, wide),
            f32(2 * per, tok, wide),
            jax.ShapeDtypeStruct((heads, tok, key_dim), BF16),
            f32(heads - 2 * per, tok, key_dim),
            f32(4, heads, tok),
            f32(heads - 2 * per, tok, tok),
            jax.ShapeDtypeStruct((heads - 2 * per, tok, value_dim), BF16),
        ),
        in_specs=[pl.BlockSpec(memory_space=pltpu.HBM)] * 4,
        out_specs=tuple(vmem(8)),
        scratch_shapes=[
            pltpu.VMEM((tok, heads, key_dim), BF16),
            pltpu.VMEM((tok, heads, value_dim), BF16),
            pltpu.VMEM((heads, tok), F32),
            pltpu.VMEM((heads, tok), F32),
            tall(key_dim),
            tall(value_dim // 2),
            tall(value_dim // 2),
            pltpu.SemaphoreType.DMA((4,)),
        ],
        compiler_params=pltpu.CompilerParams(vmem_limit_bytes=VMEM_LIMIT),
        cost_estimate=pl.CostEstimate(
            flops=50 * heads * unit, bytes_accessed=0, transcendentals=0
        ),
    )(
        *(
            pltpu.with_memory_space_constraint(a, pltpu.HBM)
            for a in (key_rows, value_rows, log_gate, beta_rate)
        )
    )
    got_first = lax.ppermute(give_first, "seq", sibling)
    give_rest, own_rest, rest_basis = call(
        rest_kernel,
        (
            f32(half - per, key_dim, wide),
            f32(half - per, key_dim, wide),
            f32(heads - 2 * per, tok, wide),
        ),
        flops=200 * heads * unit,
    )(inverse, k_heads, v_rest, trail, rows)
    give_rest, got_first = lax.optimization_barrier((give_rest, got_first))
    got_rest = lax.ppermute(give_rest, "seq", sibling)

    def chip_maps(slots, *maps):
        return call(
            functools.partial(chip_kernel, key_dim, chips, slots),
            [f32(per, key_dim, wide)] * len(slots),
        )(*maps)

    slots = list(range(chips))
    if half % chips:
        made = chip_maps(slots, own_first, own_rest, got_first, got_rest)
    else:
        made = chip_maps(slots[:1], own_first, got_first)
        if chips > 1:
            made = made + chip_maps(slots[1:], own_rest, got_rest)
    distances = slot_list(chips)

    def across(parts, to_owner):
        moved = []
        for slot in slots[:-1]:
            swap = [(i, i ^ (2 * distances[i % 2][slot])) for i in range(seq)]
            pairs = [(a, b) for a, b in swap if (b if to_owner else a) // 2 < owners]
            moved.append(lax.ppermute(parts[slot], "seq", pairs))
        return moved + [parts[-1]]

    def folded_by(kernel, *arrays):
        return call(
            functools.partial(kernel, chips),
            f32(heads, tok, wide),
            [tall(key_dim)],
            flops=20 * heads * unit,
        )(*arrays, queries, k_heads, rows, first_basis, rest_basis)

    made = list(made)
    folded = folded_by(query_kernel)
    made[0], folded = lax.optimization_barrier((made[0], folded))
    owned = across(made, True)
    owned[0], folded = lax.optimization_barrier((owned[0], folded))
    folded = folded_by(query_late_kernel, folded)
    owned, folded = lax.optimization_barrier((owned, folded))
    total = call(functools.partial(total_kernel, key_dim), f32(per, key_dim, wide))(
        *owned
    )
    total, *owned = lax.optimization_barrier((total, *owned))
    prefix = call(
        functools.partial(prefix_kernel, key_dim), f32(chips - 1, per, key_dim, wide)
    )(*owned)
    level = 0
    while 2 << level <= grp:
        swap = [(i, i ^ (1 << level)) for i in range(grp)]
        if 2 << level == grp:
            if level == 0:
                total = total[:, :, key_dim:]
            got_state = lax.ppermute(total, "grp", swap)
            states = call(
                functools.partial(enter_kernel, key_dim, level),
                [f32(per, key_dim, value_dim)] * chips,
            )(got_state, prefix)
        else:
            got = lax.ppermute(total, "grp", swap)
            width = value_dim if 4 << level == grp else wide
            total = call(
                functools.partial(group_total_kernel, key_dim, level), f32(per, key_dim, width)
            )(total, got)
            prefix = call(
                functools.partial(before_kernel, key_dim, level),
                f32(chips, per, key_dim, wide),
            )(got, prefix)
        level += 1
    arrived = across(states, False)
    arrived[0], arrived[-1] = lax.optimization_barrier((arrived[0], arrived[-1]))
    kept, others = [], []
    for slot, part in enumerate(arrived):
        keep, give = call(
            functools.partial(pair_kernel, chips, slot),
            [f32(per, key_dim, value_dim)] * 2,
        )(own_first, own_rest, got_first, got_rest, part)
        kept.append(keep)
        others.append(lax.ppermute(give, "seq", sibling))
    early = (slots[-1:] + slots[:-1])[: max(chips // 2, 1)]
    late = [slot for slot in slots if slot not in early]
    early_outs = call(
        functools.partial(early_kernel, per, early, chips),
        f32(len(early), 2, per, tok, value_dim),
        flops=6 * len(early) * per * unit,
    )(folded, *(kept[n] for n in early), *(others[n] for n in early))
    inputs = (
        folded,
        early_outs,
        *(kept[n] for n in late),
        *(others[n] for n in late),
    )
    return pl.pallas_call(
        placed(functools.partial(output_kernel, per, early, late, chips)),
        out_shape=jax.ShapeDtypeStruct((tok, heads, value_dim), BF16),
        in_specs=vmem(len(inputs)),
        out_specs=pl.BlockSpec(memory_space=pltpu.HBM),
        scratch_shapes=[
            pltpu.VMEM((tok, heads, value_dim), BF16),
            tall(value_dim // 2),
            tall(value_dim // 2),
            pltpu.SemaphoreType.DMA((4 if tok % 64 == 0 else 1,)),
        ],
        compiler_params=pltpu.CompilerParams(vmem_limit_bytes=VMEM_LIMIT),
    )(*inputs)


def solution(mesh):
    return jax.shard_map(
        body,
        mesh=mesh,
        in_specs=(
            P(("grp", "seq"), None, None),
            P(("grp", "seq"), None, None),
            P(("grp", "seq"), None, None),
            P(None, ("grp", "seq")),
            P(None, ("grp", "seq")),
        ),
        out_specs=P(("grp", "seq"), None, None),
        check_vma=False,
    )
```
